32 devices in a mesh: dp: 16 (over z, y, x), fsdp: 2 (over core).
Axes of the slice: x: 2, y: 2, z: 4, core: 2. Of those that a mesh axis runs over, the one named last changes fastest.
Arguments:
- tokens: bfloat16 [8192, 768], P(('dp', 'fsdp')), may hold values from -6 to 6
- cotangent: bfloat16 [8192, 768], P(('dp', 'fsdp')), may hold values from -6 to 6
- lengths: int32 [32, 6], P(('dp', 'fsdp')), may hold values from 1 to 160, 256 in all within a row
- mix_weight: float32 [768, 2304], P(None, ('dp', 'fsdp')), may hold values from -0.21875 to 0.21875
- out_weight: float32 [768, 768], P(('dp', 'fsdp')), may hold values from -0.875 to 0.875
- up_weight: float32 [768, 3072], P(None, ('dp', 'fsdp')), may hold values from -0.21875 to 0.21875
- down_weight: float32 [3072, 768], P(('dp', 'fsdp')), may hold values from -0.109375 to 0.109375
- norm_params: float32 [4, 768], replicated, may hold values from 0.5 to 1.5
- mix_first: float32 [768, 2304], P(None, ('dp', 'fsdp')), may hold values from -0.00061035156 to 0.00061035156
- out_first: float32 [768, 768], P(('dp', 'fsdp')), may hold values from -0.00061035156 to 0.00061035156
- up_first: float32 [768, 3072], P(None, ('dp', 'fsdp')), may hold values from -0.00061035156 to 0.00061035156
- down_first: float32 [3072, 768], P(('dp', 'fsdp')), may hold values from -0.00061035156 to 0.00061035156
- norm_first: float32 [4, 768], replicated, may hold values from -0.0029296875 to 0.0029296875
- mix_second: float32 [768, 2304], P(None, ('dp', 'fsdp')), may hold values from 7.4283713e-09 to 2.9656995e-08
- out_second: float32 [768, 768], P(('dp', 'fsdp')), may hold values from 7.4283713e-09 to 2.9656995e-08
- up_second: float32 [768, 3072], P(None, ('dp', 'fsdp')), may hold values from 7.4283713e-09 to 2.9656995e-08
- down_second: float32 [3072, 768], P(('dp', 'fsdp')), may hold values from 7.4283713e-09 to 2.9656995e-08
- norm_second: float32 [4, 768], replicated, may hold values from 1.8359093e-07 to 7.4848606e-07
Outputs:
- output: bfloat16 [8192, 768], P(('dp', 'fsdp'))
- grad_tokens: float32 [8192, 768], P(('dp', 'fsdp'))
- global_norm: float32 [], replicated
- new_mix: float32 [768, 2304], P(None, ('dp', 'fsdp'))
- new_out: float32 [768, 768], P(('dp', 'fsdp'))
- new_up: float32 [768, 3072], P(None, ('dp', 'fsdp'))
- new_down: float32 [3072, 768], P(('dp', 'fsdp'))
- new_norm: float32 [4, 768], replicated
- mix_first_new: float32 [768, 2304], P(None, ('dp', 'fsdp'))
- out_first_new: float32 [768, 768], P(('dp', 'fsdp'))
- up_first_new: float32 [768, 3072], P(None, ('dp', 'fsdp'))
- down_first_new: float32 [3072, 768], P(('dp', 'fsdp'))
- norm_first_new: float32 [4, 768], replicated
- mix_second_new: float32 [768, 2304], P(None, ('dp', 'fsdp'))
- out_second_new: float32 [768, 768], P(('dp', 'fsdp'))
- up_second_new: float32 [768, 3072], P(None, ('dp', 'fsdp'))
- down_second_new: float32 [3072, 768], P(('dp', 'fsdp'))
- norm_second_new: float32 [4, 768], replicated
The draws below stay inside these ranges and needn't reach their ends.
Inputs may be any that keep to these rules, and one draw needn't show every extreme that they name: In each row the first 5 entries are sequence lengths and the last is the padding at the buffer's end; the row sums to 256.
All inputs are finite; a program needn't handle non-finite values.
Results may differ from the reference program's by a relative error of at most 0.007.
Values may be sent and summed in bfloat16 or wider, within the bound.
No kernel may reach another device: no remote copies, remote signals or barrier semaphores. Data moves between devices by JAX's collectives and lax.ppermute only.
A program may use at most 192 MiB of HBM per device.

```python
import math
import jax
import jax.numpy as jnp
import numpy as np
from jax import lax

D = 768
FF = 3072
DH = 64
ROWS = 256
SLOTS = 6
LONGEST = 160
BUFFERS = 32
TOKENS = 8192
PARAMS = 7080960
STEP = 10


def block_levels(stream_key, shape, split, least, largest):
    level, own = 1.0, jax.random.fold_in(stream_key, 6)
    for axis_at, parts in split:
        heights = jnp.exp(jax.random.uniform(jax.random.fold_in(own, axis_at), (parts,), jnp.float32, least / len(split), largest / len(split)))
        level = level * jnp.repeat(heights, shape[axis_at] // parts).reshape([-1 if axis == axis_at else 1 for axis in range(len(shape))])
    return level


def split_up(number_of, total, most, slope):
    weights = [(1 << 20) // math.isqrt(standing ** slope) + 1 for standing in range(2, number_of + 1)]
    rest, holding = total - most - (number_of - 1), [1] * (number_of - 1)
    while rest > 0:
        candidates = [i for i in range(number_of - 1) if holding[i] < most]
        whole, remaining = sum([weights[i] for i in candidates]), rest
        for i in candidates:
            more = min(most - holding[i], max(1, remaining * weights[i] // whole), rest)
            holding[i] = holding[i] + more
            rest = rest - more
    return np.array([most] + holding)


def ragged(stream_key, amount, total, limit, lean):
    if amount == 2:
        one = jax.random.randint(stream_key, (), max(1, total - limit), min(limit, total - 1) + 1)
        return jnp.stack([one, total - one])
    sizes = jnp.asarray(split_up(amount, total, limit, lean), jnp.int32)
    twos = (amount - 1) // 2
    source_of, taker = sizes[1:1 + 2 * twos:2], sizes[2:2 + 2 * twos:2]
    margin = jnp.minimum(source_of - 1, limit - taker)
    passed = jax.random.randint(jax.random.fold_in(stream_key, 1), (twos,), 0, 1 << 20) % (margin + 1)
    sizes = sizes.at[1:1 + 2 * twos:2].set(source_of - passed).at[2:2 + 2 * twos:2].set(taker + passed)
    return sizes[jax.random.permutation(jax.random.fold_in(stream_key, 2), amount)]


def gaussian(own_key, shape, scale, reach, pieces=(), held_as=jnp.bfloat16):
    array = scale * jax.random.normal(own_key, shape, jnp.float32)
    if pieces:
        array = array * block_levels(own_key, shape, pieces, -0.22, 0.18)
    return jnp.clip(array, -reach, reach).astype(held_as)


def setup_inputs(seed: int = 0) -> dict:
    key_of = jax.random.split(jax.random.key(seed), 19)
    return {
        "tokens": gaussian(key_of[0], (TOKENS, D), 1.0, 6.0, ((0, 32),)),
        "cotangent": gaussian(key_of[1], (TOKENS, D), 1.0, 6.0, ((0, 32),)),
        "lengths": jax.vmap(lambda own: ragged(own, SLOTS, ROWS, LONGEST, 2))(jax.random.split(key_of[2], BUFFERS)).reshape((BUFFERS, SLOTS)).astype(jnp.int32),
        "mix_weight": gaussian(key_of[3], (D, 3 * D), D ** -0.5, 0.21875, ((1, 32),), jnp.float32),
        "out_weight": gaussian(key_of[4], (D, D), (D // 16) ** -0.5, 0.875, ((0, 32),), jnp.float32),
        "up_weight": gaussian(key_of[5], (D, FF), D ** -0.5, 0.21875, ((1, 32),), jnp.float32),
        "down_weight": gaussian(key_of[6], (FF, D), FF ** -0.5, 0.109375, ((0, 32),), jnp.float32),
        "norm_params": jnp.clip(1.0 + 0.1 * jax.random.normal(key_of[7], (4, D), jnp.float32), 0.5, 1.5),
        "mix_first": gaussian(key_of[8], (D, 3 * D), (0.111 / PARAMS ** 0.5), 0.00061035156, ((1, 32),), jnp.float32),
        "out_first": gaussian(key_of[9], (D, D), (0.111 / PARAMS ** 0.5), 0.00061035156, ((0, 32),), jnp.float32),
        "up_first": gaussian(key_of[10], (D, FF), (0.111 / PARAMS ** 0.5), 0.00061035156, ((1, 32),), jnp.float32),
        "down_first": gaussian(key_of[11], (FF, D), (0.111 / PARAMS ** 0.5), 0.00061035156, ((0, 32),), jnp.float32),
        "norm_first": gaussian(key_of[12], (4, D), (0.555 / PARAMS ** 0.5), 0.0029296875, (), jnp.float32),
        "mix_second": jnp.clip(jnp.exp(math.log(2.96569950819503e-08) - 1.3843914 * jax.random.uniform(key_of[13], (D, 3 * D), jnp.float32) ** block_levels(key_of[13], (D, 3 * D), ((1, 32),), -0.2, 0.2)), 7.428371251450017e-09, 2.96569950819503e-08),
        "out_second": jnp.clip(jnp.exp(math.log(2.96569950819503e-08) - 1.3843914 * jax.random.uniform(key_of[14], (D, D), jnp.float32) ** block_levels(key_of[14], (D, D), ((0, 32),), -0.2, 0.2)), 7.428371251450017e-09, 2.96569950819503e-08),
        "up_second": jnp.clip(jnp.exp(math.log(2.96569950819503e-08) - 1.3843914 * jax.random.uniform(key_of[15], (D, FF), jnp.float32) ** block_levels(key_of[15], (D, FF), ((1, 32),), -0.2, 0.2)), 7.428371251450017e-09, 2.96569950819503e-08),
        "down_second": jnp.clip(jnp.exp(math.log(2.96569950819503e-08) - 1.3843914 * jax.random.uniform(key_of[16], (FF, D), jnp.float32) ** block_levels(key_of[16], (FF, D), ((0, 32),), -0.2, 0.2)), 7.428371251450017e-09, 2.96569950819503e-08),
        "norm_second": jnp.clip(jnp.exp(jax.random.uniform(key_of[17], (4, D), jnp.float32, math.log(1.8359092734954174e-07), math.log(7.484860589102027e-07))), 1.8359092734954174e-07, 7.484860589102027e-07),
    }


HIGH = lax.Precision.HIGHEST
RATES = (0.01, 0.08, 0.01, 0.01, 0.2)
DECAYS = (0.1, 0.1, 0.1, 0.1, 0.0)

@jax.custom_vjp
def low(v):
    return lax.optimization_barrier(v.astype(jnp.bfloat16)).astype(jnp.float32)

@jax.custom_vjp
def low_back(v):
    return v

def low_keep(v):
    return (low(v), None)

def low_pass(kept, grad):
    return (grad,)

def back_keep(v):
    return (v, None)

def back_low(kept, grad):
    return (low(grad),)
low.defvjp(low_keep, low_pass)
low_back.defvjp(back_keep, back_low)

def segment_tables(lengths, rows):
    ends = jnp.cumsum(lengths).astype(jnp.int32)
    starts = ends - lengths
    places = jnp.arange(rows, dtype=jnp.int32)
    inside = (places[None, :] >= starts[:, None]) & (places[None, :] < ends[:, None])
    member = inside[:-1].astype(jnp.float32)
    live = lax.optimization_barrier(jnp.sum(member, axis=0))
    offset = places.astype(jnp.float32) - lax.optimization_barrier(jnp.sum(member * starts[:-1, None].astype(jnp.float32), axis=0))
    extent = lax.optimization_barrier(jnp.sum(member * lengths[:-1, None].astype(jnp.float32), axis=0)) + (1.0 - live)
    angle = 0.5 * math.pi * offset / extent
    return (member, live, angle)

def cos_attention(queries, keys, values, member, live, angle):
    rows = queries.shape[0]
    feat_q = jax.nn.softplus(queries).reshape(rows, -1, DH)
    feat_k = jax.nn.softplus(keys).reshape(rows, -1, DH)
    vals = values.reshape(rows, -1, DH)
    phases = jnp.stack([jnp.cos(angle), jnp.sin(angle)])
    weighted = member[None] * phases[:, None, :]
    scaled = jnp.einsum('psr,rhd->psrhd', weighted, feat_k)
    state = jnp.einsum('psrhd,rhe->pshde', scaled, vals, precision=HIGH)
    normal = lax.optimization_barrier(jnp.sum(scaled, axis=2))
    query_side = feat_q[None] * phases[:, :, None, None]
    per_slot = jnp.einsum('prhd,pshde->rshe', query_side, state, precision=HIGH)
    numer = jnp.einsum('sr,rshe->rhe', member, per_slot, precision=HIGH)
    slot_den = jnp.einsum('prhd,pshd->rsh', query_side, normal, precision=HIGH)
    denom = jnp.einsum('sr,rsh->rh', member, slot_den, precision=HIGH) + (1.0 - live)[:, None]
    return (numer / denom[:, :, None]).reshape(rows, -1)

def layer_norm(hidden, gain, shift):
    centered = hidden - lax.optimization_barrier(jnp.mean(hidden, axis=-1, keepdims=True))
    spread = lax.optimization_barrier(jnp.mean(centered * centered, axis=-1, keepdims=True))
    return centered * lax.rsqrt(spread + 1e-05) * gain + shift

def layer(tokens, mix_weight, out_weight, up_weight, down_weight, norm_params, member, live, angle):
    width = tokens.shape[1]
    mixed = low_back(jnp.dot(tokens, low(mix_weight), precision=HIGH))
    attended = low(cos_attention(mixed[:, :width], mixed[:, width:2 * width], mixed[:, 2 * width:], member, live, angle))
    branch = low_back(jnp.dot(attended, low(out_weight), precision=HIGH))
    first = layer_norm(tokens + branch, norm_params[0], norm_params[1])
    upper = low_back(jnp.dot(low(first), low(up_weight), precision=HIGH))
    hidden = low(jax.nn.gelu(upper, approximate=True))
    second = low_back(jnp.dot(hidden, low(down_weight), precision=HIGH))
    final = layer_norm(first + second, norm_params[2], norm_params[3])
    return final * live[:, None]

def adamw(weight, grad, first, second, rate, decay):
    first_new = 0.9 * first + 0.1 * grad
    second_new = 0.95 * second + 0.05 * grad * grad
    step_dir = first_new / (1.0 - 0.9 ** STEP) / (jnp.sqrt(second_new / (1.0 - 0.95 ** STEP)) + 1e-08)
    return (weight - rate * (step_dir + decay * weight), first_new, second_new)

def reference(tokens, cotangent, lengths, mix_weight, out_weight, up_weight, down_weight, norm_params, mix_first, out_first, up_first, down_first, norm_first, mix_second, out_second, up_second, down_second, norm_second):
    params = (mix_weight, out_weight, up_weight, down_weight, norm_params)
    width = tokens.shape[1]
    token_blocks = tokens.reshape(-1, ROWS, width)
    cot_blocks = cotangent.reshape(-1, ROWS, width)

    def one_buffer(totals, inputs):
        block, cot_block, length_row = inputs
        member, live, angle = segment_tables(length_row, ROWS)

        def forward(inp, mix_w, out_w, up_w, down_w, norms):
            return layer(inp, mix_w, out_w, up_w, down_w, norms, member, live, angle)
        result, pull = jax.vjp(forward, block.astype(jnp.float32), *params)
        grads = pull(cot_block.astype(jnp.float32))
        totals = tuple((acc + g for acc, g in zip(totals, grads[1:])))
        return (totals, (result.astype(jnp.bfloat16), grads[0]))
    start = tuple((jnp.zeros_like(p) for p in params))
    totals, (outputs, input_grads) = lax.scan(one_buffer, start, (token_blocks, cot_blocks, lengths))
    total_sq = sum((jnp.sum(g * g) for g in totals))
    global_norm = jnp.sqrt(total_sq)
    scale = 1.0 / jnp.maximum(global_norm, 1.0)
    firsts = (mix_first, out_first, up_first, down_first, norm_first)
    seconds = (mix_second, out_second, up_second, down_second, norm_second)
    news = []
    for index in range(5):
        news.append(adamw(params[index], scale * totals[index], firsts[index], seconds[index], RATES[index], DECAYS[index]))
    return (outputs.reshape(-1, width), input_grads.reshape(-1, width), global_norm, news[0][0], news[1][0], news[2][0], news[3][0], news[4][0], news[0][1], news[1][1], news[2][1], news[3][1], news[4][1], news[0][2], news[1][2], news[2][2], news[3][2], news[4][2])
```

```python
import math

import jax
import jax.numpy as jnp
from jax import lax
from jax.experimental import pallas as pl
from jax.experimental.pallas import tpu as pltpu
from jax.sharding import PartitionSpec as P

DH = 64
STEP = 10


HIGH = lax.Precision.HIGHEST
RATES = (0.01, 0.08, 0.01, 0.01, 0.2)
DECAYS = (0.1, 0.1, 0.1, 0.1, 0.0)


def segment_tables(lengths, rows):
    ends = jnp.cumsum(lengths)
    starts = ends - lengths
    places = jnp.arange(rows, dtype=jnp.int32)
    inside = (places[None, :] >= starts[:, None]) & (places[None, :] < ends[:, None])
    member = inside[:-1].astype(jnp.float32)
    live = jnp.sum(member, axis=0)
    offset = places.astype(jnp.float32) - jnp.sum(
        member * starts[:-1, None].astype(jnp.float32), axis=0
    )
    extent = jnp.sum(member * lengths[:-1, None].astype(jnp.float32), axis=0) + (1.0 - live)
    angle = 0.5 * math.pi * offset / extent
    return (member, live, angle)


def cos_attention(queries, keys, values, member, live, angle):
    rows = queries.shape[0]
    feat_q = jax.nn.softplus(queries).reshape(rows, -1, DH)
    feat_k = jax.nn.softplus(keys).reshape(rows, -1, DH)
    vals = values.reshape(rows, -1, DH)
    phases = jnp.stack([jnp.cos(angle), jnp.sin(angle)])
    weighted = member[None] * phases[:, None, :]
    scaled = jnp.einsum("psr,rhd->psrhd", weighted, feat_k)
    state = jnp.einsum("psrhd,rhe->pshde", scaled, vals, precision=HIGH)
    normal = jnp.sum(scaled, axis=2)
    query_side = feat_q[None] * phases[:, :, None, None]
    per_slot = jnp.einsum("prhd,pshde->rshe", query_side, state, precision=HIGH)
    numer = jnp.einsum("sr,rshe->rhe", member, per_slot, precision=HIGH)
    slot_den = jnp.einsum("prhd,pshd->rsh", query_side, normal, precision=HIGH)
    denom = jnp.einsum("sr,rsh->rh", member, slot_den, precision=HIGH) + (1.0 - live)[:, None]
    return (numer / denom[:, :, None]).reshape(rows, -1)


def layer_norm(hidden, gain, shift):
    centered = hidden - jnp.mean(hidden, axis=-1, keepdims=True)
    spread = jnp.mean(centered * centered, axis=-1, keepdims=True)
    return centered * lax.rsqrt(spread + 1e-05) * gain + shift


def gelu_tanh(values):
    return jax.nn.gelu(values, approximate=True)


def inner_rows(left, right):
    return lax.dot_general(
        left, right, (((0,), (0,)), ((), ())), preferred_element_type=jnp.float32
    )


def times_transpose(left, right):
    return lax.dot_general(
        left, right, (((1,), (1,)), ((), ())), preferred_element_type=jnp.float32
    )


def by_owner_rows(grad, owners):
    return grad.reshape(owners, -1, 128)


def by_owner_columns(grad, owners):
    height, across = grad.shape
    split = grad.reshape(height, owners, across // owners)
    return jnp.transpose(split, (1, 0, 2)).reshape(owners, -1, 128)


def unpack_owned(packed, shapes):
    pieces = []
    offset = 0
    for shape in shapes:
        blocks = shape[0] * shape[1] // 128
        pieces.append(packed[0, offset : offset + blocks].reshape(shape))
        offset = offset + blocks
    return pieces


def adamw(weight, grad, first, second, rate, decay):
    first_new = 0.9 * first + 0.1 * grad
    second_new = 0.95 * second + 0.05 * grad * grad
    step_dir = first_new / (1.0 - 0.9**STEP) / (jnp.sqrt(second_new / (1.0 - 0.95**STEP)) + 1e-08)
    return (weight - rate * (step_dir + decay * weight), first_new, second_new)


def on_device(
    tokens,
    cotangent,
    lengths,
    mix_weight,
    out_weight,
    up_weight,
    down_weight,
    norm_params,
    mix_first,
    out_first,
    up_first,
    down_first,
    norm_first,
    mix_second,
    out_second,
    up_second,
    down_second,
    norm_second,
):
    rows, width = tokens.shape
    owners = lax.axis_size(("dp", "fsdp"))
    rounded = (
        mix_weight.astype(jnp.bfloat16),
        out_weight.astype(jnp.bfloat16),
        up_weight.astype(jnp.bfloat16),
        down_weight.astype(jnp.bfloat16),
    )
    mix_full, out_full, up_full, down_full = (
        lax.all_gather(rounded[0], ("dp", "fsdp"), axis=1, tiled=True),
        lax.all_gather(rounded[1], ("dp", "fsdp"), axis=0, tiled=True),
        lax.all_gather(rounded[2], ("dp", "fsdp"), axis=1, tiled=True),
        lax.all_gather(rounded[3], ("dp", "fsdp"), axis=0, tiled=True),
    )
    member, live, angle = segment_tables(lengths[0], rows)
    mixed = jnp.dot(tokens, mix_full, preferred_element_type=jnp.float32)

    def attend(queries, keys, values):
        return cos_attention(queries, keys, values, member, live, angle)

    attended, attention_pull = jax.vjp(
        attend, mixed[:, :width], mixed[:, width : 2 * width], mixed[:, 2 * width :]
    )
    attended_low = attended.astype(jnp.bfloat16)
    branch = jnp.dot(attended_low, out_full, preferred_element_type=jnp.float32)
    first, first_pull = jax.vjp(
        layer_norm, tokens.astype(jnp.float32) + branch, norm_params[0], norm_params[1]
    )
    first_low = first.astype(jnp.bfloat16)
    upper = jnp.dot(first_low, up_full, preferred_element_type=jnp.float32)
    hidden, gelu_pull = jax.vjp(gelu_tanh, upper)
    hidden_low = hidden.astype(jnp.bfloat16)
    second = jnp.dot(hidden_low, down_full, preferred_element_type=jnp.float32)
    final, final_pull = jax.vjp(layer_norm, first + second, norm_params[2], norm_params[3])
    output = (final * live[:, None]).astype(jnp.bfloat16)
    mix_full, out_full, up_full, down_full = (
        lax.all_gather(rounded[0], ("dp", "fsdp"), axis=1, tiled=True),
        lax.all_gather(rounded[1], ("dp", "fsdp"), axis=0, tiled=True),
        lax.all_gather(rounded[2], ("dp", "fsdp"), axis=1, tiled=True),
        lax.all_gather(rounded[3], ("dp", "fsdp"), axis=0, tiled=True),
    )
    grad_final = cotangent.astype(jnp.float32) * live[:, None]
    grad_sum_two, grad_gain_two, grad_bias_two = final_pull(grad_final)
    grad_second = grad_sum_two.astype(jnp.bfloat16)
    grad_down = inner_rows(hidden_low, grad_second)
    grad_hidden = times_transpose(grad_second, down_full)
    (grad_upper,) = gelu_pull(grad_hidden)
    grad_upper_low = grad_upper.astype(jnp.bfloat16)
    grad_up = inner_rows(first_low, grad_upper_low)
    grad_first = grad_sum_two + times_transpose(grad_upper_low, up_full)
    grad_sum_one, grad_gain_one, grad_bias_one = first_pull(grad_first)
    grad_branch = grad_sum_one.astype(jnp.bfloat16)
    grad_out = inner_rows(attended_low, grad_branch)
    grad_attended = times_transpose(grad_branch, out_full)
    grad_q, grad_k, grad_v = attention_pull(grad_attended)
    grad_mixed = jnp.concatenate([grad_q, grad_k, grad_v], axis=1).astype(jnp.bfloat16)
    grad_mix = inner_rows(tokens, grad_mixed)
    grad_tokens = grad_sum_one + times_transpose(grad_mixed, mix_full)
    norm_terms = jnp.stack([grad_gain_one, grad_bias_one, grad_gain_two, grad_bias_two])
    norm_grad = lax.psum(norm_terms, ("dp", "fsdp"))
    packed_all = jnp.concatenate(
        [
            by_owner_columns(grad_mix, owners),
            by_owner_rows(grad_out, owners),
            by_owner_columns(grad_up, owners),
            by_owner_rows(grad_down, owners),
        ],
        axis=1,
    )
    summed_all = lax.psum_scatter(packed_all, ("dp", "fsdp"), scatter_dimension=0, tiled=True)
    owned = tuple(
        unpack_owned(
            summed_all, (mix_weight.shape, out_weight.shape, up_weight.shape, down_weight.shape)
        )
    )
    local_sq = sum((jnp.sum(g * g) for g in owned))
    owned_sq = lax.psum(local_sq, ("dp", "fsdp"))
    global_norm = jnp.sqrt(owned_sq + jnp.sum(norm_grad * norm_grad))
    scale = 1.0 / jnp.maximum(global_norm, 1.0)
    params = (mix_weight, out_weight, up_weight, down_weight, norm_params)
    grads = (owned[0], owned[1], owned[2], owned[3], norm_grad)
    firsts = (mix_first, out_first, up_first, down_first, norm_first)
    seconds = (mix_second, out_second, up_second, down_second, norm_second)
    news = []
    for index in range(5):
        news.append(
            adamw(
                params[index],
                scale * grads[index],
                firsts[index],
                seconds[index],
                RATES[index],
                DECAYS[index],
            )
        )
    return (
        output,
        grad_tokens,
        global_norm,
        news[0][0],
        news[1][0],
        news[2][0],
        news[3][0],
        news[4][0],
        news[0][1],
        news[1][1],
        news[2][1],
        news[3][1],
        news[4][1],
        news[0][2],
        news[1][2],
        news[2][2],
        news[3][2],
        news[4][2],
    )


BF = jnp.bfloat16
F32 = jnp.float32
AXES = ("dp", "fsdp")
CHIPS = 16
BLOCK = 96
QKV = 72
PLANE = 4 * BLOCK
ZROWS = 3 * BLOCK
HALF = CHIPS * BLOCK
STEPS_Z = (4, 8, 12)


def nt(left, right):
    return lax.dot_general(
        left, right, (((1,), (1,)), ((), ())), preferred_element_type=F32
    )


def tn(left, right):
    return lax.dot_general(
        left, right, (((0,), (0,)), ((), ())), preferred_element_type=F32
    )


def nn(left, right):
    return jnp.dot(left, right, preferred_element_type=F32)


def block_places():
    places = [(BLOCK * p, p, 0) for p in range(4)]
    for p in range(4):
        for j, step in enumerate(STEPS_Z):
            places.append((PLANE + ZROWS * p + BLOCK * j, p, step))
    return places


PLACES = block_places()
PIECES = [(0, PLANE)] + [(PLANE + ZROWS * p, ZROWS) for p in range(4)]


def shard_index(chip, core, plane, step, other):
    owner = 1 - core if other else core
    first = 1 + owner
    mask = (0, first, 3 - first, 3)[plane]
    return 2 * (chip ^ mask ^ step) + owner


def call(body, outs, args, scratch=(), smem=0, flops=0, moved=0, mb=56):
    in_specs = [
        pl.BlockSpec(memory_space=pltpu.SMEM if i < smem else pltpu.VMEM)
        for i in range(len(args))
    ]
    return pl.pallas_call(
        body,
        out_shape=[jax.ShapeDtypeStruct(s, t) for s, t in outs],
        in_specs=in_specs,
        out_specs=[pl.BlockSpec(memory_space=pltpu.VMEM) for _ in outs],
        scratch_shapes=list(scratch),
        compiler_params=pltpu.CompilerParams(vmem_limit_bytes=mb << 20),
        cost_estimate=pl.CostEstimate(flops=flops, bytes_accessed=moved, transcendentals=0),
        name=body.__name__,
    )(*args)


def pack_weights(mix, out, up, down, s_ref, g1, g2, g3):
    def flip(ref):
        held = ref[...].astype(BF)
        n = held.shape[1]
        eye = (
            lax.broadcasted_iota(jnp.int32, (n, n), 0)
            == lax.broadcasted_iota(jnp.int32, (n, n), 1)
        )
        return nt(eye.astype(F32).astype(BF), held)

    first = jnp.concatenate([flip(mix), out[...]], axis=0).astype(BF)
    second = flip(up).astype(BF)
    third = down[...].astype(BF)
    s_ref[0:BLOCK, :] = first
    s_ref[BLOCK : 2 * BLOCK, :] = second
    s_ref[2 * BLOCK : 3 * BLOCK, :] = third
    g1[...] = first
    g2[...] = second
    g3[...] = third


def segment_of(lengths, place):
    start = jnp.int32(0)
    seg = jnp.full(place.shape, -1, jnp.int32)
    offset = jnp.zeros(place.shape, F32)
    extent = jnp.ones(place.shape, F32)
    for s in range(5):
        size = lengths[0, s]
        inside = (place >= start) & (place < start + size)
        seg = jnp.where(inside, s, seg)
        offset = jnp.where(inside, (place - start).astype(F32), offset)
        extent = jnp.where(inside, size.astype(F32), extent)
        start = start + size
    angle = 0.5 * math.pi * offset / extent
    return seg, jnp.cos(angle), jnp.sin(angle)


def pair_mask(lengths, rows):
    seg_i, cos_i, sin_i = segment_of(lengths, lax.broadcasted_iota(jnp.int32, (1, rows), 1))
    seg_j, cos_j, sin_j = segment_of(lengths, lax.broadcasted_iota(jnp.int32, (rows, 1), 0))
    same = (seg_i == seg_j) & (seg_i >= 0)
    dead = jnp.where(seg_i >= 0, 0.0, 1.0)
    return jnp.where(same, cos_j * cos_i + sin_j * sin_i, 0.0), dead


def softplus(v):
    return jnp.maximum(v, 0.0) + jnp.log1p(jnp.exp(-jnp.abs(v)))


def attend_forward(
    lengths, me, x_ref, so, z0, z1, z2, z3, sp, y0, y1, y2, y3, norms,
    mix, att, den, rel_own, rel_par, first, first_low, xhat, rstd,
):
    rows = x_ref.shape[0]
    width = x_ref.shape[1]
    chip, core = me[0], me[1]
    x = x_ref[...]
    sides = ((False, (so, z0, z1, z2, z3), rel_own), (True, (sp, y0, y1, y2, y3), rel_par))
    for other, refs, _ in sides:
        for (base, size), ref in zip(PIECES, refs):
            got = nt(ref[...], x)
            for at, plane, step in PLACES:
                if base <= at < base + size:
                    d = shard_index(chip, core, plane, step, other)
                    mix[pl.ds(pl.multiple_of(QKV * d, 8), QKV), :] = got[
                        at - base : at - base + QKV
                    ]
    mask, dead = pair_mask(lengths, rows)
    for h in range(width // DH):
        here = slice(DH * h, DH * h + DH)
        fq = softplus(mix[here, :]).astype(BF)
        fk = softplus(mix[width + DH * h : width + DH * h + DH, :]).astype(BF)
        v = mix[2 * width + DH * h : 2 * width + DH * h + DH, :].astype(BF)
        pairs = tn(fk, fq) * mask
        total = jnp.sum(pairs, axis=0, keepdims=True) + dead
        den[h : h + 1, :] = total
        att[here, :] = nn(v, pairs.astype(BF)) / total
    side = QKV // 3
    blank = jnp.zeros((QKV, rows), F32)
    branch = x.astype(F32)
    for other, refs, rel in sides:
        for at, plane, step in PLACES:
            d = shard_index(chip, core, plane, step, other)
            part = att[pl.ds(pl.multiple_of(side * d, 8), side), :]
            rel[at : at + BLOCK, :] = jnp.concatenate([blank, part], axis=0).astype(BF)
        for (base, size), ref in zip(PIECES, refs):
            branch = branch + tn(rel[base : base + size, :], ref[...])
    centered = branch - jnp.mean(branch, axis=-1, keepdims=True)
    spread = jnp.mean(centered * centered, axis=-1, keepdims=True)
    scale = lax.rsqrt(spread + 1e-05)
    hat = centered * scale
    xhat[...] = hat
    rstd[...] = scale
    out = hat * norms[0:1, :] + norms[1:2, :]
    first[...] = out
    first_low[...] = out.astype(BF)


GELU_A = math.sqrt(2.0 / math.pi)
GELU_B = 0.044715


def feed_up(ya, yb, s, z0, z1, z2, z3, hid, slope):
    rows = ya.shape[0]
    for half, y in ((0, ya), (1, yb)):
        cols = slice(half * rows, half * rows + rows)
        for (base, size), ref in zip(PIECES, (s, z0, z1, z2, z3)):
            u = nt(ref[...], y[...])
            sq = u * u
            t = jnp.tanh(GELU_A * u * (1.0 + GELU_B * sq))
            half_up = 0.5 * (1.0 + t)
            hid[base : base + size, cols] = (u * half_up).astype(BF)
            slope[base : base + size, cols] = half_up + 0.5 * u * (1.0 - t * t) * (
                GELU_A * (1.0 + 3.0 * GELU_B * sq)
            )


def feed_down(hid, s, z0, z1, z2, z3, own, other, whole):
    for (base, size), ref in zip(PIECES, (s, z0, z1, z2, z3)):
        whole[base : base + size, :] = ref[...]
    rows = own.shape[0]
    w = whole[...]
    own[...] = tn(hid[:, 0:rows], w)
    other[...] = tn(hid[:, rows : 2 * rows], w)


def norm_back(dy, gain, hat, scale):
    dhat = dy * gain
    return scale * (
        dhat
        - jnp.mean(dhat, axis=-1, keepdims=True)
        - hat * jnp.mean(dhat * hat, axis=-1, keepdims=True)
    )


def finish_forward(lengths, first, own, got, cot, norms, out, ds2, dz, terms):
    rows = first.shape[0]
    used = jnp.int32(0)
    for s in range(5):
        used = used + lengths[0, s]
    live = jnp.where(lax.broadcasted_iota(jnp.int32, (rows, 1), 0) < used, 1.0, 0.0)
    h = first[...] + (own[...] + got[...])
    centered = h - jnp.mean(h, axis=-1, keepdims=True)
    spread = jnp.mean(centered * centered, axis=-1, keepdims=True)
    scale = lax.rsqrt(spread + 1e-05)
    hat = centered * scale
    out[...] = ((hat * norms[2:3, :] + norms[3:4, :]) * live).astype(BF)
    dy = cot[...].astype(F32) * live
    back = norm_back(dy, norms[2:3, :], hat, scale)
    ds2[...] = back
    dz[...] = back.astype(BF)
    terms[0:1, :] = jnp.sum(dy * hat, axis=0, keepdims=True)
    terms[1:2, :] = jnp.sum(dy, axis=0, keepdims=True)


def spread_rows(get, send, turn, own):
    goals = ((own, 0), (turn, 0), (send, 0), (send, PLANE))
    for base, size in PIECES:
        g = get(base, size)
        if base == 0:
            for p, (ref, off) in enumerate(goals):
                ref[off : off + BLOCK, :] = g[BLOCK * p : BLOCK * p + BLOCK].astype(ref.dtype)
        else:
            ref, off = goals[(base - PLANE) // ZROWS]
            ref[off + BLOCK : off + PLANE, :] = g.astype(ref.dtype)


def grad_down(hid, za, zb, send, turn, own):
    rows = za.shape[0]

    def get(base, size):
        return nn(hid[base : base + size, 0:rows], za[...]) + nn(
            hid[base : base + size, rows : 2 * rows], zb[...]
        )

    spread_rows(get, send, turn, own)


def grad_up(
    slope, za, zb, ya, yb, s, z0, z1, z2, z3, s2, v0, v1, v2, v3,
    send, turn, own, mine, other, dup, whole,
):
    rows = za.shape[0]
    for (base, size), ref, ref2 in zip(PIECES, (s, z0, z1, z2, z3), (s2, v0, v1, v2, v3)):
        here = slice(base, base + size)
        whole[here, :] = ref2[...]
        dup[here, 0:rows] = (nt(ref[...], za[...]) * slope[here, 0:rows]).astype(BF)
        dup[here, rows:] = (nt(ref[...], zb[...]) * slope[here, rows:]).astype(BF)

    def get(base, size):
        return nn(dup[base : base + size, 0:rows], ya[...]) + nn(
            dup[base : base + size, rows : 2 * rows], yb[...]
        )

    spread_rows(get, send, turn, own)
    w = whole[...]
    mine[...] = tn(dup[:, 0:rows], w)
    other[...] = tn(dup[:, rows : 2 * rows], w)


def attend_backward(
    lengths, me, ds2, mine, got, xhat, rstd, norms, mix, att, den,
    so, z0, z1, z2, z3, sp, y0, y1, y2, y3,
    dh_ref, do_ref, terms, rel_own, rel_par, datt, dmix,
):
    rows, width = ds2.shape
    chip, core = me[0], me[1]
    dy1 = ds2[...] + (mine[...] + got[...])
    hat = xhat[...]
    terms[0:1, :] = jnp.sum(dy1 * hat, axis=0, keepdims=True)
    terms[1:2, :] = jnp.sum(dy1, axis=0, keepdims=True)
    dh = norm_back(dy1, norms[0:1, :], hat, rstd[...])
    dh_ref[...] = dh
    do = dh.astype(BF)
    do_ref[...] = do
    side = QKV // 3
    sides = ((False, (so, z0, z1, z2, z3), rel_own), (True, (sp, y0, y1, y2, y3), rel_par))
    for other, refs, _ in sides:
        for (base, size), ref in zip(PIECES, refs):
            got_t = nt(ref[...], do)
            for at, plane, step in PLACES:
                if base <= at < base + size:
                    d = shard_index(chip, core, plane, step, other)
                    datt[pl.ds(pl.multiple_of(side * d, 8), side), :] = got_t[
                        at - base + QKV : at - base + BLOCK
                    ]
    mask, _ = pair_mask(lengths, rows)
    for h in range(width // DH):
        here = slice(DH * h, DH * h + DH)
        q = mix[here, :]
        k = mix[width + DH * h : width + DH * h + DH, :]
        v = mix[2 * width + DH * h : 2 * width + DH * h + DH, :].astype(BF)
        fq = softplus(q).astype(BF)
        fk = softplus(k).astype(BF)
        pairs = (tn(fk, fq) * mask).astype(BF)
        da = datt[here, :]
        total = den[h : h + 1, :]
        dnum = da / total
        dden = -jnp.sum(dnum * att[here, :], axis=0, keepdims=True)
        dnum = dnum.astype(BF)
        dpairs = ((tn(v, dnum) + dden) * mask).astype(BF)
        dmix[2 * width + DH * h : 2 * width + DH * h + DH, :] = nt(dnum, pairs)
        dmix[width + DH * h : width + DH * h + DH, :] = nt(fq, dpairs) * jax.nn.sigmoid(k)
        dmix[here, :] = nn(fk, dpairs) * jax.nn.sigmoid(q)
    blank = jnp.zeros((BLOCK - QKV, rows), F32)
    for other, _, rel in sides:
        for at, plane, step in PLACES:
            d = shard_index(chip, core, plane, step, other)
            part = dmix[pl.ds(pl.multiple_of(QKV * d, 8), QKV), :]
            rel[at : at + BLOCK, :] = jnp.concatenate([part, blank], axis=0).astype(BF)


def grad_mix(dma, dmb, xa, xb, ata, atb, doa, dob, send, turn, own):
    def get(base, size):
        here = slice(base, base + size)
        return (nn(dma[here, :], xa[...]) + nn(dmb[here, :], xb[...])) + (
            nn(ata[here, :], doa[...]) + nn(atb[here, :], dob[...])
        )

    spread_rows(get, send, turn, own)


def grad_input(dh, rel_own, rel_par, so, z0, z1, z2, z3, sp, y0, y1, y2, y3, out):
    total = dh[...]
    for refs, rel in (((so, z0, z1, z2, z3), rel_own), ((sp, y0, y1, y2, y3), rel_par)):
        for (base, size), ref in zip(PIECES, refs):
            total = total + tn(rel[base : base + size, :], ref[...])
    out[...] = total


def close_sums(k1, a1, b1, c1, g2, g3, t1, t2, g1, note):
    s1 = (k1[...] + a1[...].astype(F32)) + (b1[...].astype(F32) + c1[...].astype(F32))
    g1[...] = s1
    sq = s1 * s1 + g2[...] * g2[...] + g3[...] * g3[...]
    note[0:2, :] = t1[...]
    note[2:4, :] = t2[...]
    note[4:5, :] = jnp.sum(sq, axis=0, keepdims=True)
    note[5:8, :] = jnp.zeros((3, note.shape[1]), F32)


def update(
    note, g1, g2, g3, mw, ow, uw, dw, nw, mm, om, um, dm, nm, mv, ov, uv, dv, nv,
    norm_out, mw2, ow2, uw2, dw2, nw2, mm2, om2, um2, dm2, nm2, mv2, ov2, uv2, dv2, nv2,
):
    terms = note[0:4, :]
    total = jnp.sum(note[4:5, :]) + jnp.sum(terms * terms)
    norm = jnp.sqrt(jnp.full((1, 1), total, F32))
    norm_out[...] = norm
    scale = 1.0 / jnp.maximum(norm, 1.0)

    def flip(v):
        n, width = v.shape
        padded = jnp.concatenate([v, jnp.zeros((128 - n, width), F32)], axis=0)
        return padded.T[:, 0:n]

    one = g1[...]
    grads = (flip(one[0:QKV]), one[QKV:BLOCK], flip(g2[...]), g3[...], terms)
    groups = (
        (mw, mm, mv, mw2, mm2, mv2),
        (ow, om, ov, ow2, om2, ov2),
        (uw, um, uv, uw2, um2, uv2),
        (dw, dm, dv, dw2, dm2, dv2),
        (nw, nm, nv, nw2, nm2, nv2),
    )
    for g, (w, m, v, w2, m2, v2), rate, decay in zip(grads, groups, RATES, DECAYS):
        new_w, new_m, new_v = adamw(w[...], scale * g, m[...], v[...], rate, decay)
        w2[...] = new_w
        m2[...] = new_m
        v2[...] = new_v


def tie(value, *others):
    return lax.optimization_barrier((value,) + others)[0]


def swap(value):
    return lax.ppermute(value, "fsdp", [(0, 1), (1, 0)])


def hop_first(value):
    return lax.ppermute(value, AXES, [(i, i ^ (4 if i % 2 else 2)) for i in range(2 * CHIPS)])


def hop_second(value):
    return lax.ppermute(value, AXES, [(i, i ^ (2 if i % 2 else 4)) for i in range(2 * CHIPS)])


def hop_z(value, step):
    return lax.ppermute(value, "dp", [(i, i ^ step) for i in range(CHIPS)])


def spread_plane(value):
    turned = hop_first(value)
    across = hop_second(value)
    return value, turned, across, hop_second(turned)


def reduce_group(send, turn, own):
    got = hop_second(send)
    turned = (turn + got[PLANE:].astype(F32)).astype(BF)
    back = hop_first(turned)
    total = own + got[:PLANE].astype(F32) + back.astype(F32)
    low = total.astype(BF)
    parts = [
        hop_z(low[BLOCK * (j + 1) : BLOCK * (j + 2)], step) for j, step in enumerate(STEPS_Z)
    ]
    return total[:BLOCK], parts


def tuned_device(
    tokens, cotangent, lengths,
    mix_weight, out_weight, up_weight, down_weight, norm_params,
    mix_first, out_first, up_first, down_first, norm_first,
    mix_second, out_second, up_second, down_second, norm_second,
):
    rows, width = tokens.shape
    chip, core = lax.axis_index("dp"), lax.axis_index("fsdp")
    me = jnp.stack([chip, core]).astype(jnp.int32)
    wide = 3 * width

    s_all, *blocks = call(
        pack_weights,
        [((3 * BLOCK, width), BF)] + [((BLOCK, width), BF)] * 3,
        (mix_weight, out_weight, up_weight, down_weight),
        flops=1 << 20, moved=3 << 20,
    )
    s_parts = spread_plane(s_all)
    z_parts = []
    gate = ()
    link = ()
    for group in range(3):
        block = tie(blocks[group], *gate) if gate else blocks[group]
        arrived = [hop_z(block, step) for step in STEPS_Z]
        gate = (arrived[2],)
        joined = jnp.concatenate(arrived, axis=0)
        if link:
            joined = tie(joined, *link)
        z_parts.append(spread_plane(joined))
        link = (z_parts[-1][2],)
    s_groups = [
        jnp.concatenate([p[BLOCK * g : BLOCK * g + BLOCK] for p in s_parts], axis=0)
        for g in range(3)
    ]
    weights = [(s_groups[g],) + tuple(z_parts[g]) for g in range(3)]
    attn_own = weights[0]
    attn_par = tuple(swap(p) for p in attn_own)
    x_par = swap(tokens)

    mix, att, den, at_own, at_par, first, first_low, xhat, rstd = call(
        attend_forward,
        [
            ((wide, rows), F32), ((width, rows), F32), ((16, rows), F32),
            ((HALF, rows), BF), ((HALF, rows), BF),
            ((rows, width), F32), ((rows, width), BF), ((rows, width), F32), ((rows, 1), F32),
        ],
        (lengths, me, tokens) + attn_own + attn_par + (norm_params,),
        smem=2, flops=12 << 30, moved=16 << 20,
    )
    at_got = swap(at_par)
    first_par = swap(first_low)
    hid, slope = call(
        feed_up,
        [((HALF, 2 * rows), BF), ((HALF, 2 * rows), F32)],
        (first_low, first_par) + weights[1],
        flops=4 << 30, moved=8 << 20,
    )
    down_own, down_par = call(
        feed_down,
        [((rows, width), F32)] * 2,
        (hid,) + weights[2],
        scratch=[pltpu.VMEM((HALF, width), BF)],
        flops=2 << 30, moved=6 << 20,
    )
    output, ds2, dz, terms_two = call(
        finish_forward,
        [((rows, width), BF), ((rows, width), F32), ((rows, width), BF), ((2, width), F32)],
        (lengths, first, down_own, swap(down_par), cotangent, norm_params),
        smem=1, flops=1 << 28, moved=6 << 20,
    )
    dz_par = swap(dz)
    spread_shapes = [((2 * PLANE, width), BF), ((PLANE, width), F32), ((PLANE, width), F32)]
    send3, turn3, own3 = call(
        grad_down, spread_shapes, (hid, dz, dz_par), flops=2 << 30, moved=6 << 20
    )
    keep3, parts3 = reduce_group(send3, turn3, own3)
    send2, turn2, own2, dy_own, dy_par = call(
        grad_up,
        spread_shapes + [((rows, width), F32)] * 2,
        (slope, dz, dz_par, first_low, first_par) + weights[2] + weights[1],
        scratch=[pltpu.VMEM((HALF, 2 * rows), BF), pltpu.VMEM((HALF, width), BF)],
        flops=5 << 30, moved=16 << 20,
    )
    keep2, parts2 = reduce_group(send2, turn2, own2)
    dh, do, terms_one, dm_own, dm_par = call(
        attend_backward,
        [
            ((rows, width), F32), ((rows, width), BF), ((2, width), F32),
            ((HALF, rows), BF), ((HALF, rows), BF),
        ],
        (lengths, me, ds2, dy_own, swap(dy_par), xhat, rstd, norm_params, mix, att, den)
        + attn_own + attn_par,
        scratch=[pltpu.VMEM((width, rows), F32), pltpu.VMEM((wide, rows), F32)],
        smem=2, flops=16 << 30, moved=20 << 20,
    )
    send1, turn1, own1 = call(
        grad_mix,
        spread_shapes,
        (dm_own, swap(dm_par), tokens, x_par, at_own, at_got, do, swap(do)),
        flops=3 << 30, moved=8 << 20,
    )
    keep1, parts1 = reduce_group(send1, turn1, own1)
    (grad_tokens,) = call(
        grad_input,
        [((rows, width), F32)],
        (dh, dm_own, dm_par) + attn_own + attn_par,
        flops=3 << 30, moved=9 << 20,
    )
    g3 = (keep3 + parts3[0]) + (parts3[1].astype(F32) + parts3[2].astype(F32))
    g2 = (keep2 + parts2[0]) + (parts2[1].astype(F32) + parts2[2].astype(F32))
    g1, note = call(
        close_sums,
        [((BLOCK, width), F32), ((8, width), F32)],
        (keep1,) + tuple(parts1) + (g2, g3, terms_one, terms_two),
        flops=1 << 22, moved=1 << 21,
    )
    note = note + swap(note)
    for step in (1, 2, 4, 8):
        note = note + hop_z(note, step)
    shapes = [
        (mix_weight.shape, F32), (out_weight.shape, F32), (up_weight.shape, F32),
        (down_weight.shape, F32), (norm_params.shape, F32),
    ]
    norm, *news = call(
        update,
        [((1, 1), F32)] + shapes * 3,
        (
            note, g1, g2, g3, mix_weight, out_weight, up_weight, down_weight, norm_params,
            mix_first, out_first, up_first, down_first, norm_first,
            mix_second, out_second, up_second, down_second, norm_second,
        ),
        flops=1 << 23, moved=8 << 20,
    )
    return (output, grad_tokens, norm.reshape(())) + tuple(news)


def solution(mesh):
    in_specs = (
        P(("dp", "fsdp"), None),
        P(("dp", "fsdp"), None),
        P(("dp", "fsdp"), None),
        P(None, ("dp", "fsdp")),
        P(("dp", "fsdp"), None),
        P(None, ("dp", "fsdp")),
        P(("dp", "fsdp"), None),
        P(),
        P(None, ("dp", "fsdp")),
        P(("dp", "fsdp"), None),
        P(None, ("dp", "fsdp")),
        P(("dp", "fsdp"), None),
        P(),
        P(None, ("dp", "fsdp")),
        P(("dp", "fsdp"), None),
        P(None, ("dp", "fsdp")),
        P(("dp", "fsdp"), None),
        P(),
    )
    out_specs = (
        P(("dp", "fsdp"), None),
        P(("dp", "fsdp"), None),
        P(),
        P(None, ("dp", "fsdp")),
        P(("dp", "fsdp"), None),
        P(None, ("dp", "fsdp")),
        P(("dp", "fsdp"), None),
        P(),
        P(None, ("dp", "fsdp")),
        P(("dp", "fsdp"), None),
        P(None, ("dp", "fsdp")),
        P(("dp", "fsdp"), None),
        P(),
        P(None, ("dp", "fsdp")),
        P(("dp", "fsdp"), None),
        P(None, ("dp", "fsdp")),
        P(("dp", "fsdp"), None),
        P(),
    )
    sizes = dict(mesh.shape)
    tuned = sizes["dp"] == CHIPS and sizes["fsdp"] == 2
    return jax.shard_map(
        tuned_device if tuned else on_device, mesh=mesh, in_specs=in_specs, out_specs=out_specs, check_vma=False
    )
```

```python
import math

import jax
import jax.numpy as jnp
from jax import lax
from jax.experimental import pallas as pl
from jax.experimental.pallas import tpu as pltpu
from jax.sharding import PartitionSpec as P

DH = 64
STEP = 10


HIGH = lax.Precision.HIGHEST
RATES = (0.01, 0.08, 0.01, 0.01, 0.2)
DECAYS = (0.1, 0.1, 0.1, 0.1, 0.0)


def segment_tables(lengths, rows):
    ends = jnp.cumsum(lengths)
    starts = ends - lengths
    places = jnp.arange(rows, dtype=jnp.int32)
    inside = (places[None, :] >= starts[:, None]) & (places[None, :] < ends[:, None])
    member = inside[:-1].astype(jnp.float32)
    live = jnp.sum(member, axis=0)
    offset = places.astype(jnp.float32) - jnp.sum(
        member * starts[:-1, None].astype(jnp.float32), axis=0
    )
    extent = jnp.sum(member * lengths[:-1, None].astype(jnp.float32), axis=0) + (1.0 - live)
    angle = 0.5 * math.pi * offset / extent
    return (member, live, angle)


def cos_attention(queries, keys, values, member, live, angle):
    rows = queries.shape[0]
    feat_q = jax.nn.softplus(queries).reshape(rows, -1, DH)
    feat_k = jax.nn.softplus(keys).reshape(rows, -1, DH)
    vals = values.reshape(rows, -1, DH)
    phases = jnp.stack([jnp.cos(angle), jnp.sin(angle)])
    weighted = member[None] * phases[:, None, :]
    scaled = jnp.einsum("psr,rhd->psrhd", weighted, feat_k)
    state = jnp.einsum("psrhd,rhe->pshde", scaled, vals, precision=HIGH)
    normal = jnp.sum(scaled, axis=2)
    query_side = feat_q[None] * phases[:, :, None, None]
    per_slot = jnp.einsum("prhd,pshde->rshe", query_side, state, precision=HIGH)
    numer = jnp.einsum("sr,rshe->rhe", member, per_slot, precision=HIGH)
    slot_den = jnp.einsum("prhd,pshd->rsh", query_side, normal, precision=HIGH)
    denom = jnp.einsum("sr,rsh->rh", member, slot_den, precision=HIGH) + (1.0 - live)[:, None]
    return (numer / denom[:, :, None]).reshape(rows, -1)


def layer_norm(hidden, gain, shift):
    centered = hidden - jnp.mean(hidden, axis=-1, keepdims=True)
    spread = jnp.mean(centered * centered, axis=-1, keepdims=True)
    return centered * lax.rsqrt(spread + 1e-05) * gain + shift


def gelu_tanh(values):
    return jax.nn.gelu(values, approximate=True)


def inner_rows(left, right):
    return lax.dot_general(
        left, right, (((0,), (0,)), ((), ())), preferred_element_type=jnp.float32
    )


def times_transpose(left, right):
    return lax.dot_general(
        left, right, (((1,), (1,)), ((), ())), preferred_element_type=jnp.float32
    )


def by_owner_rows(grad, owners):
    return grad.reshape(owners, -1, 128)


def by_owner_columns(grad, owners):
    height, across = grad.shape
    split = grad.reshape(height, owners, across // owners)
    return jnp.transpose(split, (1, 0, 2)).reshape(owners, -1, 128)


def unpack_owned(packed, shapes):
    pieces = []
    offset = 0
    for shape in shapes:
        blocks = shape[0] * shape[1] // 128
        pieces.append(packed[0, offset : offset + blocks].reshape(shape))
        offset = offset + blocks
    return pieces


def adamw(weight, grad, first, second, rate, decay):
    first_new = 0.9 * first + 0.1 * grad
    second_new = 0.95 * second + 0.05 * grad * grad
    step_dir = first_new / (1.0 - 0.9**STEP) / (jnp.sqrt(second_new / (1.0 - 0.95**STEP)) + 1e-08)
    return (weight - rate * (step_dir + decay * weight), first_new, second_new)


def on_device(
    tokens,
    cotangent,
    lengths,
    mix_weight,
    out_weight,
    up_weight,
    down_weight,
    norm_params,
    mix_first,
    out_first,
    up_first,
    down_first,
    norm_first,
    mix_second,
    out_second,
    up_second,
    down_second,
    norm_second,
):
    rows, width = tokens.shape
    owners = lax.axis_size(("dp", "fsdp"))
    rounded = (
        mix_weight.astype(jnp.bfloat16),
        out_weight.astype(jnp.bfloat16),
        up_weight.astype(jnp.bfloat16),
        down_weight.astype(jnp.bfloat16),
    )
    mix_full, out_full, up_full, down_full = (
        lax.all_gather(rounded[0], ("dp", "fsdp"), axis=1, tiled=True),
        lax.all_gather(rounded[1], ("dp", "fsdp"), axis=0, tiled=True),
        lax.all_gather(rounded[2], ("dp", "fsdp"), axis=1, tiled=True),
        lax.all_gather(rounded[3], ("dp", "fsdp"), axis=0, tiled=True),
    )
    member, live, angle = segment_tables(lengths[0], rows)
    mixed = jnp.dot(tokens, mix_full, preferred_element_type=jnp.float32)

    def attend(queries, keys, values):
        return cos_attention(queries, keys, values, member, live, angle)

    attended, attention_pull = jax.vjp(
        attend, mixed[:, :width], mixed[:, width : 2 * width], mixed[:, 2 * width :]
    )
    attended_low = attended.astype(jnp.bfloat16)
    branch = jnp.dot(attended_low, out_full, preferred_element_type=jnp.float32)
    first, first_pull = jax.vjp(
        layer_norm, tokens.astype(jnp.float32) + branch, norm_params[0], norm_params[1]
    )
    first_low = first.astype(jnp.bfloat16)
    upper = jnp.dot(first_low, up_full, preferred_element_type=jnp.float32)
    hidden, gelu_pull = jax.vjp(gelu_tanh, upper)
    hidden_low = hidden.astype(jnp.bfloat16)
    second = jnp.dot(hidden_low, down_full, preferred_element_type=jnp.float32)
    final, final_pull = jax.vjp(layer_norm, first + second, norm_params[2], norm_params[3])
    output = (final * live[:, None]).astype(jnp.bfloat16)
    mix_full, out_full, up_full, down_full = (
        lax.all_gather(rounded[0], ("dp", "fsdp"), axis=1, tiled=True),
        lax.all_gather(rounded[1], ("dp", "fsdp"), axis=0, tiled=True),
        lax.all_gather(rounded[2], ("dp", "fsdp"), axis=1, tiled=True),
        lax.all_gather(rounded[3], ("dp", "fsdp"), axis=0, tiled=True),
    )
    grad_final = cotangent.astype(jnp.float32) * live[:, None]
    grad_sum_two, grad_gain_two, grad_bias_two = final_pull(grad_final)
    grad_second = grad_sum_two.astype(jnp.bfloat16)
    grad_down = inner_rows(hidden_low, grad_second)
    grad_hidden = times_transpose(grad_second, down_full)
    (grad_upper,) = gelu_pull(grad_hidden)
    grad_upper_low = grad_upper.astype(jnp.bfloat16)
    grad_up = inner_rows(first_low, grad_upper_low)
    grad_first = grad_sum_two + times_transpose(grad_upper_low, up_full)
    grad_sum_one, grad_gain_one, grad_bias_one = first_pull(grad_first)
    grad_branch = grad_sum_one.astype(jnp.bfloat16)
    grad_out = inner_rows(attended_low, grad_branch)
    grad_attended = times_transpose(grad_branch, out_full)
    grad_q, grad_k, grad_v = attention_pull(grad_attended)
    grad_mixed = jnp.concatenate([grad_q, grad_k, grad_v], axis=1).astype(jnp.bfloat16)
    grad_mix = inner_rows(tokens, grad_mixed)
    grad_tokens = grad_sum_one + times_transpose(grad_mixed, mix_full)
    norm_terms = jnp.stack([grad_gain_one, grad_bias_one, grad_gain_two, grad_bias_two])
    norm_grad = lax.psum(norm_terms, ("dp", "fsdp"))
    packed_all = jnp.concatenate(
        [
            by_owner_columns(grad_mix, owners),
            by_owner_rows(grad_out, owners),
            by_owner_columns(grad_up, owners),
            by_owner_rows(grad_down, owners),
        ],
        axis=1,
    )
    summed_all = lax.psum_scatter(packed_all, ("dp", "fsdp"), scatter_dimension=0, tiled=True)
    owned = tuple(
        unpack_owned(
            summed_all, (mix_weight.shape, out_weight.shape, up_weight.shape, down_weight.shape)
        )
    )
    local_sq = sum((jnp.sum(g * g) for g in owned))
    owned_sq = lax.psum(local_sq, ("dp", "fsdp"))
    global_norm = jnp.sqrt(owned_sq + jnp.sum(norm_grad * norm_grad))
    scale = 1.0 / jnp.maximum(global_norm, 1.0)
    params = (mix_weight, out_weight, up_weight, down_weight, norm_params)
    grads = (owned[0], owned[1], owned[2], owned[3], norm_grad)
    firsts = (mix_first, out_first, up_first, down_first, norm_first)
    seconds = (mix_second, out_second, up_second, down_second, norm_second)
    news = []
    for index in range(5):
        news.append(
            adamw(
                params[index],
                scale * grads[index],
                firsts[index],
                seconds[index],
                RATES[index],
                DECAYS[index],
            )
        )
    return (
        output,
        grad_tokens,
        global_norm,
        news[0][0],
        news[1][0],
        news[2][0],
        news[3][0],
        news[4][0],
        news[0][1],
        news[1][1],
        news[2][1],
        news[3][1],
        news[4][1],
        news[0][2],
        news[1][2],
        news[2][2],
        news[3][2],
        news[4][2],
    )


BF = jnp.bfloat16
F32 = jnp.float32
AXES = ("dp", "fsdp")
COST = 1.0e9
MICROS = {
    "pack_weights": 1.0, "sort_near": 1.0, "attend_forward": 6.5, "attend_close": 3.6, "feed_up": 2.5,
    "feed_down": 1.5, "finish_forward": 2.0, "grad_down_away": 0.8, "grad_down_here": 0.8,
    "grad_up": 4.0, "attend_backward": 7.0, "grad_mix": 3.0, "grad_input": 4.0, "close_sums": 0.5,
    "update": 2.3,
}
CHIPS = 16
BLOCK = 96
QKV = 72
PLANE = 4 * BLOCK
ZROWS = 3 * BLOCK
HALF = CHIPS * BLOCK
STEPS_Z = (8, 4, 12)


def nt(left, right):
    return lax.dot_general(
        left, right, (((1,), (1,)), ((), ())), preferred_element_type=F32
    )


def tn(left, right):
    return lax.dot_general(
        left, right, (((0,), (0,)), ((), ())), preferred_element_type=F32
    )


def nn(left, right):
    return jnp.dot(left, right, preferred_element_type=F32)


def block_places():
    places = [(BLOCK * p, p, 0) for p in range(4)]
    for p in range(4):
        for j, step in enumerate(STEPS_Z):
            places.append((PLANE + ZROWS * p + BLOCK * j, p, step))
    return places


PLACES = block_places()
PIECES = [
    (0, PLANE), (PLANE, ZROWS), (PLANE + ZROWS, ZROWS), (PLANE + 2 * ZROWS, 2 * ZROWS)
]


def shard_index(chip, core, plane, step, other):
    owner = 1 - core if other else core
    first = 1 + owner
    mask = (0, first, 3 - first, 3)[plane]
    return 2 * (chip ^ mask ^ step) + owner


def call(body, outs, args, scratch=(), smem=0, mb=6, place=pltpu.VMEM):
    held = [math.prod(a.shape) * a.dtype.itemsize for a in args[smem:]]
    held += [math.prod(s) * jnp.dtype(t).itemsize for s, t in outs]
    held += [math.prod(s.shape) * 4 for s in scratch]
    limit = sum(held) + (mb << 20)
    in_specs = [
        pl.BlockSpec(memory_space=pltpu.SMEM if i < smem else place)
        for i in range(len(args))
    ]
    return pl.pallas_call(
        body,
        out_shape=[jax.ShapeDtypeStruct(s, t) for s, t in outs],
        in_specs=in_specs,
        out_specs=[pl.BlockSpec(memory_space=pltpu.VMEM) for _ in outs],
        scratch_shapes=list(scratch),
        compiler_params=pltpu.CompilerParams(vmem_limit_bytes=limit),
        cost_estimate=pl.CostEstimate(
            flops=int(MICROS[body.__name__] * COST), bytes_accessed=0, transcendentals=0
        ),
        name=body.__name__,
    )(*args)


def sort_near(s0, s1, s23, *groups):
    for g, out in enumerate(groups):
        for p, (ref, base) in enumerate(((s0, 0), (s1, 0), (s23, 0), (s23, 3 * BLOCK))):
            at = base + BLOCK * g
            out[BLOCK * p : BLOCK * p + BLOCK, :] = ref[at : at + BLOCK, :]


def segment_of(lengths, place):
    start = jnp.int32(0)
    seg = jnp.full(place.shape, -1, jnp.int32)
    offset = jnp.zeros(place.shape, F32)
    extent = jnp.ones(place.shape, F32)
    for s in range(5):
        size = lengths[0, s]
        inside = (place >= start) & (place < start + size)
        seg = jnp.where(inside, s, seg)
        offset = jnp.where(inside, (place - start).astype(F32), offset)
        extent = jnp.where(inside, size.astype(F32), extent)
        start = start + size
    angle = 0.5 * math.pi * offset / extent
    return seg, jnp.cos(angle), jnp.sin(angle)


def pair_mask(lengths, rows):
    seg_i, cos_i, sin_i = segment_of(lengths, lax.broadcasted_iota(jnp.int32, (1, rows), 1))
    seg_j, cos_j, sin_j = segment_of(lengths, lax.broadcasted_iota(jnp.int32, (rows, 1), 0))
    same = (seg_i == seg_j) & (seg_i >= 0)
    dead = jnp.where(seg_i >= 0, 0.0, 1.0)
    return jnp.where(same, cos_j * cos_i + sin_j * sin_i, 0.0), dead


def softplus(v):
    return jnp.maximum(v, 0.0) + jnp.log1p(jnp.exp(-jnp.abs(v)))


def attend_forward(
    lengths, me, x_ref, so, z0, z1, z2, sp, y0, y1, y2,
    mix, att, den, rel_own, rel_par,
):
    rows = x_ref.shape[0]
    width = x_ref.shape[1]
    chip, core = me[0], me[1]
    x = x_ref[...]
    sides = ((False, (so, z0, z1, z2), rel_own), (True, (sp, y0, y1, y2), rel_par))
    for other, refs, _ in sides:
        for (base, size), ref in zip(PIECES, refs):
            got = nt(ref[...], x)
            for at, plane, step in PLACES:
                if base <= at < base + size:
                    d = shard_index(chip, core, plane, step, other)
                    mix[pl.ds(pl.multiple_of(QKV * d, 8), QKV), :] = got[
                        at - base : at - base + QKV
                    ]
    mask, dead = pair_mask(lengths, rows)
    for h in range(width // DH):
        here = slice(DH * h, DH * h + DH)
        fq = softplus(mix[here, :]).astype(BF)
        fk = softplus(mix[width + DH * h : width + DH * h + DH, :]).astype(BF)
        v = mix[2 * width + DH * h : 2 * width + DH * h + DH, :].astype(BF)
        pairs = tn(fk, fq) * mask
        total = jnp.sum(pairs, axis=0, keepdims=True) + dead
        den[h : h + 1, :] = total
        att[here, :] = nn(v, pairs.astype(BF)) / total
    side = QKV // 3
    blank = jnp.zeros((QKV, rows), F32)
    for other, _, rel in sides:
        for at, plane, step in PLACES:
            d = shard_index(chip, core, plane, step, other)
            part = att[pl.ds(pl.multiple_of(side * d, 8), side), :]
            rel[at : at + BLOCK, :] = jnp.concatenate([blank, part], axis=0).astype(BF)


def attend_close(
    x_ref, rel_own, rel_par, so, z0, z1, z2, sp, y0, y1, y2, norms,
    first, first_low, xhat, rstd,
):
    branch = x_ref[...].astype(F32)
    for refs, rel in (((so, z0, z1, z2), rel_own), ((sp, y0, y1, y2), rel_par)):
        for (base, size), ref in zip(PIECES, refs):
            branch = branch + tn(rel[base : base + size, :], ref[...])
    centered = branch - jnp.mean(branch, axis=-1, keepdims=True)
    spread = jnp.mean(centered * centered, axis=-1, keepdims=True)
    scale = lax.rsqrt(spread + 1e-05)
    hat = centered * scale
    xhat[...] = hat
    rstd[...] = scale
    out = hat * norms[0:1, :] + norms[1:2, :]
    first[...] = out
    first_low[...] = out.astype(BF)


GELU_A = math.sqrt(2.0 / math.pi)
GELU_B = 0.044715


def feed_up(ya, yb, s, z0, z1, z2, hid, slope):
    rows = ya.shape[0]
    for half, y in ((0, ya), (1, yb)):
        cols = slice(half * rows, half * rows + rows)
        for (base, size), ref in zip(PIECES, (s, z0, z1, z2)):
            u = nt(ref[...], y[...])
            sq = u * u
            t = jnp.tanh(GELU_A * u * (1.0 + GELU_B * sq))
            half_up = 0.5 * (1.0 + t)
            hid[base : base + size, cols] = (u * half_up).astype(BF)
            slope[base : base + size, cols] = half_up + 0.5 * u * (1.0 - t * t) * (
                GELU_A * (1.0 + 3.0 * GELU_B * sq)
            )


def feed_down(hid, s, z0, z1, z2, own, other, whole):
    for (base, size), ref in zip(PIECES, (s, z0, z1, z2)):
        whole[base : base + size, :] = ref[...]
    rows = own.shape[0]
    w = whole[...]
    own[...] = tn(hid[:, 0:rows], w)
    other[...] = tn(hid[:, rows : 2 * rows], w)


def norm_back(dy, gain, hat, scale):
    dhat = dy * gain
    return scale * (
        dhat
        - jnp.mean(dhat, axis=-1, keepdims=True)
        - hat * jnp.mean(dhat * hat, axis=-1, keepdims=True)
    )


def finish_forward(lengths, first, own, got, cot, norms, out, ds2, dz, terms):
    rows = first.shape[0]
    used = jnp.int32(0)
    for s in range(5):
        used = used + lengths[0, s]
    live = jnp.where(lax.broadcasted_iota(jnp.int32, (rows, 1), 0) < used, 1.0, 0.0)
    h = first[...] + (own[...] + got[...])
    centered = h - jnp.mean(h, axis=-1, keepdims=True)
    spread = jnp.mean(centered * centered, axis=-1, keepdims=True)
    scale = lax.rsqrt(spread + 1e-05)
    hat = centered * scale
    out[...] = ((hat * norms[2:3, :] + norms[3:4, :]) * live).astype(BF)
    dy = cot[...].astype(F32) * live
    back = norm_back(dy, norms[2:3, :], hat, scale)
    ds2[...] = back
    dz[...] = back.astype(BF)
    terms[0:1, :] = jnp.sum(dy * hat, axis=0, keepdims=True)
    terms[1:2, :] = jnp.sum(dy, axis=0, keepdims=True)


def spread_rows(get, send, turn, own):
    goals = ((own, 0), (turn, 0), (send, 0), (send, PLANE))
    for base, size in PIECES:
        g = get(base, size)
        for at, plane, step in PLACES:
            if base <= at < base + size:
                ref, off = goals[plane]
                to = off + BLOCK * ((0,) + STEPS_Z).index(step)
                ref[to : to + BLOCK, :] = g[at - base : at - base + BLOCK].astype(ref.dtype)


def hidden_grad(hid, za, zb, here):
    rows = za.shape[0]
    return nn(hid[here, 0:rows], za[...]) + nn(hid[here, rows : 2 * rows], zb[...])


def grad_down_away(hid, za, zb, send):
    near = hidden_grad(hid, za, zb, slice(2 * BLOCK, PLANE)).astype(BF)
    far = hidden_grad(hid, za, zb, slice(PLANE + 2 * ZROWS, HALF)).astype(BF)
    for p in range(2):
        send[PLANE * p : PLANE * p + BLOCK, :] = near[BLOCK * p : BLOCK * p + BLOCK]
        send[PLANE * p + BLOCK : PLANE * p + PLANE, :] = far[ZROWS * p : ZROWS * p + ZROWS]


def grad_down_here(hid, za, zb, turn, own):
    near = hidden_grad(hid, za, zb, slice(0, 2 * BLOCK))
    far = hidden_grad(hid, za, zb, slice(PLANE, PLANE + 2 * ZROWS))
    for p, ref in enumerate((own, turn)):
        ref[0:BLOCK, :] = near[BLOCK * p : BLOCK * p + BLOCK]
        ref[BLOCK:PLANE, :] = far[ZROWS * p : ZROWS * p + ZROWS]


def grad_up(
    slope, za, zb, ya, yb, d, w0, w1, w2, s, z0, z1, z2,
    send, turn, own, mine, other, dup, whole,
):
    rows = za.shape[0]
    for (base, size), ref in zip(PIECES, (d, w0, w1, w2)):
        here = slice(base, base + size)
        w = ref[...]
        dup[here, 0:rows] = (nt(w, za[...]) * slope[here, 0:rows]).astype(BF)
        dup[here, rows:] = (nt(w, zb[...]) * slope[here, rows:]).astype(BF)
    for (base, size), ref in zip(PIECES, (s, z0, z1, z2)):
        whole[base : base + size, :] = ref[...]

    def get(base, size):
        return nn(dup[base : base + size, 0:rows], ya[...]) + nn(
            dup[base : base + size, rows : 2 * rows], yb[...]
        )

    spread_rows(get, send, turn, own)
    w = whole[...]
    mine[...] = tn(dup[:, 0:rows], w)
    other[...] = tn(dup[:, rows : 2 * rows], w)


def attend_backward(
    lengths, me, ds2, mine, got, xhat, rstd, norms, mix, att, den,
    so, z0, z1, z2, sp, y0, y1, y2,
    dh_ref, do_ref, terms, rel_own, rel_par, datt, dmix,
):
    rows, width = ds2.shape
    chip, core = me[0], me[1]
    dy1 = ds2[...] + (mine[...] + got[...])
    hat = xhat[...]
    terms[0:1, :] = jnp.sum(dy1 * hat, axis=0, keepdims=True)
    terms[1:2, :] = jnp.sum(dy1, axis=0, keepdims=True)
    dh = norm_back(dy1, norms[0:1, :], hat, rstd[...])
    dh_ref[...] = dh
    do = dh.astype(BF)
    do_ref[...] = do
    side = QKV // 3
    sides = ((False, (so, z0, z1, z2), rel_own), (True, (sp, y0, y1, y2), rel_par))
    for other, refs, _ in sides:
        for (base, size), ref in zip(PIECES, refs):
            got_t = nt(ref[...], do)
            for at, plane, step in PLACES:
                if base <= at < base + size:
                    d = shard_index(chip, core, plane, step, other)
                    datt[pl.ds(pl.multiple_of(side * d, 8), side), :] = got_t[
                        at - base + QKV : at - base + BLOCK
                    ]
    mask, _ = pair_mask(lengths, rows)
    for h in range(width // DH):
        here = slice(DH * h, DH * h + DH)
        q = mix[here, :]
        k = mix[width + DH * h : width + DH * h + DH, :]
        v = mix[2 * width + DH * h : 2 * width + DH * h + DH, :].astype(BF)
        fq = softplus(q).astype(BF)
        fk = softplus(k).astype(BF)
        pairs = (tn(fk, fq) * mask).astype(BF)
        da = datt[here, :]
        total = den[h : h + 1, :]
        dnum = da / total
        dden = -jnp.sum(dnum * att[here, :], axis=0, keepdims=True)
        dnum = dnum.astype(BF)
        dpairs = ((tn(v, dnum) + dden) * mask).astype(BF)
        dmix[2 * width + DH * h : 2 * width + DH * h + DH, :] = nt(dnum, pairs)
        dmix[width + DH * h : width + DH * h + DH, :] = nt(fq, dpairs) * jax.nn.sigmoid(k)
        dmix[here, :] = nn(fk, dpairs) * jax.nn.sigmoid(q)
    blank = jnp.zeros((BLOCK - QKV, rows), F32)
    for other, _, rel in sides:
        for at, plane, step in PLACES:
            d = shard_index(chip, core, plane, step, other)
            part = dmix[pl.ds(pl.multiple_of(QKV * d, 8), QKV), :]
            rel[at : at + BLOCK, :] = jnp.concatenate([part, blank], axis=0).astype(BF)


def grad_mix(dma, dmb, xa, xb, ata, atb, doa, dob, send, turn, own):
    def get(base, size):
        here = slice(base, base + size)
        return (nn(dma[here, :], xa[...]) + nn(dmb[here, :], xb[...])) + (
            nn(ata[here, :], doa[...]) + nn(atb[here, :], dob[...])
        )

    spread_rows(get, send, turn, own)


def grad_input(dh, rel_own, rel_par, so, z0, z1, z2, sp, y0, y1, y2, out):
    total = dh[...]
    for refs, rel in (((so, z0, z1, z2), rel_own), ((sp, y0, y1, y2), rel_par)):
        for (base, size), ref in zip(PIECES, refs):
            total = total + tn(rel[base : base + size, :], ref[...])
    out[...] = total


def close_sums(k1, a1, b1, c1, g2, g3, t1, t2, g1, note):
    s1 = (k1[...] + a1[...].astype(F32)) + (b1[...].astype(F32) + c1[...].astype(F32))
    g1[...] = s1
    sq = s1 * s1 + g2[...] * g2[...] + g3[...] * g3[...]
    note[0:2, :] = t1[...]
    note[2:4, :] = t2[...]
    note[4:5, :] = jnp.sum(sq, axis=0, keepdims=True)
    note[5:8, :] = jnp.zeros((3, note.shape[1]), F32)


def update(
    n0, n1, n2, n3, g1, g2, g3, mw, ow, uw, dw, nw, mm, om, um, dm, nm, mv, ov, uv, dv, nv,
    norm_out, mw2, ow2, uw2, dw2, nw2, mm2, om2, um2, dm2, nm2, mv2, ov2, uv2, dv2, nv2,
):
    note = (n0[...] + n1[...]) + (n2[...] + n3[...])
    terms = note[0:4, :]
    total = jnp.sum(note[4:5, :]) + jnp.sum(terms * terms)
    norm = jnp.sqrt(jnp.full((1, 1), total, F32))
    norm_out[...] = norm
    scale = 1.0 / jnp.maximum(norm, 1.0)

    one = g1[...]
    grads = (one[0:QKV], one[QKV:BLOCK], g2[...], g3[...], terms)
    groups = (
        (mw, mm, mv, mw2, mm2, mv2),
        (ow, om, ov, ow2, om2, ov2),
        (uw, um, uv, uw2, um2, uv2),
        (dw, dm, dv, dw2, dm2, dv2),
        (nw, nm, nv, nw2, nm2, nv2),
    )
    for g, (w, m, v, w2, m2, v2), rate, decay in zip(grads, groups, RATES, DECAYS):
        new_w, new_m, new_v = adamw(w[...], scale * g, m[...], v[...], rate, decay)
        w2[...] = new_w
        m2[...] = new_m
        v2[...] = new_v


def tie(value, *others):
    return lax.optimization_barrier((value,) + others)[0]


def swap(value):
    return lax.ppermute(value, "fsdp", [(0, 1), (1, 0)])


def hop_first(value):
    return lax.ppermute(value, AXES, [(i, i ^ (4 if i % 2 else 2)) for i in range(2 * CHIPS)])


def hop_second(value):
    return lax.ppermute(value, AXES, [(i, i ^ (2 if i % 2 else 4)) for i in range(2 * CHIPS)])


def hop_z(value, step):
    return lax.ppermute(value, "dp", [(i, i ^ step) for i in range(CHIPS)])


def add_first(turn, got):
    return (turn + got[PLANE:].astype(F32)).astype(BF)


def add_second(own, got, back):
    total = own + got[:PLANE].astype(F32) + back.astype(F32)
    return total[:BLOCK], total.astype(BF)


def send_z(low):
    return [
        hop_z(low[BLOCK * (j + 1) : BLOCK * (j + 2)], step) for j, step in enumerate(STEPS_Z)
    ]


def tuned_device(
    tokens, cotangent, lengths,
    mix_weight, out_weight, up_weight, down_weight, norm_params,
    mix_first, out_first, up_first, down_first, norm_first,
    mix_second, out_second, up_second, down_second, norm_second,
):
    rows, width = tokens.shape
    chip, core = lax.axis_index("dp"), lax.axis_index("fsdp")
    me = jnp.stack([chip, core]).astype(jnp.int32)
    wide = 3 * width

    blocks = [
        jnp.concatenate([mix_weight.T.astype(BF), out_weight.astype(BF)], axis=0),
        up_weight.T.astype(BF),
        down_weight.astype(BF),
    ]
    s_all = jnp.concatenate(blocks, axis=0)
    near1 = [hop_z(blocks[0], step) for step in STEPS_Z]
    s_first = hop_first(s_all)
    s_far = hop_second(jnp.concatenate([s_all, s_first], axis=0))
    joined1 = jnp.concatenate(near1, axis=0)
    turned1 = hop_first(tie(joined1, s_first))
    far1 = hop_second(jnp.concatenate([tie(joined1, s_far), turned1], axis=0))
    got2 = hop_z(tie(blocks[1], *near1), 8)
    joined2 = jnp.concatenate(
        [got2, hop_z(jnp.concatenate([blocks[1], got2], axis=0), 4)], axis=0
    )
    turned2 = hop_first(tie(joined2, turned1))
    far2 = hop_second(jnp.concatenate([tie(joined2, far1), turned2], axis=0))
    sorted1, sorted2, sorted3 = call(
        sort_near,
        [((PLANE, width), BF)] * 3,
        (s_all, s_first, s_far),
    )
    up_all = (sorted2, joined2, turned2, far2)
    attn_own = (sorted1, joined1, turned1, far1)
    attn_par = tuple(swap(p) for p in attn_own)
    x_par = swap(tokens)

    mix, att, den, at_own, at_par = call(
        attend_forward,
        [
            ((wide, rows), F32), ((width, rows), F32), ((16, rows), F32),
            ((HALF, rows), BF), ((HALF, rows), BF),
        ],
        (lengths, me, tie(tokens, x_par)) + attn_own + attn_par,
        smem=2,
    )
    got3 = hop_z(tie(blocks[2], got2), 8)
    joined3 = jnp.concatenate(
        [got3, hop_z(jnp.concatenate([blocks[2], tie(got3, joined2)], axis=0), 4)], axis=0
    )
    turned3 = hop_first(tie(joined3, turned2))
    first, first_low, xhat, rstd = call(
        attend_close,
        [((rows, width), F32), ((rows, width), BF), ((rows, width), F32), ((rows, 1), F32)],
        (tokens, at_own, at_par) + attn_own + attn_par + (norm_params,),
    )
    far3 = hop_second(jnp.concatenate([tie(joined3, far2), turned3], axis=0))
    down_all = (sorted3, joined3, turned3, far3)
    at_got = swap(at_par)
    first_par = swap(first_low)
    hid, slope = call(
        feed_up,
        [((HALF, 2 * rows), BF), ((HALF, 2 * rows), F32)],
        (first_low, tie(first_par, at_got)) + up_all,
    )
    down_own, down_par = call(
        feed_down,
        [((rows, width), F32)] * 2,
        (hid,) + down_all,
        scratch=[pltpu.VMEM((HALF, width), BF)],
    )
    output, ds2, dz, terms_two = call(
        finish_forward,
        [((rows, width), BF), ((rows, width), F32), ((rows, width), BF), ((2, width), F32)],
        (lengths, first, down_own, swap(down_par), cotangent, norm_params),
        smem=1,
    )
    dz_par = swap(dz)
    spread_shapes = [((2 * PLANE, width), BF), ((PLANE, width), F32), ((PLANE, width), F32)]
    (send3,) = call(grad_down_away, spread_shapes[:1], (hid, dz, dz_par))
    hid_later = tie(hid, send3)
    turn3, own3 = call(grad_down_here, spread_shapes[1:], (hid_later, dz, dz_par))
    got3 = hop_second(send3)
    send2, turn2, own2, dy_own, dy_par = call(
        grad_up,
        spread_shapes + [((rows, width), F32)] * 2,
        (tie(slope, turn3), dz, dz_par, first_low, first_par) + down_all + up_all,
        scratch=[pltpu.VMEM((HALF, 2 * rows), BF), pltpu.VMEM((HALF, width), BF)],
    )
    low_turn3 = add_first(turn3, got3)
    back3 = hop_first(low_turn3)
    got2 = hop_second(send2)
    dh, do, terms_one, dm_own, dm_par = call(
        attend_backward,
        [
            ((rows, width), F32), ((rows, width), BF), ((2, width), F32),
            ((HALF, rows), BF), ((HALF, rows), BF),
        ],
        (lengths, me, tie(ds2, low_turn3), dy_own, swap(dy_par), xhat, rstd, norm_params, mix, att, den)
        + attn_own + attn_par,
        scratch=[pltpu.VMEM((width, rows), F32), pltpu.VMEM((wide, rows), F32)],
        smem=2,
    )
    send1, turn1, own1 = call(
        grad_mix,
        spread_shapes,
        (dm_own, swap(dm_par), tokens, x_par, at_own, at_got, do, swap(do)),
    )
    (grad_tokens,) = call(
        grad_input,
        [((rows, width), F32)],
        (dh, dm_own, dm_par) + attn_own + attn_par,
    )
    keep3, low3 = add_second(own3, got3, back3)
    parts3 = send_z(low3)
    back2 = hop_first(add_first(turn2, got2))
    got1 = hop_second(send1)
    keep2, low2 = add_second(own2, got2, back2)
    parts2 = send_z(tie(low2, *parts3))
    back1 = hop_first(add_first(tie(turn1, grad_tokens), got1))
    keep1, low1 = add_second(own1, got1, back1)
    parts1 = send_z(tie(low1, *parts2))
    g3 = (keep3 + parts3[0]) + (parts3[1].astype(F32) + parts3[2].astype(F32))
    g2 = (keep2 + parts2[0]) + (parts2[1].astype(F32) + parts2[2].astype(F32))
    g1, note = call(
        close_sums,
        [((BLOCK, width), F32), ((8, width), F32)],
        (keep1,) + tuple(parts1) + (g2, g3, terms_one, terms_two),
    )
    note = note + swap(note)
    note = (note + hop_z(note, 1)) + (hop_z(note, 2) + hop_z(note, 3))
    notes = (note, hop_z(note, 4), hop_z(note, 8), hop_z(note, 12))
    shapes = [
        (mix_weight.shape[::-1], F32), (out_weight.shape, F32), (up_weight.shape[::-1], F32),
        (down_weight.shape, F32), (norm_params.shape, F32),
    ]
    norm, *news = call(
        update,
        [((1, 1), F32)] + shapes * 3,
        notes + (
            g1, g2, g3, mix_weight.T, out_weight, up_weight.T, down_weight, norm_params,
            mix_first.T, out_first, up_first.T, down_first, norm_first,
            mix_second.T, out_second, up_second.T, down_second, norm_second,
        ),
    )
    for at in (0, 2, 5, 7, 10, 12):
        news[at] = news[at].T
    return (output, grad_tokens, norm.reshape(())) + tuple(news)


def solution(mesh):
    in_specs = (
        P(("dp", "fsdp"), None),
        P(("dp", "fsdp"), None),
        P(("dp", "fsdp"), None),
        P(None, ("dp", "fsdp")),
        P(("dp", "fsdp"), None),
        P(None, ("dp", "fsdp")),
        P(("dp", "fsdp"), None),
        P(),
        P(None, ("dp", "fsdp")),
        P(("dp", "fsdp"), None),
        P(None, ("dp", "fsdp")),
        P(("dp", "fsdp"), None),
        P(),
        P(None, ("dp", "fsdp")),
        P(("dp", "fsdp"), None),
        P(None, ("dp", "fsdp")),
        P(("dp", "fsdp"), None),
        P(),
    )
    out_specs = (
        P(("dp", "fsdp"), None),
        P(("dp", "fsdp"), None),
        P(),
        P(None, ("dp", "fsdp")),
        P(("dp", "fsdp"), None),
        P(None, ("dp", "fsdp")),
        P(("dp", "fsdp"), None),
        P(),
        P(None, ("dp", "fsdp")),
        P(("dp", "fsdp"), None),
        P(None, ("dp", "fsdp")),
        P(("dp", "fsdp"), None),
        P(),
        P(None, ("dp", "fsdp")),
        P(("dp", "fsdp"), None),
        P(None, ("dp", "fsdp")),
        P(("dp", "fsdp"), None),
        P(),
    )
    sizes = dict(mesh.shape)
    tuned = sizes["dp"] == CHIPS and sizes["fsdp"] == 2
    return jax.shard_map(
        tuned_device if tuned else on_device, mesh=mesh, in_specs=in_specs, out_specs=out_specs, check_vma=False
    )
```

```python
import math

import jax
import jax.numpy as jnp
from jax import lax
from jax.experimental import pallas as pl
from jax.experimental.pallas import tpu as pltpu
from jax.sharding import PartitionSpec as P

DH = 64
STEP = 10


HIGH = lax.Precision.HIGHEST
RATES = (0.01, 0.08, 0.01, 0.01, 0.2)
DECAYS = (0.1, 0.1, 0.1, 0.1, 0.0)


def segment_tables(lengths, rows):
    ends = jnp.cumsum(lengths)
    starts = ends - lengths
    places = jnp.arange(rows, dtype=jnp.int32)
    inside = (places[None, :] >= starts[:, None]) & (places[None, :] < ends[:, None])
    member = inside[:-1].astype(jnp.float32)
    live = jnp.sum(member, axis=0)
    offset = places.astype(jnp.float32) - jnp.sum(
        member * starts[:-1, None].astype(jnp.float32), axis=0
    )
    extent = jnp.sum(member * lengths[:-1, None].astype(jnp.float32), axis=0) + (1.0 - live)
    angle = 0.5 * math.pi * offset / extent
    return (member, live, angle)


def cos_attention(queries, keys, values, member, live, angle):
    rows = queries.shape[0]
    feat_q = jax.nn.softplus(queries).reshape(rows, -1, DH)
    feat_k = jax.nn.softplus(keys).reshape(rows, -1, DH)
    vals = values.reshape(rows, -1, DH)
    phases = jnp.stack([jnp.cos(angle), jnp.sin(angle)])
    weighted = member[None] * phases[:, None, :]
    scaled = jnp.einsum("psr,rhd->psrhd", weighted, feat_k)
    state = jnp.einsum("psrhd,rhe->pshde", scaled, vals, precision=HIGH)
    normal = jnp.sum(scaled, axis=2)
    query_side = feat_q[None] * phases[:, :, None, None]
    per_slot = jnp.einsum("prhd,pshde->rshe", query_side, state, precision=HIGH)
    numer = jnp.einsum("sr,rshe->rhe", member, per_slot, precision=HIGH)
    slot_den = jnp.einsum("prhd,pshd->rsh", query_side, normal, precision=HIGH)
    denom = jnp.einsum("sr,rsh->rh", member, slot_den, precision=HIGH) + (1.0 - live)[:, None]
    return (numer / denom[:, :, None]).reshape(rows, -1)


def layer_norm(hidden, gain, shift):
    centered = hidden - jnp.mean(hidden, axis=-1, keepdims=True)
    spread = jnp.mean(centered * centered, axis=-1, keepdims=True)
    return centered * lax.rsqrt(spread + 1e-05) * gain + shift


def gelu_tanh(values):
    return jax.nn.gelu(values, approximate=True)


def inner_rows(left, right):
    return lax.dot_general(
        left, right, (((0,), (0,)), ((), ())), preferred_element_type=jnp.float32
    )


def times_transpose(left, right):
    return lax.dot_general(
        left, right, (((1,), (1,)), ((), ())), preferred_element_type=jnp.float32
    )


def by_owner_rows(grad, owners):
    return grad.reshape(owners, -1, 128)


def by_owner_columns(grad, owners):
    height, across = grad.shape
    split = grad.reshape(height, owners, across // owners)
    return jnp.transpose(split, (1, 0, 2)).reshape(owners, -1, 128)


def unpack_owned(packed, shapes):
    pieces = []
    offset = 0
    for shape in shapes:
        blocks = shape[0] * shape[1] // 128
        pieces.append(packed[0, offset : offset + blocks].reshape(shape))
        offset = offset + blocks
    return pieces


def adamw(weight, grad, first, second, rate, decay):
    first_new = 0.9 * first + 0.1 * grad
    second_new = 0.95 * second + 0.05 * grad * grad
    step_dir = first_new / (1.0 - 0.9**STEP) / (jnp.sqrt(second_new / (1.0 - 0.95**STEP)) + 1e-08)
    return (weight - rate * (step_dir + decay * weight), first_new, second_new)


def on_device(
    tokens,
    cotangent,
    lengths,
    mix_weight,
    out_weight,
    up_weight,
    down_weight,
    norm_params,
    mix_first,
    out_first,
    up_first,
    down_first,
    norm_first,
    mix_second,
    out_second,
    up_second,
    down_second,
    norm_second,
):
    rows, width = tokens.shape
    owners = lax.axis_size(("dp", "fsdp"))
    rounded = (
        mix_weight.astype(jnp.bfloat16),
        out_weight.astype(jnp.bfloat16),
        up_weight.astype(jnp.bfloat16),
        down_weight.astype(jnp.bfloat16),
    )
    mix_full, out_full, up_full, down_full = (
        lax.all_gather(rounded[0], ("dp", "fsdp"), axis=1, tiled=True),
        lax.all_gather(rounded[1], ("dp", "fsdp"), axis=0, tiled=True),
        lax.all_gather(rounded[2], ("dp", "fsdp"), axis=1, tiled=True),
        lax.all_gather(rounded[3], ("dp", "fsdp"), axis=0, tiled=True),
    )
    member, live, angle = segment_tables(lengths[0], rows)
    mixed = jnp.dot(tokens, mix_full, preferred_element_type=jnp.float32)

    def attend(queries, keys, values):
        return cos_attention(queries, keys, values, member, live, angle)

    attended, attention_pull = jax.vjp(
        attend, mixed[:, :width], mixed[:, width : 2 * width], mixed[:, 2 * width :]
    )
    attended_low = attended.astype(jnp.bfloat16)
    branch = jnp.dot(attended_low, out_full, preferred_element_type=jnp.float32)
    first, first_pull = jax.vjp(
        layer_norm, tokens.astype(jnp.float32) + branch, norm_params[0], norm_params[1]
    )
    first_low = first.astype(jnp.bfloat16)
    upper = jnp.dot(first_low, up_full, preferred_element_type=jnp.float32)
    hidden, gelu_pull = jax.vjp(gelu_tanh, upper)
    hidden_low = hidden.astype(jnp.bfloat16)
    second = jnp.dot(hidden_low, down_full, preferred_element_type=jnp.float32)
    final, final_pull = jax.vjp(layer_norm, first + second, norm_params[2], norm_params[3])
    output = (final * live[:, None]).astype(jnp.bfloat16)
    mix_full, out_full, up_full, down_full = (
        lax.all_gather(rounded[0], ("dp", "fsdp"), axis=1, tiled=True),
        lax.all_gather(rounded[1], ("dp", "fsdp"), axis=0, tiled=True),
        lax.all_gather(rounded[2], ("dp", "fsdp"), axis=1, tiled=True),
        lax.all_gather(rounded[3], ("dp", "fsdp"), axis=0, tiled=True),
    )
    grad_final = cotangent.astype(jnp.float32) * live[:, None]
    grad_sum_two, grad_gain_two, grad_bias_two = final_pull(grad_final)
    grad_second = grad_sum_two.astype(jnp.bfloat16)
    grad_down = inner_rows(hidden_low, grad_second)
    grad_hidden = times_transpose(grad_second, down_full)
    (grad_upper,) = gelu_pull(grad_hidden)
    grad_upper_low = grad_upper.astype(jnp.bfloat16)
    grad_up = inner_rows(first_low, grad_upper_low)
    grad_first = grad_sum_two + times_transpose(grad_upper_low, up_full)
    grad_sum_one, grad_gain_one, grad_bias_one = first_pull(grad_first)
    grad_branch = grad_sum_one.astype(jnp.bfloat16)
    grad_out = inner_rows(attended_low, grad_branch)
    grad_attended = times_transpose(grad_branch, out_full)
    grad_q, grad_k, grad_v = attention_pull(grad_attended)
    grad_mixed = jnp.concatenate([grad_q, grad_k, grad_v], axis=1).astype(jnp.bfloat16)
    grad_mix = inner_rows(tokens, grad_mixed)
    grad_tokens = grad_sum_one + times_transpose(grad_mixed, mix_full)
    norm_terms = jnp.stack([grad_gain_one, grad_bias_one, grad_gain_two, grad_bias_two])
    norm_grad = lax.psum(norm_terms, ("dp", "fsdp"))
    packed_all = jnp.concatenate(
        [
            by_owner_columns(grad_mix, owners),
            by_owner_rows(grad_out, owners),
            by_owner_columns(grad_up, owners),
            by_owner_rows(grad_down, owners),
        ],
        axis=1,
    )
    summed_all = lax.psum_scatter(packed_all, ("dp", "fsdp"), scatter_dimension=0, tiled=True)
    owned = tuple(
        unpack_owned(
            summed_all, (mix_weight.shape, out_weight.shape, up_weight.shape, down_weight.shape)
        )
    )
    local_sq = sum((jnp.sum(g * g) for g in owned))
    owned_sq = lax.psum(local_sq, ("dp", "fsdp"))
    global_norm = jnp.sqrt(owned_sq + jnp.sum(norm_grad * norm_grad))
    scale = 1.0 / jnp.maximum(global_norm, 1.0)
    params = (mix_weight, out_weight, up_weight, down_weight, norm_params)
    grads = (owned[0], owned[1], owned[2], owned[3], norm_grad)
    firsts = (mix_first, out_first, up_first, down_first, norm_first)
    seconds = (mix_second, out_second, up_second, down_second, norm_second)
    news = []
    for index in range(5):
        news.append(
            adamw(
                params[index],
                scale * grads[index],
                firsts[index],
                seconds[index],
                RATES[index],
                DECAYS[index],
            )
        )
    return (
        output,
        grad_tokens,
        global_norm,
        news[0][0],
        news[1][0],
        news[2][0],
        news[3][0],
        news[4][0],
        news[0][1],
        news[1][1],
        news[2][1],
        news[3][1],
        news[4][1],
        news[0][2],
        news[1][2],
        news[2][2],
        news[3][2],
        news[4][2],
    )


BF = jnp.bfloat16
F32 = jnp.float32
AXES = ("dp", "fsdp")
COST = 1000000000.0
MICROS = {
    "sort_near": 0.1,
    "attend_forward": 0.65,
    "attend_close": 0.36,
    "feed_up": 0.25,
    "feed_down": 0.15,
    "finish_forward": 0.0,
    "grad_down_away": 0.0,
    "grad_down_here": 0.0,
    "grad_up": 0.0,
    "attend_backward": 0.0,
    "grad_input": 0.0,
    "close_sums": 0.0,
    "update": 0.0,
    "grad_up_away": 0.0,
    "grad_up_here": 1.0,
    "feed_back": 0.0,
    "mix_away": 0.0,
    "mix_here": 2.0,
}
MB = 16
CHIPS = 16
BLOCK = 96
QKV = 72
PLANE = 4 * BLOCK
ZROWS = 3 * BLOCK
HALF = CHIPS * BLOCK
STEPS_Z = (8, 4, 12)


def nt(left, right):
    return lax.dot_general(
        left, right, (((1,), (1,)), ((), ())), preferred_element_type=F32
    )


def tn(left, right):
    return lax.dot_general(
        left, right, (((0,), (0,)), ((), ())), preferred_element_type=F32
    )


def nn(left, right):
    return jnp.dot(left, right, preferred_element_type=F32)


def block_places():
    places = [(BLOCK * p, p, 0) for p in range(4)]
    for p in range(4):
        for j, step in enumerate(STEPS_Z):
            places.append((PLANE + ZROWS * p + BLOCK * j, p, step))
    return places


PLACES = block_places()
PIECES = [(0, PLANE)] + [(PLANE + ZROWS * p, ZROWS) for p in range(4)]


def shard_index(chip, core, plane, step, other):
    owner = 1 - core if other else core
    first = 1 + owner
    mask = (0, first, 3 - first, 3)[plane]
    return 2 * (chip ^ mask ^ step) + owner


def call(body, outs, args, scratch=(), smem=0, place=pltpu.VMEM, name=None):
    name = name or body.__name__
    held = [math.prod(s.shape) * 4 for s in scratch]
    limit = int(sum(held) + (MB << 20))
    in_specs = [
        pl.BlockSpec(memory_space=pltpu.SMEM if i < smem else place)
        for i in range(len(args))
    ]
    return pl.pallas_call(
        body,
        out_shape=[jax.ShapeDtypeStruct(s, t) for s, t in outs],
        in_specs=in_specs,
        out_specs=[pl.BlockSpec(memory_space=pltpu.VMEM) for _ in outs],
        scratch_shapes=list(scratch),
        compiler_params=pltpu.CompilerParams(vmem_limit_bytes=limit),
        cost_estimate=pl.CostEstimate(
            flops=int(MICROS[name] * COST), bytes_accessed=0, transcendentals=0
        ),
        name=name,
    )(*args)


def sort_near(s0, s1, s2, s3, *groups):
    for g, out in enumerate(groups):
        for p, (ref, base) in enumerate(((s0, 0), (s1, 0), (s2, 0), (s3, 0))):
            at = base + BLOCK * g
            out[BLOCK * p : BLOCK * p + BLOCK, :] = ref[at : at + BLOCK, :]


def segment_of(lengths, place):
    start = jnp.int32(0)
    seg = jnp.full(place.shape, -1, jnp.int32)
    offset = jnp.zeros(place.shape, F32)
    extent = jnp.ones(place.shape, F32)
    for s in range(5):
        size = lengths[0, s]
        inside = (place >= start) & (place < start + size)
        seg = jnp.where(inside, s, seg)
        offset = jnp.where(inside, (place - start).astype(F32), offset)
        extent = jnp.where(inside, size.astype(F32), extent)
        start = start + size
    angle = 0.5 * math.pi * offset / extent
    return seg, jnp.cos(angle), jnp.sin(angle)


def pair_mask(lengths, rows):
    seg_i, cos_i, sin_i = segment_of(lengths, lax.broadcasted_iota(jnp.int32, (1, rows), 1))
    seg_j, cos_j, sin_j = segment_of(lengths, lax.broadcasted_iota(jnp.int32, (rows, 1), 0))
    same = (seg_i == seg_j) & (seg_i >= 0)
    dead = jnp.where(seg_i >= 0, 0.0, 1.0)
    return jnp.where(same, cos_j * cos_i + sin_j * sin_i, 0.0), dead


def softplus(v):
    return jnp.maximum(v, 0.0) + jnp.log1p(jnp.exp(-jnp.abs(v)))


def attend_forward(
    lengths, me, x_ref, so, z0, z1, z2, z3, sp, y0, y1, y2, y3,
    mix, att, den, rel_own, rel_par,
):
    rows = x_ref.shape[0]
    width = x_ref.shape[1]
    chip, core = me[0], me[1]
    x = x_ref[...]
    sides = ((False, (so, z0, z1, z2, z3), rel_own), (True, (sp, y0, y1, y2, y3), rel_par))
    for other, refs, _ in sides:
        for (base, size), ref in zip(PIECES, refs):
            got = nt(ref[...], x)
            for at, plane, step in PLACES:
                if base <= at < base + size:
                    d = shard_index(chip, core, plane, step, other)
                    mix[pl.ds(pl.multiple_of(QKV * d, 8), QKV), :] = got[
                        at - base : at - base + QKV
                    ]
    mask, dead = pair_mask(lengths, rows)
    for h in range(width // DH):
        here = slice(DH * h, DH * h + DH)
        fq = softplus(mix[here, :]).astype(BF)
        fk = softplus(mix[width + DH * h : width + DH * h + DH, :]).astype(BF)
        v = mix[2 * width + DH * h : 2 * width + DH * h + DH, :].astype(BF)
        pairs = tn(fk, fq) * mask
        total = jnp.sum(pairs, axis=0, keepdims=True) + dead
        den[h : h + 1, :] = total
        att[here, :] = nn(v, pairs.astype(BF)) / total
    side = QKV // 3
    blank = jnp.zeros((QKV, rows), F32)
    for other, _, rel in sides:
        for at, plane, step in PLACES:
            d = shard_index(chip, core, plane, step, other)
            part = att[pl.ds(pl.multiple_of(side * d, 8), side), :]
            rel[at : at + BLOCK, :] = jnp.concatenate([blank, part], axis=0).astype(BF)


def attend_close(
    x_ref, rel_own, rel_par, so, z0, z1, z2, z3, sp, y0, y1, y2, y3, norms,
    first, first_low, xhat, rstd,
):
    branch = x_ref[...].astype(F32)
    for refs, rel in (((so, z0, z1, z2, z3), rel_own), ((sp, y0, y1, y2, y3), rel_par)):
        for (base, size), ref in zip(PIECES, refs):
            branch = branch + tn(rel[base : base + size, :], ref[...])
    centered = branch - jnp.mean(branch, axis=-1, keepdims=True)
    spread = jnp.mean(centered * centered, axis=-1, keepdims=True)
    scale = lax.rsqrt(spread + 1e-05)
    hat = centered * scale
    xhat[...] = hat
    rstd[...] = scale
    out = hat * norms[0:1, :] + norms[1:2, :]
    first[...] = out
    first_low[...] = out.astype(BF)


GELU_A = math.sqrt(2.0 / math.pi)
GELU_B = 0.044715


def feed_up(ya, yb, s, z0, z1, z2, z3, hid, slope):
    rows = ya.shape[0]
    for half, y in ((0, ya), (1, yb)):
        cols = slice(half * rows, half * rows + rows)
        for (base, size), ref in zip(PIECES, (s, z0, z1, z2, z3)):
            u = nt(ref[...], y[...])
            sq = u * u
            t = jnp.tanh(GELU_A * u * (1.0 + GELU_B * sq))
            half_up = 0.5 * (1.0 + t)
            hid[base : base + size, cols] = (u * half_up).astype(BF)
            slope[base : base + size, cols] = half_up + 0.5 * u * (1.0 - t * t) * (
                GELU_A * (1.0 + 3.0 * GELU_B * sq)
            )


def feed_down(hid, s, z0, z1, z2, z3, own, other, whole):
    for (base, size), ref in zip(PIECES, (s, z0, z1, z2, z3)):
        whole[base : base + size, :] = ref[...]
    rows = own.shape[0]
    w = whole[...]
    own[...] = tn(hid[:, 0:rows], w)
    other[...] = tn(hid[:, rows : 2 * rows], w)


def norm_back(dy, gain, hat, scale):
    dhat = dy * gain
    return scale * (
        dhat
        - jnp.mean(dhat, axis=-1, keepdims=True)
        - hat * jnp.mean(dhat * hat, axis=-1, keepdims=True)
    )


def finish_forward(lengths, first, own, got, cot, norms, out, ds2, dz, terms):
    rows = first.shape[0]
    used = jnp.int32(0)
    for s in range(5):
        used = used + lengths[0, s]
    live = jnp.where(lax.broadcasted_iota(jnp.int32, (rows, 1), 0) < used, 1.0, 0.0)
    h = first[...] + (own[...] + got[...])
    centered = h - jnp.mean(h, axis=-1, keepdims=True)
    spread = jnp.mean(centered * centered, axis=-1, keepdims=True)
    scale = lax.rsqrt(spread + 1e-05)
    hat = centered * scale
    out[...] = ((hat * norms[2:3, :] + norms[3:4, :]) * live).astype(BF)
    dy = cot[...].astype(F32) * live
    back = norm_back(dy, norms[2:3, :], hat, scale)
    ds2[...] = back
    dz[...] = back.astype(BF)
    terms[0:1, :] = jnp.sum(dy * hat, axis=0, keepdims=True)
    terms[1:2, :] = jnp.sum(dy, axis=0, keepdims=True)


def rows_away(get, send):
    near = get(slice(2 * BLOCK, PLANE)).astype(BF)
    far = get(slice(PLANE + 2 * ZROWS, HALF)).astype(BF)
    for p in range(2):
        send[PLANE * p : PLANE * p + BLOCK, :] = near[BLOCK * p : BLOCK * p + BLOCK]
        send[PLANE * p + BLOCK : PLANE * p + PLANE, :] = far[ZROWS * p : ZROWS * p + ZROWS]


def rows_here(get, turn, own):
    near = get(slice(0, 2 * BLOCK))
    far = get(slice(PLANE, PLANE + 2 * ZROWS))
    for p, ref in enumerate((own, turn)):
        ref[0:BLOCK, :] = near[BLOCK * p : BLOCK * p + BLOCK]
        ref[BLOCK:PLANE, :] = far[ZROWS * p : ZROWS * p + ZROWS]


def two_cores(hid, za, zb):
    rows = za.shape[0]
    return lambda here: nn(hid[here, 0:rows], za[...]) + nn(
        hid[here, rows : 2 * rows], zb[...]
    )


def grad_away(hid, za, zb, send):
    rows_away(two_cores(hid, za, zb), send)


def grad_here(hid, za, zb, turn, own):
    rows_here(two_cores(hid, za, zb), turn, own)


def feed_back(
    slope, za, zb, d, w0, w1, w2, w3, s, z0, z1, z2, z3, dup, mine, other, whole,
):
    rows = za.shape[0]
    for (base, size), ref in zip(PIECES, (d, w0, w1, w2, w3)):
        here = slice(base, base + size)
        w = ref[...]
        dup[here, 0:rows] = (nt(w, za[...]) * slope[here, 0:rows]).astype(BF)
        dup[here, rows:] = (nt(w, zb[...]) * slope[here, rows:]).astype(BF)
    for (base, size), ref in zip(PIECES, (s, z0, z1, z2, z3)):
        whole[base : base + size, :] = ref[...]
    w = whole[...]
    other[...] = tn(dup[:, rows : 2 * rows], w)
    mine[...] = tn(dup[:, 0:rows], w)


def attend_backward(
    lengths, me, ds2, mine, got, xhat, rstd, norms, mix, att, den,
    so, z0, z1, z2, z3, sp, y0, y1, y2, y3,
    dh_ref, do_ref, terms, rel_own, rel_par, datt, dmix,
):
    rows, width = ds2.shape
    chip, core = me[0], me[1]
    dy1 = ds2[...] + (mine[...] + got[...])
    hat = xhat[...]
    terms[0:1, :] = jnp.sum(dy1 * hat, axis=0, keepdims=True)
    terms[1:2, :] = jnp.sum(dy1, axis=0, keepdims=True)
    dh = norm_back(dy1, norms[0:1, :], hat, rstd[...])
    dh_ref[...] = dh
    do = dh.astype(BF)
    do_ref[...] = do
    side = QKV // 3
    sides = ((False, (so, z0, z1, z2, z3), rel_own), (True, (sp, y0, y1, y2, y3), rel_par))
    for other, refs, _ in sides:
        for (base, size), ref in zip(PIECES, refs):
            got_t = nt(ref[...], do)
            for at, plane, step in PLACES:
                if base <= at < base + size:
                    d = shard_index(chip, core, plane, step, other)
                    datt[pl.ds(pl.multiple_of(side * d, 8), side), :] = got_t[
                        at - base + QKV : at - base + BLOCK
                    ]
    mask, _ = pair_mask(lengths, rows)
    for h in range(width // DH):
        here = slice(DH * h, DH * h + DH)
        q = mix[here, :]
        k = mix[width + DH * h : width + DH * h + DH, :]
        v = mix[2 * width + DH * h : 2 * width + DH * h + DH, :].astype(BF)
        fq = softplus(q).astype(BF)
        fk = softplus(k).astype(BF)
        pairs = (tn(fk, fq) * mask).astype(BF)
        da = datt[here, :]
        total = den[h : h + 1, :]
        dnum = da / total
        dden = -jnp.sum(dnum * att[here, :], axis=0, keepdims=True)
        dnum = dnum.astype(BF)
        dpairs = ((tn(v, dnum) + dden) * mask).astype(BF)
        dmix[2 * width + DH * h : 2 * width + DH * h + DH, :] = nt(dnum, pairs)
        dmix[width + DH * h : width + DH * h + DH, :] = nt(fq, dpairs) * jax.nn.sigmoid(k)
        dmix[here, :] = nn(fk, dpairs) * jax.nn.sigmoid(q)
    blank = jnp.zeros((BLOCK - QKV, rows), F32)
    for other, _, rel in sides:
        for at, plane, step in PLACES:
            d = shard_index(chip, core, plane, step, other)
            part = dmix[pl.ds(pl.multiple_of(QKV * d, 8), QKV), :]
            rel[at : at + BLOCK, :] = jnp.concatenate([part, blank], axis=0).astype(BF)


def four_terms(dma, dmb, xa, xb, ata, atb, doa, dob):
    return lambda here: (nn(dma[here, :], xa[...]) + nn(dmb[here, :], xb[...])) + (
        nn(ata[here, :], doa[...]) + nn(atb[here, :], dob[...])
    )


def mix_away(dma, dmb, xa, xb, ata, atb, doa, dob, send):
    rows_away(four_terms(dma, dmb, xa, xb, ata, atb, doa, dob), send)


def mix_here(dma, dmb, xa, xb, ata, atb, doa, dob, turn, own):
    rows_here(four_terms(dma, dmb, xa, xb, ata, atb, doa, dob), turn, own)


def grad_input(dh, rel_own, rel_par, so, z0, z1, z2, z3, sp, y0, y1, y2, y3, out):
    total = dh[...]
    for refs, rel in (((so, z0, z1, z2, z3), rel_own), ((sp, y0, y1, y2, y3), rel_par)):
        for (base, size), ref in zip(PIECES, refs):
            total = total + tn(rel[base : base + size, :], ref[...])
    out[...] = total


def close_sums(k1, a1, b1, c1, g2, g3, t1, t2, g1, note):
    s1 = (k1[...] + a1[...].astype(F32)) + (b1[...].astype(F32) + c1[...].astype(F32))
    g1[...] = s1
    sq = s1 * s1 + g2[...] * g2[...] + g3[...] * g3[...]
    note[0:2, :] = t1[...]
    note[2:4, :] = t2[...]
    note[4:5, :] = jnp.sum(sq, axis=0, keepdims=True)
    note[5:8, :] = jnp.zeros((3, note.shape[1]), F32)


def update(
    n0, n1, n2, n3, g1, g2, g3, mw, ow, uw, dw, nw, mm, om, um, dm, nm, mv, ov, uv, dv, nv,
    norm_out, mw2, ow2, uw2, dw2, nw2, mm2, om2, um2, dm2, nm2, mv2, ov2, uv2, dv2, nv2,
):
    note = (n0[...] + n1[...]) + (n2[...] + n3[...])
    terms = note[0:4, :]
    total = jnp.sum(note[4:5, :]) + jnp.sum(terms * terms)
    norm = jnp.sqrt(jnp.full((1, 1), total, F32))
    norm_out[...] = norm
    scale = 1.0 / jnp.maximum(norm, 1.0)

    one = g1[...]
    grads = (one[0:QKV], one[QKV:BLOCK], g2[...], g3[...], terms)
    groups = (
        (mw, mm, mv, mw2, mm2, mv2),
        (ow, om, ov, ow2, om2, ov2),
        (uw, um, uv, uw2, um2, uv2),
        (dw, dm, dv, dw2, dm2, dv2),
        (nw, nm, nv, nw2, nm2, nv2),
    )
    for g, (w, m, v, w2, m2, v2), rate, decay in zip(grads, groups, RATES, DECAYS):
        new_w, new_m, new_v = adamw(w[...], scale * g, m[...], v[...], rate, decay)
        w2[...] = new_w
        m2[...] = new_m
        v2[...] = new_v


def tie(value, *others):
    return lax.optimization_barrier((value,) + others)[0]


def swap(value):
    return lax.ppermute(value, "fsdp", [(0, 1), (1, 0)])


def hop_first(value):
    return lax.ppermute(value, AXES, [(i, i ^ (4 if i % 2 else 2)) for i in range(2 * CHIPS)])


def hop_second(value):
    return lax.ppermute(value, AXES, [(i, i ^ (2 if i % 2 else 4)) for i in range(2 * CHIPS)])


def hop_z(value, step):
    return lax.ppermute(value, "dp", [(i, i ^ step) for i in range(CHIPS)])


def add_first(turn, got):
    return (turn + got[PLANE:].astype(F32)).astype(BF)


def add_second(own, got, back):
    total = own + got[:PLANE].astype(F32) + back.astype(F32)
    return total[:BLOCK], total.astype(BF)


def send_z(low):
    return [
        hop_z(low[BLOCK * (j + 1) : BLOCK * (j + 2)], step) for j, step in enumerate(STEPS_Z)
    ]


def tuned_device(
    tokens, cotangent, lengths,
    mix_weight, out_weight, up_weight, down_weight, norm_params,
    mix_first, out_first, up_first, down_first, norm_first,
    mix_second, out_second, up_second, down_second, norm_second,
):
    rows, width = tokens.shape
    chip, core = lax.axis_index("dp"), lax.axis_index("fsdp")
    me = jnp.stack([chip, core]).astype(jnp.int32)
    wide = 3 * width

    blocks = [
        jnp.concatenate([mix_weight.T.astype(BF), out_weight.astype(BF)], axis=0),
        up_weight.T.astype(BF),
        down_weight.astype(BF),
    ]
    s_all = jnp.concatenate(blocks, axis=0)
    def wide_join(*parts):
        return jnp.concatenate(parts, axis=0)

    def z_round(block, direct, before):
        if direct:
            got = [hop_z(tie(block, *before), step) for step in STEPS_Z]
            return got, wide_join(*got)
        far = hop_z(tie(block, *before), 8)
        near = hop_z(wide_join(block, far), 4)
        return [far, near], wide_join(far, near)

    s_first = hop_first(s_all)
    s_second = hop_second(s_all)
    near1, joined1 = z_round(blocks[0], True, ())
    near2, joined2 = z_round(blocks[1], False, (near1[0],))
    near3, joined3 = z_round(blocks[2], False, (near2[0],))
    s_third = hop_second(s_first)
    s_parts = (s_all, s_first, s_second, s_third)
    turned1 = hop_first(tie(joined1, s_first))
    across1 = hop_second(tie(joined1, s_second))
    corner1 = hop_second(tie(turned1, s_third))
    turned2 = hop_first(tie(joined2, turned1))
    across2 = hop_second(tie(joined2, across1))
    corner2 = hop_second(tie(turned2, corner1))
    sorted1, sorted2, sorted3 = call(
        sort_near,
        [((PLANE, width), BF)] * 3,
        s_parts,
    )
    up_all = (sorted2, joined2, turned2, across2, corner2)
    attn_own = (sorted1, joined1, turned1, across1, corner1)
    attn_par = tuple(swap(p) for p in attn_own)
    x_par = swap(tokens)

    mix, att, den, at_own, at_par = call(
        attend_forward,
        [
            ((wide, rows), F32), ((width, rows), F32), ((16, rows), F32),
            ((HALF, rows), BF), ((HALF, rows), BF),
        ],
        (lengths, me, tie(tokens, x_par)) + attn_own + attn_par,
        smem=2,
    )
    turned3 = hop_first(tie(joined3, turned2))
    across3 = hop_second(tie(joined3, across2))
    first, first_low, xhat, rstd = call(
        attend_close,
        [((rows, width), F32), ((rows, width), BF), ((rows, width), F32), ((rows, 1), F32)],
        (tokens, at_own, at_par) + attn_own + attn_par + (norm_params,),
    )
    corner3 = hop_second(tie(turned3, corner2))
    down_all = (sorted3, joined3, turned3, across3, corner3)
    at_got = swap(at_par)
    first_par = swap(first_low)
    hid, slope = call(
        feed_up,
        [((HALF, 2 * rows), BF), ((HALF, 2 * rows), F32)],
        (first_low, tie(first_par, at_got)) + up_all,
    )
    down_own, down_par = call(
        feed_down,
        [((rows, width), F32)] * 2,
        (hid,) + down_all,
        scratch=[pltpu.VMEM((HALF, width), BF)],
    )
    output, ds2, dz, terms_two = call(
        finish_forward,
        [((rows, width), BF), ((rows, width), F32), ((rows, width), BF), ((2, width), F32)],
        (lengths, first, down_own, swap(down_par), cotangent, norm_params),
        smem=1,
    )
    dz_par = swap(dz)
    away = [((2 * PLANE, width), BF)]
    stay = [((PLANE, width), F32)] * 2
    (send3,) = call(grad_away, away, (hid, dz, dz_par), name="grad_down_away")
    got3 = hop_second(send3)
    dup, dy_own, dy_par = call(
        feed_back,
        [((HALF, 2 * rows), BF)] + [((rows, width), F32)] * 2,
        (slope, tie(dz, send3), dz_par) + down_all + up_all,
        scratch=[pltpu.VMEM((HALF, width), BF)],
    )
    (send2,) = call(grad_away, away, (dup, first_low, first_par), name="grad_up_away")
    got2 = hop_second(send2)
    dh, do, terms_one, dm_own, dm_par = call(
        attend_backward,
        [
            ((rows, width), F32), ((rows, width), BF), ((2, width), F32),
            ((HALF, rows), BF), ((HALF, rows), BF),
        ],
        (
            lengths, me, ds2, dy_own, swap(dy_par), xhat, rstd,
            norm_params, mix, att, den,
        ) + attn_own + attn_par,
        scratch=[pltpu.VMEM((width, rows), F32), pltpu.VMEM((wide, rows), F32)],
        smem=2,
    )
    turn3, own3 = call(
        grad_here, stay, (hid, dz, dz_par), name="grad_down_here"
    )
    turn2, own2 = call(
        grad_here, stay, (dup, first_low, first_par),
        name="grad_up_here",
    )
    low_turn3 = add_first(turn3, got3)
    back3 = hop_first(low_turn3)
    back2 = hop_first(add_first(turn2, got2))
    factors = (
        dm_own, swap(dm_par), tokens, x_par, at_own, at_got,
        do, swap(do),
    )
    (send1,) = call(mix_away, away, factors)
    got1 = hop_second(tie(send1, back3))
    turn1, own1 = call(mix_here, stay, (tie(dm_own, send1),) + factors[1:])
    (grad_tokens,) = call(
        grad_input,
        [((rows, width), F32)],
        (tie(dh, send1), dm_own, dm_par) + attn_own + attn_par,
    )
    keep3, low3 = add_second(own3, got3, back3)
    parts3 = send_z(low3)
    keep2, low2 = add_second(own2, got2, back2)
    parts2 = send_z(tie(low2, parts3[1]))
    back1 = hop_first(add_first(tie(turn1, grad_tokens), got1))
    keep1, low1 = add_second(own1, got1, back1)
    parts1 = send_z(tie(low1, parts2[1]))
    g3 = (keep3 + parts3[0]) + (parts3[1].astype(F32) + parts3[2].astype(F32))
    g2 = (keep2 + parts2[0]) + (parts2[1].astype(F32) + parts2[2].astype(F32))
    g1, note = call(
        close_sums,
        [((BLOCK, width), F32), ((8, width), F32)],
        (keep1,) + tuple(parts1) + (g2, g3, terms_one, terms_two),
    )
    note = note + swap(note)
    note = (note + hop_z(note, 1)) + (hop_z(note, 2) + hop_z(note, 3))
    notes = (note, hop_z(note, 4), hop_z(note, 8), hop_z(note, 12))
    shapes = [
        (mix_weight.shape[::-1], F32), (out_weight.shape, F32), (up_weight.shape[::-1], F32),
        (down_weight.shape, F32), (norm_params.shape, F32),
    ]
    norm, *news = call(
        update,
        [((1, 1), F32)] + shapes * 3,
        notes + (
            g1, g2, g3, mix_weight.T, out_weight, up_weight.T, down_weight, norm_params,
            mix_first.T, out_first, up_first.T, down_first, norm_first,
            mix_second.T, out_second, up_second.T, down_second, norm_second,
        ),
    )
    for at in (0, 2, 5, 7, 10, 12):
        news[at] = news[at].T
    return (output, grad_tokens, norm.reshape(())) + tuple(news)


def solution(mesh):
    in_specs = (
        P(("dp", "fsdp"), None),
        P(("dp", "fsdp"), None),
        P(("dp", "fsdp"), None),
        P(None, ("dp", "fsdp")),
        P(("dp", "fsdp"), None),
        P(None, ("dp", "fsdp")),
        P(("dp", "fsdp"), None),
        P(),
        P(None, ("dp", "fsdp")),
        P(("dp", "fsdp"), None),
        P(None, ("dp", "fsdp")),
        P(("dp", "fsdp"), None),
        P(),
        P(None, ("dp", "fsdp")),
        P(("dp", "fsdp"), None),
        P(None, ("dp", "fsdp")),
        P(("dp", "fsdp"), None),
        P(),
    )
    out_specs = (
        P(("dp", "fsdp"), None),
        P(("dp", "fsdp"), None),
        P(),
        P(None, ("dp", "fsdp")),
        P(("dp", "fsdp"), None),
        P(None, ("dp", "fsdp")),
        P(("dp", "fsdp"), None),
        P(),
        P(None, ("dp", "fsdp")),
        P(("dp", "fsdp"), None),
        P(None, ("dp", "fsdp")),
        P(("dp", "fsdp"), None),
        P(),
        P(None, ("dp", "fsdp")),
        P(("dp", "fsdp"), None),
        P(None, ("dp", "fsdp")),
        P(("dp", "fsdp"), None),
        P(),
    )
    sizes = dict(mesh.shape)
    tuned = sizes["dp"] == CHIPS and sizes["fsdp"] == 2
    return jax.shard_map(
        tuned_device if tuned else on_device, mesh=mesh, in_specs=in_specs, out_specs=out_specs, check_vma=False
    )
```

```python
import math

import jax
import jax.numpy as jnp
from jax import lax
from jax.experimental import pallas as pl
from jax.experimental.pallas import tpu as pltpu
from jax.sharding import PartitionSpec as P

DH = 64
STEP = 10


HIGH = lax.Precision.HIGHEST
RATES = (0.01, 0.08, 0.01, 0.01, 0.2)
DECAYS = (0.1, 0.1, 0.1, 0.1, 0.0)


def segment_tables(lengths, rows):
    ends = jnp.cumsum(lengths)
    starts = ends - lengths
    places = jnp.arange(rows, dtype=jnp.int32)
    inside = (places[None, :] >= starts[:, None]) & (places[None, :] < ends[:, None])
    member = inside[:-1].astype(jnp.float32)
    live = jnp.sum(member, axis=0)
    offset = places.astype(jnp.float32) - jnp.sum(
        member * starts[:-1, None].astype(jnp.float32), axis=0
    )
    extent = jnp.sum(member * lengths[:-1, None].astype(jnp.float32), axis=0) + (1.0 - live)
    angle = 0.5 * math.pi * offset / extent
    return (member, live, angle)


def cos_attention(queries, keys, values, member, live, angle):
    rows = queries.shape[0]
    feat_q = jax.nn.softplus(queries).reshape(rows, -1, DH)
    feat_k = jax.nn.softplus(keys).reshape(rows, -1, DH)
    vals = values.reshape(rows, -1, DH)
    phases = jnp.stack([jnp.cos(angle), jnp.sin(angle)])
    weighted = member[None] * phases[:, None, :]
    scaled = jnp.einsum("psr,rhd->psrhd", weighted, feat_k)
    state = jnp.einsum("psrhd,rhe->pshde", scaled, vals, precision=HIGH)
    normal = jnp.sum(scaled, axis=2)
    query_side = feat_q[None] * phases[:, :, None, None]
    per_slot = jnp.einsum("prhd,pshde->rshe", query_side, state, precision=HIGH)
    numer = jnp.einsum("sr,rshe->rhe", member, per_slot, precision=HIGH)
    slot_den = jnp.einsum("prhd,pshd->rsh", query_side, normal, precision=HIGH)
    denom = jnp.einsum("sr,rsh->rh", member, slot_den, precision=HIGH) + (1.0 - live)[:, None]
    return (numer / denom[:, :, None]).reshape(rows, -1)


def layer_norm(hidden, gain, shift):
    centered = hidden - jnp.mean(hidden, axis=-1, keepdims=True)
    spread = jnp.mean(centered * centered, axis=-1, keepdims=True)
    return centered * lax.rsqrt(spread + 1e-05) * gain + shift


def gelu_tanh(values):
    return jax.nn.gelu(values, approximate=True)


def inner_rows(left, right):
    return lax.dot_general(
        left, right, (((0,), (0,)), ((), ())), preferred_element_type=jnp.float32
    )


def times_transpose(left, right):
    return lax.dot_general(
        left, right, (((1,), (1,)), ((), ())), preferred_element_type=jnp.float32
    )


def by_owner_rows(grad, owners):
    return grad.reshape(owners, -1, 128)


def by_owner_columns(grad, owners):
    height, across = grad.shape
    split = grad.reshape(height, owners, across // owners)
    return jnp.transpose(split, (1, 0, 2)).reshape(owners, -1, 128)


def unpack_owned(packed, shapes):
    pieces = []
    offset = 0
    for shape in shapes:
        blocks = shape[0] * shape[1] // 128
        pieces.append(packed[0, offset : offset + blocks].reshape(shape))
        offset = offset + blocks
    return pieces


def adamw(weight, grad, first, second, rate, decay):
    first_new = 0.9 * first + 0.1 * grad
    second_new = 0.95 * second + 0.05 * grad * grad
    step_dir = first_new / (1.0 - 0.9**STEP) / (jnp.sqrt(second_new / (1.0 - 0.95**STEP)) + 1e-08)
    return (weight - rate * (step_dir + decay * weight), first_new, second_new)


def on_device(
    tokens,
    cotangent,
    lengths,
    mix_weight,
    out_weight,
    up_weight,
    down_weight,
    norm_params,
    mix_first,
    out_first,
    up_first,
    down_first,
    norm_first,
    mix_second,
    out_second,
    up_second,
    down_second,
    norm_second,
):
    rows, width = tokens.shape
    owners = lax.axis_size(("dp", "fsdp"))
    rounded = (
        mix_weight.astype(jnp.bfloat16),
        out_weight.astype(jnp.bfloat16),
        up_weight.astype(jnp.bfloat16),
        down_weight.astype(jnp.bfloat16),
    )
    mix_full, out_full, up_full, down_full = (
        lax.all_gather(rounded[0], ("dp", "fsdp"), axis=1, tiled=True),
        lax.all_gather(rounded[1], ("dp", "fsdp"), axis=0, tiled=True),
        lax.all_gather(rounded[2], ("dp", "fsdp"), axis=1, tiled=True),
        lax.all_gather(rounded[3], ("dp", "fsdp"), axis=0, tiled=True),
    )
    member, live, angle = segment_tables(lengths[0], rows)
    mixed = jnp.dot(tokens, mix_full, preferred_element_type=jnp.float32)

    def attend(queries, keys, values):
        return cos_attention(queries, keys, values, member, live, angle)

    attended, attention_pull = jax.vjp(
        attend, mixed[:, :width], mixed[:, width : 2 * width], mixed[:, 2 * width :]
    )
    attended_low = attended.astype(jnp.bfloat16)
    branch = jnp.dot(attended_low, out_full, preferred_element_type=jnp.float32)
    first, first_pull = jax.vjp(
        layer_norm, tokens.astype(jnp.float32) + branch, norm_params[0], norm_params[1]
    )
    first_low = first.astype(jnp.bfloat16)
    upper = jnp.dot(first_low, up_full, preferred_element_type=jnp.float32)
    hidden, gelu_pull = jax.vjp(gelu_tanh, upper)
    hidden_low = hidden.astype(jnp.bfloat16)
    second = jnp.dot(hidden_low, down_full, preferred_element_type=jnp.float32)
    final, final_pull = jax.vjp(layer_norm, first + second, norm_params[2], norm_params[3])
    output = (final * live[:, None]).astype(jnp.bfloat16)
    mix_full, out_full, up_full, down_full = (
        lax.all_gather(rounded[0], ("dp", "fsdp"), axis=1, tiled=True),
        lax.all_gather(rounded[1], ("dp", "fsdp"), axis=0, tiled=True),
        lax.all_gather(rounded[2], ("dp", "fsdp"), axis=1, tiled=True),
        lax.all_gather(rounded[3], ("dp", "fsdp"), axis=0, tiled=True),
    )
    grad_final = cotangent.astype(jnp.float32) * live[:, None]
    grad_sum_two, grad_gain_two, grad_bias_two = final_pull(grad_final)
    grad_second = grad_sum_two.astype(jnp.bfloat16)
    grad_down = inner_rows(hidden_low, grad_second)
    grad_hidden = times_transpose(grad_second, down_full)
    (grad_upper,) = gelu_pull(grad_hidden)
    grad_upper_low = grad_upper.astype(jnp.bfloat16)
    grad_up = inner_rows(first_low, grad_upper_low)
    grad_first = grad_sum_two + times_transpose(grad_upper_low, up_full)
    grad_sum_one, grad_gain_one, grad_bias_one = first_pull(grad_first)
    grad_branch = grad_sum_one.astype(jnp.bfloat16)
    grad_out = inner_rows(attended_low, grad_branch)
    grad_attended = times_transpose(grad_branch, out_full)
    grad_q, grad_k, grad_v = attention_pull(grad_attended)
    grad_mixed = jnp.concatenate([grad_q, grad_k, grad_v], axis=1).astype(jnp.bfloat16)
    grad_mix = inner_rows(tokens, grad_mixed)
    grad_tokens = grad_sum_one + times_transpose(grad_mixed, mix_full)
    norm_terms = jnp.stack([grad_gain_one, grad_bias_one, grad_gain_two, grad_bias_two])
    norm_grad = lax.psum(norm_terms, ("dp", "fsdp"))
    packed_all = jnp.concatenate(
        [
            by_owner_columns(grad_mix, owners),
            by_owner_rows(grad_out, owners),
            by_owner_columns(grad_up, owners),
            by_owner_rows(grad_down, owners),
        ],
        axis=1,
    )
    summed_all = lax.psum_scatter(packed_all, ("dp", "fsdp"), scatter_dimension=0, tiled=True)
    owned = tuple(
        unpack_owned(
            summed_all, (mix_weight.shape, out_weight.shape, up_weight.shape, down_weight.shape)
        )
    )
    local_sq = sum((jnp.sum(g * g) for g in owned))
    owned_sq = lax.psum(local_sq, ("dp", "fsdp"))
    global_norm = jnp.sqrt(owned_sq + jnp.sum(norm_grad * norm_grad))
    scale = 1.0 / jnp.maximum(global_norm, 1.0)
    params = (mix_weight, out_weight, up_weight, down_weight, norm_params)
    grads = (owned[0], owned[1], owned[2], owned[3], norm_grad)
    firsts = (mix_first, out_first, up_first, down_first, norm_first)
    seconds = (mix_second, out_second, up_second, down_second, norm_second)
    news = []
    for index in range(5):
        news.append(
            adamw(
                params[index],
                scale * grads[index],
                firsts[index],
                seconds[index],
                RATES[index],
                DECAYS[index],
            )
        )
    return (
        output,
        grad_tokens,
        global_norm,
        news[0][0],
        news[1][0],
        news[2][0],
        news[3][0],
        news[4][0],
        news[0][1],
        news[1][1],
        news[2][1],
        news[3][1],
        news[4][1],
        news[0][2],
        news[1][2],
        news[2][2],
        news[3][2],
        news[4][2],
    )


BF = jnp.bfloat16
F32 = jnp.float32
AXES = ("dp", "fsdp")
COST = 1000000000.0
MICROS = {
    "sort_near": 0.1,
    "attend_forward": 0.65,
    "attend_close": 0.36,
    "feed_up": 0.25,
    "down_away": 0.1,
    "down_here": 0.0,
    "turn_round": 0.0,
    "finish_forward": 0.0,
    "grad_down_away": 0.0,
    "grad_down_here": 0.0,
    "grad_up": 0.0,
    "attend_backward": 0.0,
    "grad_input": 0.0,
    "close_sums": 0.0,
    "update": 0.0,
    "grad_up_away": 0.0,
    "grad_up_here": 0.8,
    "feed_back": 0.0,
    "mix_away": 0.0,
    "mix_here": 1.5,
}
MB = 16
CHIPS = 16
BLOCK = 96
QKV = 72
PLANE = 4 * BLOCK
ZROWS = 3 * BLOCK
HALF = CHIPS * BLOCK
STEPS_Z = (8, 4, 12)


def nt(left, right):
    return lax.dot_general(
        left, right, (((1,), (1,)), ((), ())), preferred_element_type=F32
    )


def tn(left, right):
    return lax.dot_general(
        left, right, (((0,), (0,)), ((), ())), preferred_element_type=F32
    )


def nn(left, right):
    return jnp.dot(left, right, preferred_element_type=F32)


def block_places():
    places = [(BLOCK * p, p, 0) for p in range(4)]
    for p in range(4):
        for j, step in enumerate(STEPS_Z):
            places.append((PLANE + ZROWS * p + BLOCK * j, p, step))
    return places


PLACES = block_places()
PIECES = [(0, PLANE)] + [(PLANE + ZROWS * p, ZROWS) for p in range(4)]


def shard_index(chip, core, plane, step, other):
    owner = 1 - core if other else core
    first = 1 + owner
    mask = (0, first, 3 - first, 3)[plane]
    return 2 * (chip ^ mask ^ step) + owner


def call(body, outs, args, scratch=(), smem=0, place=pltpu.VMEM, name=None):
    name = name or body.__name__
    held = [math.prod(s.shape) * 4 for s in scratch]
    limit = int(sum(held) + (MB << 20))
    in_specs = [
        pl.BlockSpec(memory_space=pltpu.SMEM if i < smem else place)
        for i in range(len(args))
    ]
    return pl.pallas_call(
        body,
        out_shape=[jax.ShapeDtypeStruct(s, t) for s, t in outs],
        in_specs=in_specs,
        out_specs=[pl.BlockSpec(memory_space=pltpu.VMEM) for _ in outs],
        scratch_shapes=list(scratch),
        compiler_params=pltpu.CompilerParams(vmem_limit_bytes=limit),
        cost_estimate=pl.CostEstimate(
            flops=int(MICROS[name] * COST), bytes_accessed=0, transcendentals=0
        ),
        name=name,
    )(*args)


def sort_near(s0, s1, s2, s3, *groups):
    for g, out in enumerate(groups):
        for p, (ref, base) in enumerate(((s0, 0), (s1, 0), (s2, 0), (s3, 0))):
            at = base + BLOCK * g
            out[BLOCK * p : BLOCK * p + BLOCK, :] = ref[at : at + BLOCK, :]


def segment_of(lengths, place):
    start = jnp.int32(0)
    seg = jnp.full(place.shape, -1, jnp.int32)
    offset = jnp.zeros(place.shape, F32)
    extent = jnp.ones(place.shape, F32)
    for s in range(5):
        size = lengths[0, s]
        inside = (place >= start) & (place < start + size)
        seg = jnp.where(inside, s, seg)
        offset = jnp.where(inside, (place - start).astype(F32), offset)
        extent = jnp.where(inside, size.astype(F32), extent)
        start = start + size
    angle = 0.5 * math.pi * offset / extent
    return seg, jnp.cos(angle), jnp.sin(angle)


def pair_mask(lengths, rows):
    seg_i, cos_i, sin_i = segment_of(lengths, lax.broadcasted_iota(jnp.int32, (1, rows), 1))
    seg_j, cos_j, sin_j = segment_of(lengths, lax.broadcasted_iota(jnp.int32, (rows, 1), 0))
    same = (seg_i == seg_j) & (seg_i >= 0)
    dead = jnp.where(seg_i >= 0, 0.0, 1.0)
    return jnp.where(same, cos_j * cos_i + sin_j * sin_i, 0.0), dead


def softplus(v):
    return jnp.maximum(v, 0.0) + jnp.log1p(jnp.exp(-jnp.abs(v)))


def attend_forward(
    lengths, me, x_ref, so, z0, z1, z2, z3, sp, y0, y1, y2, y3,
    mix, att, den, rel_own, rel_par,
):
    rows = x_ref.shape[0]
    width = x_ref.shape[1]
    chip, core = me[0], me[1]
    x = x_ref[...]
    sides = ((False, (so, z0, z1, z2, z3), rel_own), (True, (sp, y0, y1, y2, y3), rel_par))
    for other, refs, _ in sides:
        for (base, size), ref in zip(PIECES, refs):
            got = nt(ref[...], x)
            for at, plane, step in PLACES:
                if base <= at < base + size:
                    d = shard_index(chip, core, plane, step, other)
                    mix[pl.ds(pl.multiple_of(QKV * d, 8), QKV), :] = got[
                        at - base : at - base + QKV
                    ]
    mask, dead = pair_mask(lengths, rows)
    for h in range(width // DH):
        here = slice(DH * h, DH * h + DH)
        fq = softplus(mix[here, :]).astype(BF)
        fk = softplus(mix[width + DH * h : width + DH * h + DH, :]).astype(BF)
        v = mix[2 * width + DH * h : 2 * width + DH * h + DH, :].astype(BF)
        pairs = tn(fk, fq) * mask
        total = jnp.sum(pairs, axis=0, keepdims=True) + dead
        den[h : h + 1, :] = total
        att[here, :] = nn(v, pairs.astype(BF)) / total
    side = QKV // 3
    blank = jnp.zeros((QKV, rows), F32)
    for other, _, rel in sides:
        for at, plane, step in PLACES:
            d = shard_index(chip, core, plane, step, other)
            part = att[pl.ds(pl.multiple_of(side * d, 8), side), :]
            rel[at : at + BLOCK, :] = jnp.concatenate([blank, part], axis=0).astype(BF)


def attend_close(
    x_ref, rel_own, rel_par, so, z0, z1, z2, z3, sp, y0, y1, y2, y3, norms,
    first, first_low, xhat, rstd,
):
    branch = x_ref[...].astype(F32)
    for refs, rel in (((so, z0, z1, z2, z3), rel_own), ((sp, y0, y1, y2, y3), rel_par)):
        for (base, size), ref in zip(PIECES, refs):
            branch = branch + tn(rel[base : base + size, :], ref[...])
    centered = branch - jnp.mean(branch, axis=-1, keepdims=True)
    spread = jnp.mean(centered * centered, axis=-1, keepdims=True)
    scale = lax.rsqrt(spread + 1e-05)
    hat = centered * scale
    xhat[...] = hat
    rstd[...] = scale
    out = hat * norms[0:1, :] + norms[1:2, :]
    first[...] = out
    first_low[...] = out.astype(BF)


GELU_A = math.sqrt(2.0 / math.pi)
GELU_B = 0.044715


def feed_up(ya, yb, s, z0, z1, z2, z3, hid, slope):
    rows = ya.shape[0]
    for half, y in ((0, ya), (1, yb)):
        cols = slice(half * rows, half * rows + rows)
        for (base, size), ref in zip(PIECES, (s, z0, z1, z2, z3)):
            u = nt(ref[...], y[...])
            sq = u * u
            t = jnp.tanh(GELU_A * u * (1.0 + GELU_B * sq))
            half_up = 0.5 * (1.0 + t)
            hid[base : base + size, cols] = (u * half_up).astype(BF)
            slope[base : base + size, cols] = half_up + 0.5 * u * (1.0 - t * t) * (
                GELU_A * (1.0 + 3.0 * GELU_B * sq)
            )


def down_away(hid, s, z0, z1, z2, z3, other, whole):
    for (base, size), ref in zip(PIECES, (s, z0, z1, z2, z3)):
        whole[base : base + size, :] = ref[...]
    rows = other.shape[0]
    other[...] = tn(hid[:, rows : 2 * rows], whole[...])


def down_here(hid, whole, own):
    own[...] = tn(hid[:, 0 : own.shape[0]], whole[...])


def norm_back(dy, gain, hat, scale):
    dhat = dy * gain
    return scale * (
        dhat
        - jnp.mean(dhat, axis=-1, keepdims=True)
        - hat * jnp.mean(dhat * hat, axis=-1, keepdims=True)
    )


def live_rows(lengths, rows):
    used = jnp.int32(0)
    for s in range(5):
        used = used + lengths[0, s]
    return jnp.where(lax.broadcasted_iota(jnp.int32, (rows, 1), 0) < used, 1.0, 0.0)


def turn_round(lengths, first, own, got, cot, norms, ds2, dz, xhat):
    h = first[...] + (own[...] + got[...])
    centered = h - jnp.mean(h, axis=-1, keepdims=True)
    spread = jnp.mean(centered * centered, axis=-1, keepdims=True)
    scale = lax.rsqrt(spread + 1e-05)
    hat = centered * scale
    xhat[...] = hat
    dy = cot[...].astype(F32) * live_rows(lengths, first.shape[0])
    back = norm_back(dy, norms[2:3, :], hat, scale)
    ds2[...] = back
    dz[...] = back.astype(BF)


def finish_forward(lengths, xhat, cot, norms, out, terms):
    live = live_rows(lengths, xhat.shape[0])
    hat = xhat[...]
    out[...] = ((hat * norms[2:3, :] + norms[3:4, :]) * live).astype(BF)
    dy = cot[...].astype(F32) * live
    terms[0:1, :] = jnp.sum(dy * hat, axis=0, keepdims=True)
    terms[1:2, :] = jnp.sum(dy, axis=0, keepdims=True)


def rows_away(get, send):
    near = get(slice(2 * BLOCK, PLANE)).astype(BF)
    far = get(slice(PLANE + 2 * ZROWS, HALF)).astype(BF)
    for p in range(2):
        send[PLANE * p : PLANE * p + BLOCK, :] = near[BLOCK * p : BLOCK * p + BLOCK]
        send[PLANE * p + BLOCK : PLANE * p + PLANE, :] = far[ZROWS * p : ZROWS * p + ZROWS]


def rows_here(get, turn, own):
    near = get(slice(0, 2 * BLOCK))
    far = get(slice(PLANE, PLANE + 2 * ZROWS))
    for p, ref in enumerate((own, turn)):
        ref[0:BLOCK, :] = near[BLOCK * p : BLOCK * p + BLOCK]
        ref[BLOCK:PLANE, :] = far[ZROWS * p : ZROWS * p + ZROWS]


def two_cores(hid, za, zb):
    rows = za.shape[0]
    return lambda here: nn(hid[here, 0:rows], za[...]) + nn(
        hid[here, rows : 2 * rows], zb[...]
    )


def grad_away(hid, za, zb, send):
    rows_away(two_cores(hid, za, zb), send)


def grad_here(hid, za, zb, turn, own):
    rows_here(two_cores(hid, za, zb), turn, own)


def feed_back(
    slope, za, zb, d, s, z0, z1, z2, z3, dup, mine, other, whole,
):
    rows = za.shape[0]
    for base, size in PIECES:
        here = slice(base, base + size)
        w = d[here, :]
        dup[here, 0:rows] = (nt(w, za[...]) * slope[here, 0:rows]).astype(BF)
        dup[here, rows:] = (nt(w, zb[...]) * slope[here, rows:]).astype(BF)
    for (base, size), ref in zip(PIECES, (s, z0, z1, z2, z3)):
        whole[base : base + size, :] = ref[...]
    w = whole[...]
    other[...] = tn(dup[:, rows : 2 * rows], w)
    mine[...] = tn(dup[:, 0:rows], w)


def attend_backward(
    lengths, me, ds2, mine, got, xhat, rstd, norms, mix, att, den,
    so, z0, z1, z2, z3, sp, y0, y1, y2, y3,
    dh_ref, do_ref, terms, rel_own, rel_par, datt, dmix,
):
    rows, width = ds2.shape
    chip, core = me[0], me[1]
    dy1 = ds2[...] + (mine[...] + got[...])
    hat = xhat[...]
    terms[0:1, :] = jnp.sum(dy1 * hat, axis=0, keepdims=True)
    terms[1:2, :] = jnp.sum(dy1, axis=0, keepdims=True)
    dh = norm_back(dy1, norms[0:1, :], hat, rstd[...])
    dh_ref[...] = dh
    do = dh.astype(BF)
    do_ref[...] = do
    side = QKV // 3
    sides = ((False, (so, z0, z1, z2, z3), rel_own), (True, (sp, y0, y1, y2, y3), rel_par))
    for other, refs, _ in sides:
        for (base, size), ref in zip(PIECES, refs):
            got_t = nt(ref[...], do)
            for at, plane, step in PLACES:
                if base <= at < base + size:
                    d = shard_index(chip, core, plane, step, other)
                    datt[pl.ds(pl.multiple_of(side * d, 8), side), :] = got_t[
                        at - base + QKV : at - base + BLOCK
                    ]
    mask, _ = pair_mask(lengths, rows)
    for h in range(width // DH):
        here = slice(DH * h, DH * h + DH)
        q = mix[here, :]
        k = mix[width + DH * h : width + DH * h + DH, :]
        v = mix[2 * width + DH * h : 2 * width + DH * h + DH, :].astype(BF)
        fq = softplus(q).astype(BF)
        fk = softplus(k).astype(BF)
        pairs = (tn(fk, fq) * mask).astype(BF)
        da = datt[here, :]
        total = den[h : h + 1, :]
        dnum = da / total
        dden = -jnp.sum(dnum * att[here, :], axis=0, keepdims=True)
        dnum = dnum.astype(BF)
        dpairs = ((tn(v, dnum) + dden) * mask).astype(BF)
        dmix[2 * width + DH * h : 2 * width + DH * h + DH, :] = nt(dnum, pairs)
        dmix[width + DH * h : width + DH * h + DH, :] = nt(fq, dpairs) * jax.nn.sigmoid(k)
        dmix[here, :] = nn(fk, dpairs) * jax.nn.sigmoid(q)
    blank = jnp.zeros((BLOCK - QKV, rows), F32)
    for other, _, rel in sides:
        for at, plane, step in PLACES:
            d = shard_index(chip, core, plane, step, other)
            part = dmix[pl.ds(pl.multiple_of(QKV * d, 8), QKV), :]
            rel[at : at + BLOCK, :] = jnp.concatenate([part, blank], axis=0).astype(BF)


def four_terms(dma, dmb, xa, xb, ata, atb, doa, dob):
    return lambda here: (nn(dma[here, :], xa[...]) + nn(dmb[here, :], xb[...])) + (
        nn(ata[here, :], doa[...]) + nn(atb[here, :], dob[...])
    )


def mix_away(dma, dmb, xa, xb, ata, atb, doa, dob, send):
    rows_away(four_terms(dma, dmb, xa, xb, ata, atb, doa, dob), send)


def mix_here(dma, dmb, xa, xb, ata, atb, doa, dob, turn, own):
    rows_here(four_terms(dma, dmb, xa, xb, ata, atb, doa, dob), turn, own)


def grad_input(dh, rel_own, rel_par, so, z0, z1, z2, z3, sp, y0, y1, y2, y3, out):
    total = dh[...]
    for refs, rel in (((so, z0, z1, z2, z3), rel_own), ((sp, y0, y1, y2, y3), rel_par)):
        for (base, size), ref in zip(PIECES, refs):
            total = total + tn(rel[base : base + size, :], ref[...])
    out[...] = total


def close_sums(k1, a1, b1, c1, g2, g3, t1, t2, g1, note):
    s1 = (k1[...] + a1[...].astype(F32)) + (b1[...].astype(F32) + c1[...].astype(F32))
    g1[...] = s1
    sq = s1 * s1 + g2[...] * g2[...] + g3[...] * g3[...]
    note[0:2, :] = t1[...]
    note[2:4, :] = t2[...]
    note[4:5, :] = jnp.sum(sq, axis=0, keepdims=True)
    note[5:8, :] = jnp.zeros((3, note.shape[1]), F32)


def update(
    n0, n1, n2, n3, g1, g2, g3, mw, ow, uw, dw, nw, mm, om, um, dm, nm, mv, ov, uv, dv, nv,
    norm_out, mw2, ow2, uw2, dw2, nw2, mm2, om2, um2, dm2, nm2, mv2, ov2, uv2, dv2, nv2,
):
    note = (n0[...] + n1[...]) + (n2[...] + n3[...])
    terms = note[0:4, :]
    total = jnp.sum(note[4:5, :]) + jnp.sum(terms * terms)
    norm = jnp.sqrt(jnp.full((1, 1), total, F32))
    norm_out[...] = norm
    scale = 1.0 / jnp.maximum(norm, 1.0)

    one = g1[...]
    grads = (one[0:QKV], one[QKV:BLOCK], g2[...], g3[...], terms)
    groups = (
        (mw, mm, mv, mw2, mm2, mv2),
        (ow, om, ov, ow2, om2, ov2),
        (uw, um, uv, uw2, um2, uv2),
        (dw, dm, dv, dw2, dm2, dv2),
        (nw, nm, nv, nw2, nm2, nv2),
    )
    for g, (w, m, v, w2, m2, v2), rate, decay in zip(grads, groups, RATES, DECAYS):
        new_w, new_m, new_v = adamw(w[...], scale * g, m[...], v[...], rate, decay)
        w2[...] = new_w
        m2[...] = new_m
        v2[...] = new_v


def tie(value, *others):
    return lax.optimization_barrier((value,) + others)[0]


def swap(value):
    return lax.ppermute(value, "fsdp", [(0, 1), (1, 0)])


def hop_first(value):
    return lax.ppermute(value, AXES, [(i, i ^ (4 if i % 2 else 2)) for i in range(2 * CHIPS)])


def hop_second(value):
    return lax.ppermute(value, AXES, [(i, i ^ (2 if i % 2 else 4)) for i in range(2 * CHIPS)])


def hop_z(value, step):
    return lax.ppermute(value, "dp", [(i, i ^ step) for i in range(CHIPS)])


def add_first(turn, got):
    return (turn + got[PLANE:].astype(F32)).astype(BF)


def add_second(own, got, back):
    total = own + got[:PLANE].astype(F32) + back.astype(F32)
    return total[:BLOCK], total.astype(BF)


def send_z(low):
    return [
        hop_z(low[BLOCK * (j + 1) : BLOCK * (j + 2)], step) for j, step in enumerate(STEPS_Z)
    ]


def tuned_device(
    tokens, cotangent, lengths,
    mix_weight, out_weight, up_weight, down_weight, norm_params,
    mix_first, out_first, up_first, down_first, norm_first,
    mix_second, out_second, up_second, down_second, norm_second,
):
    rows, width = tokens.shape
    chip, core = lax.axis_index("dp"), lax.axis_index("fsdp")
    me = jnp.stack([chip, core]).astype(jnp.int32)
    wide = 3 * width

    blocks = [
        jnp.concatenate([mix_weight.T.astype(BF), out_weight.astype(BF)], axis=0),
        up_weight.T.astype(BF),
        down_weight.astype(BF),
    ]
    s_all = jnp.concatenate(blocks, axis=0)
    def wide_join(*parts):
        return jnp.concatenate(parts, axis=0)

    def z_round(block, direct, before):
        if direct:
            got = [hop_z(tie(block, *before), step) for step in STEPS_Z]
            return got, wide_join(*got)
        far = hop_z(tie(block, *before), 8)
        near = hop_z(wide_join(block, far), 4)
        return [far, near], wide_join(far, near)

    s_first = hop_first(s_all)
    s_second = hop_second(s_all)
    near1, joined1 = z_round(blocks[0], True, ())
    near2, joined2 = z_round(blocks[1], False, (near1[0],))
    near3, joined3 = z_round(blocks[2], False, (near2[0],))
    s_third = hop_second(s_first)
    s_parts = (s_all, s_first, s_second, s_third)
    turned1 = hop_first(tie(joined1, s_second))
    across1 = hop_second(tie(joined1, s_second))
    corner1 = hop_second(tie(turned1, s_third))
    turned2 = hop_first(tie(joined2, turned1))
    across2 = hop_second(tie(joined2, across1))
    corner2 = hop_second(tie(turned2, corner1))
    sorted1, sorted2, sorted3 = call(
        sort_near,
        [((PLANE, width), BF)] * 3,
        s_parts,
    )
    up_all = (sorted2, joined2, turned2, across2, corner2)
    attn_own = (sorted1, joined1, turned1, across1, corner1)
    attn_par = tuple(swap(p) for p in attn_own)
    x_par = swap(tokens)

    mix, att, den, at_own, at_par = call(
        attend_forward,
        [
            ((wide, rows), F32), ((width, rows), F32), ((16, rows), F32),
            ((HALF, rows), BF), ((HALF, rows), BF),
        ],
        (lengths, me, tie(tokens, x_par)) + attn_own + attn_par,
        smem=2,
    )
    turned3 = hop_first(tie(joined3, turned2))
    across3 = hop_second(tie(joined3, across2))
    first, first_low, xhat, rstd = call(
        attend_close,
        [((rows, width), F32), ((rows, width), BF), ((rows, width), F32), ((rows, 1), F32)],
        (tokens, at_own, at_par) + attn_own + attn_par + (norm_params,),
    )
    corner3 = hop_second(tie(turned3, corner2, first_low))
    down_all = (sorted3, joined3, turned3, across3, corner3)
    at_got = swap(at_par)
    first_par = swap(first_low)
    hid, slope = call(
        feed_up,
        [((HALF, 2 * rows), BF), ((HALF, 2 * rows), F32)],
        (first_low, tie(first_par, at_got)) + up_all,
    )
    down_par, down_full = call(
        down_away, [((rows, width), F32), ((HALF, width), BF)], (hid,) + down_all
    )
    down_got = swap(down_par)
    (down_own,) = call(down_here, [((rows, width), F32)], (tie(hid, down_par), down_full))
    ds2, dz, xhat_two = call(
        turn_round,
        [((rows, width), F32), ((rows, width), BF), ((rows, width), F32)],
        (lengths, first, down_own, down_got, cotangent, norm_params),
        smem=1,
    )
    dz_par = swap(dz)
    output, terms_two = call(
        finish_forward,
        [((rows, width), BF), ((2, width), F32)],
        (lengths, xhat_two, cotangent, norm_params),
        smem=1,
    )
    away = [((2 * PLANE, width), BF)]
    stay = [((PLANE, width), F32)] * 2
    (send3,) = call(grad_away, away, (hid, dz, dz_par), name="grad_down_away")
    got3 = hop_second(send3)
    dup, dy_own, dy_par = call(
        feed_back,
        [((HALF, 2 * rows), BF)] + [((rows, width), F32)] * 2,
        (slope, tie(dz, send3, terms_two), dz_par, down_full) + up_all,
        scratch=[pltpu.VMEM((HALF, width), BF)],
    )
    (send2,) = call(grad_away, away, (dup, first_low, first_par), name="grad_up_away")
    got2 = hop_second(send2)
    dh, do, terms_one, dm_own, dm_par = call(
        attend_backward,
        [
            ((rows, width), F32), ((rows, width), BF), ((2, width), F32),
            ((HALF, rows), BF), ((HALF, rows), BF),
        ],
        (
            lengths, me, ds2, dy_own, swap(dy_par), xhat, rstd,
            norm_params, mix, att, den,
        ) + attn_own + attn_par,
        scratch=[pltpu.VMEM((width, rows), F32), pltpu.VMEM((wide, rows), F32)],
        smem=2,
    )
    turn3, own3 = call(
        grad_here, stay, (hid, dz, dz_par), name="grad_down_here"
    )
    turn2, own2 = call(
        grad_here, stay, (dup, first_low, first_par),
        name="grad_up_here",
    )
    low_turn3 = add_first(turn3, got3)
    back3 = hop_first(low_turn3)
    low_turn2 = add_first(turn2, got2)
    back2 = hop_first(low_turn2)
    factors = (
        dm_own, swap(dm_par), tokens, x_par, at_own, at_got,
        do, swap(do),
    )
    (send1,) = call(mix_away, away, factors)
    keep3, low3 = add_second(own3, got3, back3)
    parts3 = send_z(low3)
    got1 = hop_second(tie(send1, back3))
    turn1, own1 = call(mix_here, stay, (tie(dm_own, send1),) + factors[1:])
    (grad_tokens,) = call(
        grad_input,
        [((rows, width), F32)],
        (tie(dh, send1), dm_own, dm_par) + attn_own + attn_par,
    )
    keep2, low2 = add_second(own2, got2, back2)
    parts2 = send_z(tie(low2, parts3[1]))
    back1 = hop_first(add_first(tie(turn1, grad_tokens), got1))
    keep1, low1 = add_second(own1, got1, back1)
    parts1 = send_z(tie(low1, parts2[1]))
    g3 = (keep3 + parts3[0]) + (parts3[1].astype(F32) + parts3[2].astype(F32))
    g2 = (keep2 + parts2[0]) + (parts2[1].astype(F32) + parts2[2].astype(F32))
    g1, note = call(
        close_sums,
        [((BLOCK, width), F32), ((8, width), F32)],
        (keep1,) + tuple(parts1) + (g2, g3, terms_one, terms_two),
    )
    note = note + swap(note)
    note = (note + hop_z(note, 1)) + (hop_z(note, 2) + hop_z(note, 3))
    notes = (note, hop_z(note, 4), hop_z(note, 8), hop_z(note, 12))
    shapes = [
        (mix_weight.shape[::-1], F32), (out_weight.shape, F32), (up_weight.shape[::-1], F32),
        (down_weight.shape, F32), (norm_params.shape, F32),
    ]
    norm, *news = call(
        update,
        [((1, 1), F32)] + shapes * 3,
        notes + (
            g1, g2, g3, mix_weight.T, out_weight, up_weight.T, down_weight, norm_params,
            mix_first.T, out_first, up_first.T, down_first, norm_first,
            mix_second.T, out_second, up_second.T, down_second, norm_second,
        ),
    )
    for at in (0, 2, 5, 7, 10, 12):
        news[at] = news[at].T
    return (output, grad_tokens, norm.reshape(())) + tuple(news)


def solution(mesh):
    in_specs = (
        P(("dp", "fsdp"), None),
        P(("dp", "fsdp"), None),
        P(("dp", "fsdp"), None),
        P(None, ("dp", "fsdp")),
        P(("dp", "fsdp"), None),
        P(None, ("dp", "fsdp")),
        P(("dp", "fsdp"), None),
        P(),
        P(None, ("dp", "fsdp")),
        P(("dp", "fsdp"), None),
        P(None, ("dp", "fsdp")),
        P(("dp", "fsdp"), None),
        P(),
        P(None, ("dp", "fsdp")),
        P(("dp", "fsdp"), None),
        P(None, ("dp", "fsdp")),
        P(("dp", "fsdp"), None),
        P(),
    )
    out_specs = (
        P(("dp", "fsdp"), None),
        P(("dp", "fsdp"), None),
        P(),
        P(None, ("dp", "fsdp")),
        P(("dp", "fsdp"), None),
        P(None, ("dp", "fsdp")),
        P(("dp", "fsdp"), None),
        P(),
        P(None, ("dp", "fsdp")),
        P(("dp", "fsdp"), None),
        P(None, ("dp", "fsdp")),
        P(("dp", "fsdp"), None),
        P(),
        P(None, ("dp", "fsdp")),
        P(("dp", "fsdp"), None),
        P(None, ("dp", "fsdp")),
        P(("dp", "fsdp"), None),
        P(),
    )
    sizes = dict(mesh.shape)
    tuned = sizes["dp"] == CHIPS and sizes["fsdp"] == 2
    return jax.shard_map(
        tuned_device if tuned else on_device, mesh=mesh, in_specs=in_specs, out_specs=out_specs, check_vma=False
    )
```

```python
import math

import jax
import jax.numpy as jnp
from jax import lax
from jax.experimental import pallas as pl
from jax.experimental.pallas import tpu as pltpu
from jax.sharding import PartitionSpec as P

DH = 64
STEP = 10


HIGH = lax.Precision.HIGHEST
RATES = (0.01, 0.08, 0.01, 0.01, 0.2)
DECAYS = (0.1, 0.1, 0.1, 0.1, 0.0)


def segment_tables(lengths, rows):
    ends = jnp.cumsum(lengths)
    starts = ends - lengths
    places = jnp.arange(rows, dtype=jnp.int32)
    inside = (places[None, :] >= starts[:, None]) & (places[None, :] < ends[:, None])
    member = inside[:-1].astype(jnp.float32)
    live = jnp.sum(member, axis=0)
    offset = places.astype(jnp.float32) - jnp.sum(
        member * starts[:-1, None].astype(jnp.float32), axis=0
    )
    extent = jnp.sum(member * lengths[:-1, None].astype(jnp.float32), axis=0) + (1.0 - live)
    angle = 0.5 * math.pi * offset / extent
    return (member, live, angle)


def cos_attention(queries, keys, values, member, live, angle):
    rows = queries.shape[0]
    feat_q = jax.nn.softplus(queries).reshape(rows, -1, DH)
    feat_k = jax.nn.softplus(keys).reshape(rows, -1, DH)
    vals = values.reshape(rows, -1, DH)
    phases = jnp.stack([jnp.cos(angle), jnp.sin(angle)])
    weighted = member[None] * phases[:, None, :]
    scaled = jnp.einsum("psr,rhd->psrhd", weighted, feat_k)
    state = jnp.einsum("psrhd,rhe->pshde", scaled, vals, precision=HIGH)
    normal = jnp.sum(scaled, axis=2)
    query_side = feat_q[None] * phases[:, :, None, None]
    per_slot = jnp.einsum("prhd,pshde->rshe", query_side, state, precision=HIGH)
    numer = jnp.einsum("sr,rshe->rhe", member, per_slot, precision=HIGH)
    slot_den = jnp.einsum("prhd,pshd->rsh", query_side, normal, precision=HIGH)
    denom = jnp.einsum("sr,rsh->rh", member, slot_den, precision=HIGH) + (1.0 - live)[:, None]
    return (numer / denom[:, :, None]).reshape(rows, -1)


def layer_norm(hidden, gain, shift):
    centered = hidden - jnp.mean(hidden, axis=-1, keepdims=True)
    spread = jnp.mean(centered * centered, axis=-1, keepdims=True)
    return centered * lax.rsqrt(spread + 1e-05) * gain + shift


def gelu_tanh(values):
    return jax.nn.gelu(values, approximate=True)


def inner_rows(left, right):
    return lax.dot_general(
        left, right, (((0,), (0,)), ((), ())), preferred_element_type=jnp.float32
    )


def times_transpose(left, right):
    return lax.dot_general(
        left, right, (((1,), (1,)), ((), ())), preferred_element_type=jnp.float32
    )


def by_owner_rows(grad, owners):
    return grad.reshape(owners, -1, 128)


def by_owner_columns(grad, owners):
    height, across = grad.shape
    split = grad.reshape(height, owners, across // owners)
    return jnp.transpose(split, (1, 0, 2)).reshape(owners, -1, 128)


def unpack_owned(packed, shapes):
    pieces = []
    offset = 0
    for shape in shapes:
        blocks = shape[0] * shape[1] // 128
        pieces.append(packed[0, offset : offset + blocks].reshape(shape))
        offset = offset + blocks
    return pieces


def adamw(weight, grad, first, second, rate, decay):
    first_new = 0.9 * first + 0.1 * grad
    second_new = 0.95 * second + 0.05 * grad * grad
    step_dir = first_new / (1.0 - 0.9**STEP) / (jnp.sqrt(second_new / (1.0 - 0.95**STEP)) + 1e-08)
    return (weight - rate * (step_dir + decay * weight), first_new, second_new)


def on_device(
    tokens,
    cotangent,
    lengths,
    mix_weight,
    out_weight,
    up_weight,
    down_weight,
    norm_params,
    mix_first,
    out_first,
    up_first,
    down_first,
    norm_first,
    mix_second,
    out_second,
    up_second,
    down_second,
    norm_second,
):
    rows, width = tokens.shape
    owners = lax.axis_size(("dp", "fsdp"))
    rounded = (
        mix_weight.astype(jnp.bfloat16),
        out_weight.astype(jnp.bfloat16),
        up_weight.astype(jnp.bfloat16),
        down_weight.astype(jnp.bfloat16),
    )
    mix_full, out_full, up_full, down_full = (
        lax.all_gather(rounded[0], ("dp", "fsdp"), axis=1, tiled=True),
        lax.all_gather(rounded[1], ("dp", "fsdp"), axis=0, tiled=True),
        lax.all_gather(rounded[2], ("dp", "fsdp"), axis=1, tiled=True),
        lax.all_gather(rounded[3], ("dp", "fsdp"), axis=0, tiled=True),
    )
    member, live, angle = segment_tables(lengths[0], rows)
    mixed = jnp.dot(tokens, mix_full, preferred_element_type=jnp.float32)

    def attend(queries, keys, values):
        return cos_attention(queries, keys, values, member, live, angle)

    attended, attention_pull = jax.vjp(
        attend, mixed[:, :width], mixed[:, width : 2 * width], mixed[:, 2 * width :]
    )
    attended_low = attended.astype(jnp.bfloat16)
    branch = jnp.dot(attended_low, out_full, preferred_element_type=jnp.float32)
    first, first_pull = jax.vjp(
        layer_norm, tokens.astype(jnp.float32) + branch, norm_params[0], norm_params[1]
    )
    first_low = first.astype(jnp.bfloat16)
    upper = jnp.dot(first_low, up_full, preferred_element_type=jnp.float32)
    hidden, gelu_pull = jax.vjp(gelu_tanh, upper)
    hidden_low = hidden.astype(jnp.bfloat16)
    second = jnp.dot(hidden_low, down_full, preferred_element_type=jnp.float32)
    final, final_pull = jax.vjp(layer_norm, first + second, norm_params[2], norm_params[3])
    output = (final * live[:, None]).astype(jnp.bfloat16)
    mix_full, out_full, up_full, down_full = (
        lax.all_gather(rounded[0], ("dp", "fsdp"), axis=1, tiled=True),
        lax.all_gather(rounded[1], ("dp", "fsdp"), axis=0, tiled=True),
        lax.all_gather(rounded[2], ("dp", "fsdp"), axis=1, tiled=True),
        lax.all_gather(rounded[3], ("dp", "fsdp"), axis=0, tiled=True),
    )
    grad_final = cotangent.astype(jnp.float32) * live[:, None]
    grad_sum_two, grad_gain_two, grad_bias_two = final_pull(grad_final)
    grad_second = grad_sum_two.astype(jnp.bfloat16)
    grad_down = inner_rows(hidden_low, grad_second)
    grad_hidden = times_transpose(grad_second, down_full)
    (grad_upper,) = gelu_pull(grad_hidden)
    grad_upper_low = grad_upper.astype(jnp.bfloat16)
    grad_up = inner_rows(first_low, grad_upper_low)
    grad_first = grad_sum_two + times_transpose(grad_upper_low, up_full)
    grad_sum_one, grad_gain_one, grad_bias_one = first_pull(grad_first)
    grad_branch = grad_sum_one.astype(jnp.bfloat16)
    grad_out = inner_rows(attended_low, grad_branch)
    grad_attended = times_transpose(grad_branch, out_full)
    grad_q, grad_k, grad_v = attention_pull(grad_attended)
    grad_mixed = jnp.concatenate([grad_q, grad_k, grad_v], axis=1).astype(jnp.bfloat16)
    grad_mix = inner_rows(tokens, grad_mixed)
    grad_tokens = grad_sum_one + times_transpose(grad_mixed, mix_full)
    norm_terms = jnp.stack([grad_gain_one, grad_bias_one, grad_gain_two, grad_bias_two])
    norm_grad = lax.psum(norm_terms, ("dp", "fsdp"))
    packed_all = jnp.concatenate(
        [
            by_owner_columns(grad_mix, owners),
            by_owner_rows(grad_out, owners),
            by_owner_columns(grad_up, owners),
            by_owner_rows(grad_down, owners),
        ],
        axis=1,
    )
    summed_all = lax.psum_scatter(packed_all, ("dp", "fsdp"), scatter_dimension=0, tiled=True)
    owned = tuple(
        unpack_owned(
            summed_all, (mix_weight.shape, out_weight.shape, up_weight.shape, down_weight.shape)
        )
    )
    local_sq = sum((jnp.sum(g * g) for g in owned))
    owned_sq = lax.psum(local_sq, ("dp", "fsdp"))
    global_norm = jnp.sqrt(owned_sq + jnp.sum(norm_grad * norm_grad))
    scale = 1.0 / jnp.maximum(global_norm, 1.0)
    params = (mix_weight, out_weight, up_weight, down_weight, norm_params)
    grads = (owned[0], owned[1], owned[2], owned[3], norm_grad)
    firsts = (mix_first, out_first, up_first, down_first, norm_first)
    seconds = (mix_second, out_second, up_second, down_second, norm_second)
    news = []
    for index in range(5):
        news.append(
            adamw(
                params[index],
                scale * grads[index],
                firsts[index],
                seconds[index],
                RATES[index],
                DECAYS[index],
            )
        )
    return (
        output,
        grad_tokens,
        global_norm,
        news[0][0],
        news[1][0],
        news[2][0],
        news[3][0],
        news[4][0],
        news[0][1],
        news[1][1],
        news[2][1],
        news[3][1],
        news[4][1],
        news[0][2],
        news[1][2],
        news[2][2],
        news[3][2],
        news[4][2],
    )


BF = jnp.bfloat16
F32 = jnp.float32
AXES = ("dp", "fsdp")
COST = 1000000000.0
MICROS = {
    "sort_near": 0.1,
    "attend_forward": 0.65,
    "attend_close": 0.36,
    "feed_up": 0.25,
    "down_away": 0.1,
    "down_here": 0.0,
    "turn_round": 0.0,
    "finish_forward": 0.0,
    "grad_down_away": 0.0,
    "grad_down_here": 0.0,
    "grad_up": 0.0,
    "attend_backward": 0.0,
    "grad_input": 0.0,
    "close_sums": 0.0,
    "update": 0.0,
    "grad_up_away": 0.0,
    "grad_up_here": 0.8,
    "feed_back": 1.0,
    "mix_away": 0.4,
    "mix_here": 1.5,
}
MB = 16
CHIPS = 16
BLOCK = 96
QKV = 72
PLANE = 4 * BLOCK
ZROWS = 3 * BLOCK
HALF = CHIPS * BLOCK
STEPS_Z = (8, 4, 12)


def nt(left, right):
    return lax.dot_general(
        left, right, (((1,), (1,)), ((), ())), preferred_element_type=F32
    )


def tn(left, right):
    return lax.dot_general(
        left, right, (((0,), (0,)), ((), ())), preferred_element_type=F32
    )


def nn(left, right):
    return jnp.dot(left, right, preferred_element_type=F32)


def block_places():
    places = [(BLOCK * p, p, 0) for p in range(4)]
    for p in range(4):
        for j, step in enumerate(STEPS_Z):
            places.append((PLANE + ZROWS * p + BLOCK * j, p, step))
    return places


PLACES = block_places()
PIECES = [(0, PLANE)] + [(PLANE + ZROWS * p, ZROWS) for p in range(4)]


def shard_index(chip, core, plane, step, other):
    owner = 1 - core if other else core
    first = 1 + owner
    mask = (0, first, 3 - first, 3)[plane]
    return 2 * (chip ^ mask ^ step) + owner


def call(body, outs, args, scratch=(), smem=0, place=pltpu.VMEM, name=None):
    name = name or body.__name__
    held = [math.prod(s.shape) * 4 for s in scratch]
    limit = int(sum(held) + (MB << 20))
    in_specs = [
        pl.BlockSpec(memory_space=pltpu.SMEM if i < smem else place)
        for i in range(len(args))
    ]
    return pl.pallas_call(
        body,
        out_shape=[jax.ShapeDtypeStruct(s, t) for s, t in outs],
        in_specs=in_specs,
        out_specs=[pl.BlockSpec(memory_space=pltpu.VMEM) for _ in outs],
        scratch_shapes=list(scratch),
        compiler_params=pltpu.CompilerParams(vmem_limit_bytes=limit),
        cost_estimate=pl.CostEstimate(
            flops=int(MICROS[name] * COST), bytes_accessed=0, transcendentals=0
        ),
        name=name,
    )(*args)


def sort_near(s0, s1, s2, s3, *groups):
    for g, out in enumerate(groups):
        for p, (ref, base) in enumerate(((s0, 0), (s1, 0), (s2, 0), (s3, 0))):
            at = base + BLOCK * g
            out[BLOCK * p : BLOCK * p + BLOCK, :] = ref[at : at + BLOCK, :]


def segment_of(lengths, place):
    start = jnp.int32(0)
    seg = jnp.full(place.shape, -1, jnp.int32)
    offset = jnp.zeros(place.shape, F32)
    extent = jnp.ones(place.shape, F32)
    for s in range(5):
        size = lengths[0, s]
        inside = (place >= start) & (place < start + size)
        seg = jnp.where(inside, s, seg)
        offset = jnp.where(inside, (place - start).astype(F32), offset)
        extent = jnp.where(inside, size.astype(F32), extent)
        start = start + size
    angle = 0.5 * math.pi * offset / extent
    return seg, jnp.cos(angle), jnp.sin(angle)


def pair_mask(lengths, rows):
    seg_i, cos_i, sin_i = segment_of(lengths, lax.broadcasted_iota(jnp.int32, (1, rows), 1))
    seg_j, cos_j, sin_j = segment_of(lengths, lax.broadcasted_iota(jnp.int32, (rows, 1), 0))
    same = (seg_i == seg_j) & (seg_i >= 0)
    dead = jnp.where(seg_i >= 0, 0.0, 1.0)
    return jnp.where(same, cos_j * cos_i + sin_j * sin_i, 0.0), dead


def softplus(v):
    return jnp.maximum(v, 0.0) + jnp.log1p(jnp.exp(-jnp.abs(v)))


def attend_forward(
    lengths, me, x_ref, so, z0, z1, z2, z3, sp, y0, y1, y2, y3,
    mix, att, den, rel_own, rel_par,
):
    rows = x_ref.shape[0]
    width = x_ref.shape[1]
    chip, core = me[0], me[1]
    x = x_ref[...]
    sides = ((False, (so, z0, z1, z2, z3), rel_own), (True, (sp, y0, y1, y2, y3), rel_par))
    for other, refs, _ in sides:
        for (base, size), ref in zip(PIECES, refs):
            got = nt(ref[...], x)
            for at, plane, step in PLACES:
                if base <= at < base + size:
                    d = shard_index(chip, core, plane, step, other)
                    mix[pl.ds(pl.multiple_of(QKV * d, 8), QKV), :] = got[
                        at - base : at - base + QKV
                    ]
    mask, dead = pair_mask(lengths, rows)
    for h in range(width // DH):
        here = slice(DH * h, DH * h + DH)
        fq = softplus(mix[here, :]).astype(BF)
        fk = softplus(mix[width + DH * h : width + DH * h + DH, :]).astype(BF)
        v = mix[2 * width + DH * h : 2 * width + DH * h + DH, :].astype(BF)
        pairs = tn(fk, fq) * mask
        total = jnp.sum(pairs, axis=0, keepdims=True) + dead
        den[h : h + 1, :] = total
        att[here, :] = nn(v, pairs.astype(BF)) / total
    side = QKV // 3
    blank = jnp.zeros((QKV, rows), F32)
    for other, _, rel in sides:
        for at, plane, step in PLACES:
            d = shard_index(chip, core, plane, step, other)
            part = att[pl.ds(pl.multiple_of(side * d, 8), side), :]
            rel[at : at + BLOCK, :] = jnp.concatenate([blank, part], axis=0).astype(BF)


def attend_close(
    x_ref, rel_own, rel_par, so, z0, z1, z2, z3, sp, y0, y1, y2, y3, norms,
    first, first_low, xhat, rstd,
):
    branch = x_ref[...].astype(F32)
    for refs, rel in (((so, z0, z1, z2, z3), rel_own), ((sp, y0, y1, y2, y3), rel_par)):
        for (base, size), ref in zip(PIECES, refs):
            branch = branch + tn(rel[base : base + size, :], ref[...])
    centered = branch - jnp.mean(branch, axis=-1, keepdims=True)
    spread = jnp.mean(centered * centered, axis=-1, keepdims=True)
    scale = lax.rsqrt(spread + 1e-05)
    hat = centered * scale
    xhat[...] = hat
    rstd[...] = scale
    out = hat * norms[0:1, :] + norms[1:2, :]
    first[...] = out
    first_low[...] = out.astype(BF)


GELU_A = math.sqrt(2.0 / math.pi)
GELU_B = 0.044715


def feed_up(ya, yb, s, z0, z1, z2, z3, hid, slope):
    rows = ya.shape[0]
    for half, y in ((0, ya), (1, yb)):
        cols = slice(half * rows, half * rows + rows)
        for (base, size), ref in zip(PIECES, (s, z0, z1, z2, z3)):
            u = nt(ref[...], y[...])
            sq = u * u
            t = jnp.tanh(GELU_A * u * (1.0 + GELU_B * sq))
            half_up = 0.5 * (1.0 + t)
            hid[base : base + size, cols] = (u * half_up).astype(BF)
            slope[base : base + size, cols] = half_up + 0.5 * u * (1.0 - t * t) * (
                GELU_A * (1.0 + 3.0 * GELU_B * sq)
            )


def down_away(hid, s, z0, z1, z2, z3, other, whole):
    for (base, size), ref in zip(PIECES, (s, z0, z1, z2, z3)):
        whole[base : base + size, :] = ref[...]
    rows = other.shape[0]
    other[...] = tn(hid[:, rows : 2 * rows], whole[...])


def down_here(hid, whole, own):
    own[...] = tn(hid[:, 0 : own.shape[0]], whole[...])


def norm_back(dy, gain, hat, scale):
    dhat = dy * gain
    return scale * (
        dhat
        - jnp.mean(dhat, axis=-1, keepdims=True)
        - hat * jnp.mean(dhat * hat, axis=-1, keepdims=True)
    )


def live_rows(lengths, rows):
    used = jnp.int32(0)
    for s in range(5):
        used = used + lengths[0, s]
    return jnp.where(lax.broadcasted_iota(jnp.int32, (rows, 1), 0) < used, 1.0, 0.0)


def turn_round(lengths, first, own, got, cot, norms, ds2, dz, xhat):
    h = first[...] + (own[...] + got[...])
    centered = h - jnp.mean(h, axis=-1, keepdims=True)
    spread = jnp.mean(centered * centered, axis=-1, keepdims=True)
    scale = lax.rsqrt(spread + 1e-05)
    hat = centered * scale
    xhat[...] = hat
    dy = cot[...].astype(F32) * live_rows(lengths, first.shape[0])
    back = norm_back(dy, norms[2:3, :], hat, scale)
    ds2[...] = back
    dz[...] = back.astype(BF)


def finish_forward(lengths, xhat, cot, norms, out, terms):
    live = live_rows(lengths, xhat.shape[0])
    hat = xhat[...]
    out[...] = ((hat * norms[2:3, :] + norms[3:4, :]) * live).astype(BF)
    dy = cot[...].astype(F32) * live
    terms[0:1, :] = jnp.sum(dy * hat, axis=0, keepdims=True)
    terms[1:2, :] = jnp.sum(dy, axis=0, keepdims=True)


def rows_away(get, send):
    near = get(slice(2 * BLOCK, PLANE)).astype(BF)
    far = get(slice(PLANE + 2 * ZROWS, HALF)).astype(BF)
    for p in range(2):
        send[PLANE * p : PLANE * p + BLOCK, :] = near[BLOCK * p : BLOCK * p + BLOCK]
        send[PLANE * p + BLOCK : PLANE * p + PLANE, :] = far[ZROWS * p : ZROWS * p + ZROWS]


def rows_here(get, turn, own):
    near = get(slice(0, 2 * BLOCK))
    far = get(slice(PLANE, PLANE + 2 * ZROWS))
    for p, ref in enumerate((own, turn)):
        ref[0:BLOCK, :] = near[BLOCK * p : BLOCK * p + BLOCK]
        ref[BLOCK:PLANE, :] = far[ZROWS * p : ZROWS * p + ZROWS]


def two_cores(hid, za, zb):
    rows = za.shape[0]
    return lambda here: nn(hid[here, 0:rows], za[...]) + nn(
        hid[here, rows : 2 * rows], zb[...]
    )


def grad_away(hid, za, zb, send):
    rows_away(two_cores(hid, za, zb), send)


def grad_here(hid, za, zb, turn, own):
    rows_here(two_cores(hid, za, zb), turn, own)


def feed_back(
    slope, za, zb, d, s, z0, z1, z2, z3, dup, mine, other, whole,
):
    rows = za.shape[0]
    for base, size in PIECES:
        here = slice(base, base + size)
        w = d[here, :]
        dup[here, 0:rows] = (nt(w, za[...]) * slope[here, 0:rows]).astype(BF)
        dup[here, rows:] = (nt(w, zb[...]) * slope[here, rows:]).astype(BF)
    for (base, size), ref in zip(PIECES, (s, z0, z1, z2, z3)):
        whole[base : base + size, :] = ref[...]
    w = whole[...]
    other[...] = tn(dup[:, rows : 2 * rows], w)
    mine[...] = tn(dup[:, 0:rows], w)


def attend_backward(
    lengths, me, ds2, mine, got, xhat, rstd, norms, mix, att, den,
    so, z0, z1, z2, z3, sp, y0, y1, y2, y3,
    dh_ref, do_ref, terms, rel_own, rel_par, datt, dmix,
):
    rows, width = ds2.shape
    chip, core = me[0], me[1]
    dy1 = ds2[...] + (mine[...] + got[...])
    hat = xhat[...]
    terms[0:1, :] = jnp.sum(dy1 * hat, axis=0, keepdims=True)
    terms[1:2, :] = jnp.sum(dy1, axis=0, keepdims=True)
    dh = norm_back(dy1, norms[0:1, :], hat, rstd[...])
    dh_ref[...] = dh
    do = dh.astype(BF)
    do_ref[...] = do
    side = QKV // 3
    sides = ((False, (so, z0, z1, z2, z3), rel_own), (True, (sp, y0, y1, y2, y3), rel_par))
    for other, refs, _ in sides:
        for (base, size), ref in zip(PIECES, refs):
            got_t = nt(ref[...], do)
            for at, plane, step in PLACES:
                if base <= at < base + size:
                    d = shard_index(chip, core, plane, step, other)
                    datt[pl.ds(pl.multiple_of(side * d, 8), side), :] = got_t[
                        at - base + QKV : at - base + BLOCK
                    ]
    mask, _ = pair_mask(lengths, rows)
    for h in range(width // DH):
        here = slice(DH * h, DH * h + DH)
        q = mix[here, :]
        k = mix[width + DH * h : width + DH * h + DH, :]
        v = mix[2 * width + DH * h : 2 * width + DH * h + DH, :].astype(BF)
        fq = softplus(q).astype(BF)
        fk = softplus(k).astype(BF)
        pairs = (tn(fk, fq) * mask).astype(BF)
        da = datt[here, :]
        total = den[h : h + 1, :]
        dnum = da / total
        dden = -jnp.sum(dnum * att[here, :], axis=0, keepdims=True)
        dnum = dnum.astype(BF)
        dpairs = ((tn(v, dnum) + dden) * mask).astype(BF)
        dmix[2 * width + DH * h : 2 * width + DH * h + DH, :] = nt(dnum, pairs)
        dmix[width + DH * h : width + DH * h + DH, :] = nt(fq, dpairs) * jax.nn.sigmoid(k)
        dmix[here, :] = nn(fk, dpairs) * jax.nn.sigmoid(q)
    blank = jnp.zeros((BLOCK - QKV, rows), F32)
    for other, _, rel in sides:
        for at, plane, step in PLACES:
            d = shard_index(chip, core, plane, step, other)
            part = dmix[pl.ds(pl.multiple_of(QKV * d, 8), QKV), :]
            rel[at : at + BLOCK, :] = jnp.concatenate([part, blank], axis=0).astype(BF)


def four_terms(dma, dmb, xa, xb, ata, atb, doa, dob):
    return lambda here: (nn(dma[here, :], xa[...]) + nn(dmb[here, :], xb[...])) + (
        nn(ata[here, :], doa[...]) + nn(atb[here, :], dob[...])
    )


def mix_away(dma, dmb, xa, xb, ata, atb, doa, dob, send):
    rows_away(four_terms(dma, dmb, xa, xb, ata, atb, doa, dob), send)


def mix_here(dma, dmb, xa, xb, ata, atb, doa, dob, turn, own):
    rows_here(four_terms(dma, dmb, xa, xb, ata, atb, doa, dob), turn, own)


def grad_input(dh, rel_own, rel_par, so, z0, z1, z2, z3, sp, y0, y1, y2, y3, out):
    total = dh[...]
    for refs, rel in (((so, z0, z1, z2, z3), rel_own), ((sp, y0, y1, y2, y3), rel_par)):
        for (base, size), ref in zip(PIECES, refs):
            total = total + tn(rel[base : base + size, :], ref[...])
    out[...] = total


def close_sums(k1, a1, b1, c1, g2, g3, t1, t2, g1, note):
    s1 = (k1[...] + a1[...].astype(F32)) + (b1[...].astype(F32) + c1[...].astype(F32))
    g1[...] = s1
    sq = s1 * s1 + g2[...] * g2[...] + g3[...] * g3[...]
    note[0:2, :] = t1[...]
    note[2:4, :] = t2[...]
    note[4:5, :] = jnp.sum(sq, axis=0, keepdims=True)
    note[5:8, :] = jnp.zeros((3, note.shape[1]), F32)


def update(
    n0, n1, n2, n3, g1, g2, g3, mw, ow, uw, dw, nw, mm, om, um, dm, nm, mv, ov, uv, dv, nv,
    norm_out, mw2, ow2, uw2, dw2, nw2, mm2, om2, um2, dm2, nm2, mv2, ov2, uv2, dv2, nv2,
):
    note = (n0[...] + n1[...]) + (n2[...] + n3[...])
    terms = note[0:4, :]
    total = jnp.sum(note[4:5, :]) + jnp.sum(terms * terms)
    norm = jnp.sqrt(jnp.full((1, 1), total, F32))
    norm_out[...] = norm
    scale = 1.0 / jnp.maximum(norm, 1.0)

    one = g1[...]
    grads = (one[0:QKV], one[QKV:BLOCK], g2[...], g3[...], terms)
    groups = (
        (mw, mm, mv, mw2, mm2, mv2),
        (ow, om, ov, ow2, om2, ov2),
        (uw, um, uv, uw2, um2, uv2),
        (dw, dm, dv, dw2, dm2, dv2),
        (nw, nm, nv, nw2, nm2, nv2),
    )
    for g, (w, m, v, w2, m2, v2), rate, decay in zip(grads, groups, RATES, DECAYS):
        new_w, new_m, new_v = adamw(w[...], scale * g, m[...], v[...], rate, decay)
        w2[...] = new_w
        m2[...] = new_m
        v2[...] = new_v


def tie(value, *others):
    return lax.optimization_barrier((value,) + others)[0]


def swap(value):
    return lax.ppermute(value, "fsdp", [(0, 1), (1, 0)])


def hop_first(value):
    return lax.ppermute(value, AXES, [(i, i ^ (4 if i % 2 else 2)) for i in range(2 * CHIPS)])


def hop_second(value):
    return lax.ppermute(value, AXES, [(i, i ^ (2 if i % 2 else 4)) for i in range(2 * CHIPS)])


def hop_z(value, step):
    return lax.ppermute(value, "dp", [(i, i ^ step) for i in range(CHIPS)])


def add_first(turn, got):
    return (turn + got[PLANE:].astype(F32)).astype(BF)


def add_second(own, got, back):
    total = own + got[:PLANE].astype(F32) + back.astype(F32)
    return total[:BLOCK], total.astype(BF)


def send_z(low):
    return [
        hop_z(low[BLOCK * (j + 1) : BLOCK * (j + 2)], step) for j, step in enumerate(STEPS_Z)
    ]


def tuned_device(
    tokens, cotangent, lengths,
    mix_weight, out_weight, up_weight, down_weight, norm_params,
    mix_first, out_first, up_first, down_first, norm_first,
    mix_second, out_second, up_second, down_second, norm_second,
):
    rows, width = tokens.shape
    chip, core = lax.axis_index("dp"), lax.axis_index("fsdp")
    me = jnp.stack([chip, core]).astype(jnp.int32)
    wide = 3 * width

    blocks = [
        jnp.concatenate([mix_weight.T.astype(BF), out_weight.astype(BF)], axis=0),
        up_weight.T.astype(BF),
        down_weight.astype(BF),
    ]
    s_all = jnp.concatenate(blocks, axis=0)
    def wide_join(*parts):
        return jnp.concatenate(parts, axis=0)

    def z_round(block, direct, before):
        if direct:
            got = [hop_z(tie(block, *before), step) for step in STEPS_Z]
            return got, wide_join(*got)
        far = hop_z(tie(block, *before), 8)
        near = hop_z(wide_join(block, far), 4)
        return [far, near], wide_join(far, near)

    s_first = hop_first(s_all)
    s_second = hop_second(s_all)
    near1, joined1 = z_round(blocks[0], True, ())
    near2, joined2 = z_round(blocks[1], False, (near1[2],))
    near3, joined3 = z_round(blocks[2], False, (near2[0],))
    s_third = hop_second(s_first)
    s_parts = (s_all, s_first, s_second, s_third)
    turned1 = hop_first(tie(joined1, s_first, s_second))
    across1 = hop_second(tie(joined1, s_second))
    corner1 = hop_second(tie(turned1, s_third))
    turned2 = hop_first(tie(joined2, turned1, across1))
    across2 = hop_second(tie(joined2, across1))
    corner2 = hop_second(tie(turned2, corner1, across2))
    sorted1, sorted2, sorted3 = call(
        sort_near,
        [((PLANE, width), BF)] * 3,
        s_parts,
    )
    up_all = (sorted2, joined2, turned2, across2, corner2)
    attn_own = (sorted1, joined1, turned1, across1, corner1)
    attn_par = tuple(swap(p) for p in attn_own)
    x_par = swap(tokens)

    mix, att, den, at_own, at_par = call(
        attend_forward,
        [
            ((wide, rows), F32), ((width, rows), F32), ((16, rows), F32),
            ((HALF, rows), BF), ((HALF, rows), BF),
        ],
        (lengths, me, tie(tokens, x_par)) + attn_own + attn_par,
        smem=2,
    )
    turned3 = hop_first(tie(joined3, turned2))
    across3 = hop_second(tie(joined3, across2, den))
    first, first_low, xhat, rstd = call(
        attend_close,
        [((rows, width), F32), ((rows, width), BF), ((rows, width), F32), ((rows, 1), F32)],
        (tokens, at_own, at_par) + attn_own + attn_par + (norm_params,),
    )
    corner3 = hop_second(tie(turned3, corner2, first_low))
    down_all = (sorted3, joined3, turned3, across3, corner3)
    at_got = swap(at_par)
    first_par = swap(first_low)
    hid, slope = call(
        feed_up,
        [((HALF, 2 * rows), BF), ((HALF, 2 * rows), F32)],
        (first_low, tie(first_par, at_got)) + up_all,
    )
    down_par, down_full = call(
        down_away, [((rows, width), F32), ((HALF, width), BF)], (hid,) + down_all
    )
    down_got = swap(down_par)
    (down_own,) = call(down_here, [((rows, width), F32)], (tie(hid, down_par), down_full))
    ds2, dz, xhat_two = call(
        turn_round,
        [((rows, width), F32), ((rows, width), BF), ((rows, width), F32)],
        (lengths, first, down_own, down_got, cotangent, norm_params),
        smem=1,
    )
    dz_par = swap(dz)
    output, terms_two = call(
        finish_forward,
        [((rows, width), BF), ((2, width), F32)],
        (lengths, xhat_two, cotangent, norm_params),
        smem=1,
    )
    away = [((2 * PLANE, width), BF)]
    stay = [((PLANE, width), F32)] * 2
    (send3,) = call(grad_away, away, (hid, dz, dz_par), name="grad_down_away")
    got3 = hop_second(send3)
    dup, dy_own, dy_par = call(
        feed_back,
        [((HALF, 2 * rows), BF)] + [((rows, width), F32)] * 2,
        (slope, tie(dz, send3, terms_two), dz_par, down_full) + up_all,
        scratch=[pltpu.VMEM((HALF, width), BF)],
    )
    (send2,) = call(grad_away, away, (dup, first_low, first_par), name="grad_up_away")
    got2 = hop_second(send2)
    dh, do, terms_one, dm_own, dm_par = call(
        attend_backward,
        [
            ((rows, width), F32), ((rows, width), BF), ((2, width), F32),
            ((HALF, rows), BF), ((HALF, rows), BF),
        ],
        (
            lengths, me, ds2, dy_own, swap(dy_par), xhat, rstd,
            norm_params, mix, att, den,
        ) + attn_own + attn_par,
        scratch=[pltpu.VMEM((width, rows), F32), pltpu.VMEM((wide, rows), F32)],
        smem=2,
    )
    turn3, own3 = call(
        grad_here, stay, (hid, dz, dz_par), name="grad_down_here"
    )
    turn2, own2 = call(
        grad_here, stay, (dup, first_low, first_par),
        name="grad_up_here",
    )
    low_turn3 = add_first(turn3, got3)
    back3 = hop_first(low_turn3)
    low_turn2 = add_first(turn2, got2)
    back2 = hop_first(low_turn2)
    factors = (
        dm_own, swap(dm_par), tokens, x_par, at_own, at_got,
        do, swap(do),
    )
    (send1,) = call(mix_away, away, factors)
    keep3, low3 = add_second(own3, got3, back3)
    parts3 = send_z(low3)
    got1 = hop_second(tie(send1, back3))
    turn1, own1 = call(mix_here, stay, (tie(dm_own, send1),) + factors[1:])
    (grad_tokens,) = call(
        grad_input,
        [((rows, width), F32)],
        (tie(dh, send1), dm_own, dm_par) + attn_own + attn_par,
    )
    keep2, low2 = add_second(own2, got2, back2)
    parts2 = send_z(tie(low2, parts3[1]))
    back1 = hop_first(add_first(tie(turn1, grad_tokens), got1))
    keep1, low1 = add_second(own1, got1, back1)
    parts1 = send_z(tie(low1, parts2[1]))
    g3 = (keep3 + parts3[0]) + (parts3[1].astype(F32) + parts3[2].astype(F32))
    g2 = (keep2 + parts2[0]) + (parts2[1].astype(F32) + parts2[2].astype(F32))
    g1, note = call(
        close_sums,
        [((BLOCK, width), F32), ((8, width), F32)],
        (keep1,) + tuple(parts1) + (g2, g3, terms_one, terms_two),
    )
    note = note + swap(note)
    note = (note + hop_z(note, 1)) + (hop_z(note, 2) + hop_z(note, 3))
    notes = (note, hop_z(note, 4), hop_z(note, 8), hop_z(note, 12))
    shapes = [
        (mix_weight.shape[::-1], F32), (out_weight.shape, F32), (up_weight.shape[::-1], F32),
        (down_weight.shape, F32), (norm_params.shape, F32),
    ]
    norm, *news = call(
        update,
        [((1, 1), F32)] + shapes * 3,
        notes + (
            g1, g2, g3, mix_weight.T, out_weight, up_weight.T, down_weight, norm_params,
            mix_first.T, out_first, up_first.T, down_first, norm_first,
            mix_second.T, out_second, up_second.T, down_second, norm_second,
        ),
    )
    for at in (0, 2, 5, 7, 10, 12):
        news[at] = news[at].T
    return (output, grad_tokens, norm.reshape(())) + tuple(news)


def solution(mesh):
    in_specs = (
        P(("dp", "fsdp"), None),
        P(("dp", "fsdp"), None),
        P(("dp", "fsdp"), None),
        P(None, ("dp", "fsdp")),
        P(("dp", "fsdp"), None),
        P(None, ("dp", "fsdp")),
        P(("dp", "fsdp"), None),
        P(),
        P(None, ("dp", "fsdp")),
        P(("dp", "fsdp"), None),
        P(None, ("dp", "fsdp")),
        P(("dp", "fsdp"), None),
        P(),
        P(None, ("dp", "fsdp")),
        P(("dp", "fsdp"), None),
        P(None, ("dp", "fsdp")),
        P(("dp", "fsdp"), None),
        P(),
    )
    out_specs = (
        P(("dp", "fsdp"), None),
        P(("dp", "fsdp"), None),
        P(),
        P(None, ("dp", "fsdp")),
        P(("dp", "fsdp"), None),
        P(None, ("dp", "fsdp")),
        P(("dp", "fsdp"), None),
        P(),
        P(None, ("dp", "fsdp")),
        P(("dp", "fsdp"), None),
        P(None, ("dp", "fsdp")),
        P(("dp", "fsdp"), None),
        P(),
        P(None, ("dp", "fsdp")),
        P(("dp", "fsdp"), None),
        P(None, ("dp", "fsdp")),
        P(("dp", "fsdp"), None),
        P(),
    )
    sizes = dict(mesh.shape)
    tuned = sizes["dp"] == CHIPS and sizes["fsdp"] == 2
    return jax.shard_map(
        tuned_device if tuned else on_device, mesh=mesh, in_specs=in_specs, out_specs=out_specs, check_vma=False
    )
```

```python
import math

import jax
import jax.numpy as jnp
from jax import lax
from jax.experimental import pallas as pl
from jax.experimental.pallas import tpu as pltpu
from jax.sharding import PartitionSpec as P

DH = 64
STEP = 10


HIGH = lax.Precision.HIGHEST
RATES = (0.01, 0.08, 0.01, 0.01, 0.2)
DECAYS = (0.1, 0.1, 0.1, 0.1, 0.0)


def segment_tables(lengths, rows):
    ends = jnp.cumsum(lengths)
    starts = ends - lengths
    places = jnp.arange(rows, dtype=jnp.int32)
    inside = (places[None, :] >= starts[:, None]) & (places[None, :] < ends[:, None])
    member = inside[:-1].astype(jnp.float32)
    live = jnp.sum(member, axis=0)
    offset = places.astype(jnp.float32) - jnp.sum(
        member * starts[:-1, None].astype(jnp.float32), axis=0
    )
    extent = jnp.sum(member * lengths[:-1, None].astype(jnp.float32), axis=0) + (1.0 - live)
    angle = 0.5 * math.pi * offset / extent
    return (member, live, angle)


def cos_attention(queries, keys, values, member, live, angle):
    rows = queries.shape[0]
    feat_q = jax.nn.softplus(queries).reshape(rows, -1, DH)
    feat_k = jax.nn.softplus(keys).reshape(rows, -1, DH)
    vals = values.reshape(rows, -1, DH)
    phases = jnp.stack([jnp.cos(angle), jnp.sin(angle)])
    weighted = member[None] * phases[:, None, :]
    scaled = jnp.einsum("psr,rhd->psrhd", weighted, feat_k)
    state = jnp.einsum("psrhd,rhe->pshde", scaled, vals, precision=HIGH)
    normal = jnp.sum(scaled, axis=2)
    query_side = feat_q[None] * phases[:, :, None, None]
    per_slot = jnp.einsum("prhd,pshde->rshe", query_side, state, precision=HIGH)
    numer = jnp.einsum("sr,rshe->rhe", member, per_slot, precision=HIGH)
    slot_den = jnp.einsum("prhd,pshd->rsh", query_side, normal, precision=HIGH)
    denom = jnp.einsum("sr,rsh->rh", member, slot_den, precision=HIGH) + (1.0 - live)[:, None]
    return (numer / denom[:, :, None]).reshape(rows, -1)


def layer_norm(hidden, gain, shift):
    centered = hidden - jnp.mean(hidden, axis=-1, keepdims=True)
    spread = jnp.mean(centered * centered, axis=-1, keepdims=True)
    return centered * lax.rsqrt(spread + 1e-05) * gain + shift


def gelu_tanh(values):
    return jax.nn.gelu(values, approximate=True)


def inner_rows(left, right):
    return lax.dot_general(
        left, right, (((0,), (0,)), ((), ())), preferred_element_type=jnp.float32
    )


def times_transpose(left, right):
    return lax.dot_general(
        left, right, (((1,), (1,)), ((), ())), preferred_element_type=jnp.float32
    )


def by_owner_rows(grad, owners):
    return grad.reshape(owners, -1, 128)


def by_owner_columns(grad, owners):
    height, across = grad.shape
    split = grad.reshape(height, owners, across // owners)
    return jnp.transpose(split, (1, 0, 2)).reshape(owners, -1, 128)


def unpack_owned(packed, shapes):
    pieces = []
    offset = 0
    for shape in shapes:
        blocks = shape[0] * shape[1] // 128
        pieces.append(packed[0, offset : offset + blocks].reshape(shape))
        offset = offset + blocks
    return pieces


def adamw(weight, grad, first, second, rate, decay):
    first_new = 0.9 * first + 0.1 * grad
    second_new = 0.95 * second + 0.05 * grad * grad
    step_dir = first_new / (1.0 - 0.9**STEP) / (jnp.sqrt(second_new / (1.0 - 0.95**STEP)) + 1e-08)
    return (weight - rate * (step_dir + decay * weight), first_new, second_new)


def on_device(
    tokens,
    cotangent,
    lengths,
    mix_weight,
    out_weight,
    up_weight,
    down_weight,
    norm_params,
    mix_first,
    out_first,
    up_first,
    down_first,
    norm_first,
    mix_second,
    out_second,
    up_second,
    down_second,
    norm_second,
):
    rows, width = tokens.shape
    owners = lax.axis_size(("dp", "fsdp"))
    rounded = (
        mix_weight.astype(jnp.bfloat16),
        out_weight.astype(jnp.bfloat16),
        up_weight.astype(jnp.bfloat16),
        down_weight.astype(jnp.bfloat16),
    )
    mix_full, out_full, up_full, down_full = (
        lax.all_gather(rounded[0], ("dp", "fsdp"), axis=1, tiled=True),
        lax.all_gather(rounded[1], ("dp", "fsdp"), axis=0, tiled=True),
        lax.all_gather(rounded[2], ("dp", "fsdp"), axis=1, tiled=True),
        lax.all_gather(rounded[3], ("dp", "fsdp"), axis=0, tiled=True),
    )
    member, live, angle = segment_tables(lengths[0], rows)
    mixed = jnp.dot(tokens, mix_full, preferred_element_type=jnp.float32)

    def attend(queries, keys, values):
        return cos_attention(queries, keys, values, member, live, angle)

    attended, attention_pull = jax.vjp(
        attend, mixed[:, :width], mixed[:, width : 2 * width], mixed[:, 2 * width :]
    )
    attended_low = attended.astype(jnp.bfloat16)
    branch = jnp.dot(attended_low, out_full, preferred_element_type=jnp.float32)
    first, first_pull = jax.vjp(
        layer_norm, tokens.astype(jnp.float32) + branch, norm_params[0], norm_params[1]
    )
    first_low = first.astype(jnp.bfloat16)
    upper = jnp.dot(first_low, up_full, preferred_element_type=jnp.float32)
    hidden, gelu_pull = jax.vjp(gelu_tanh, upper)
    hidden_low = hidden.astype(jnp.bfloat16)
    second = jnp.dot(hidden_low, down_full, preferred_element_type=jnp.float32)
    final, final_pull = jax.vjp(layer_norm, first + second, norm_params[2], norm_params[3])
    output = (final * live[:, None]).astype(jnp.bfloat16)
    mix_full, out_full, up_full, down_full = (
        lax.all_gather(rounded[0], ("dp", "fsdp"), axis=1, tiled=True),
        lax.all_gather(rounded[1], ("dp", "fsdp"), axis=0, tiled=True),
        lax.all_gather(rounded[2], ("dp", "fsdp"), axis=1, tiled=True),
        lax.all_gather(rounded[3], ("dp", "fsdp"), axis=0, tiled=True),
    )
    grad_final = cotangent.astype(jnp.float32) * live[:, None]
    grad_sum_two, grad_gain_two, grad_bias_two = final_pull(grad_final)
    grad_second = grad_sum_two.astype(jnp.bfloat16)
    grad_down = inner_rows(hidden_low, grad_second)
    grad_hidden = times_transpose(grad_second, down_full)
    (grad_upper,) = gelu_pull(grad_hidden)
    grad_upper_low = grad_upper.astype(jnp.bfloat16)
    grad_up = inner_rows(first_low, grad_upper_low)
    grad_first = grad_sum_two + times_transpose(grad_upper_low, up_full)
    grad_sum_one, grad_gain_one, grad_bias_one = first_pull(grad_first)
    grad_branch = grad_sum_one.astype(jnp.bfloat16)
    grad_out = inner_rows(attended_low, grad_branch)
    grad_attended = times_transpose(grad_branch, out_full)
    grad_q, grad_k, grad_v = attention_pull(grad_attended)
    grad_mixed = jnp.concatenate([grad_q, grad_k, grad_v], axis=1).astype(jnp.bfloat16)
    grad_mix = inner_rows(tokens, grad_mixed)
    grad_tokens = grad_sum_one + times_transpose(grad_mixed, mix_full)
    norm_terms = jnp.stack([grad_gain_one, grad_bias_one, grad_gain_two, grad_bias_two])
    norm_grad = lax.psum(norm_terms, ("dp", "fsdp"))
    packed_all = jnp.concatenate(
        [
            by_owner_columns(grad_mix, owners),
            by_owner_rows(grad_out, owners),
            by_owner_columns(grad_up, owners),
            by_owner_rows(grad_down, owners),
        ],
        axis=1,
    )
    summed_all = lax.psum_scatter(packed_all, ("dp", "fsdp"), scatter_dimension=0, tiled=True)
    owned = tuple(
        unpack_owned(
            summed_all, (mix_weight.shape, out_weight.shape, up_weight.shape, down_weight.shape)
        )
    )
    local_sq = sum((jnp.sum(g * g) for g in owned))
    owned_sq = lax.psum(local_sq, ("dp", "fsdp"))
    global_norm = jnp.sqrt(owned_sq + jnp.sum(norm_grad * norm_grad))
    scale = 1.0 / jnp.maximum(global_norm, 1.0)
    params = (mix_weight, out_weight, up_weight, down_weight, norm_params)
    grads = (owned[0], owned[1], owned[2], owned[3], norm_grad)
    firsts = (mix_first, out_first, up_first, down_first, norm_first)
    seconds = (mix_second, out_second, up_second, down_second, norm_second)
    news = []
    for index in range(5):
        news.append(
            adamw(
                params[index],
                scale * grads[index],
                firsts[index],
                seconds[index],
                RATES[index],
                DECAYS[index],
            )
        )
    return (
        output,
        grad_tokens,
        global_norm,
        news[0][0],
        news[1][0],
        news[2][0],
        news[3][0],
        news[4][0],
        news[0][1],
        news[1][1],
        news[2][1],
        news[3][1],
        news[4][1],
        news[0][2],
        news[1][2],
        news[2][2],
        news[3][2],
        news[4][2],
    )


BF = jnp.bfloat16
F32 = jnp.float32
AXES = ("dp", "fsdp")
COST = 1000000000.0
MICROS = {
    "sort_near": 0.1,
    "attend_forward": 0.65,
    "attend_close": 0.36,
    "feed_up": 0.25,
    "down_away": 0.1,
    "down_here": 0.0,
    "turn_round": 0.0,
    "finish_forward": 0.0,
    "grad_down_away": 0.0,
    "grad_down_here": 0.0,
    "grad_up": 0.0,
    "attend_backward": 0.0,
    "grad_input": 0.0,
    "close_sums": 0.0,
    "update": 0.0,
    "grad_up_away": 0.0,
    "grad_up_here": 0.8,
    "feed_back": 1.0,
    "mix_away": 0.4,
    "mix_here": 1.5,
}
MB = 16
CHIPS = 16
BLOCK = 96
QKV = 72
PLANE = 4 * BLOCK
ZROWS = 3 * BLOCK
HALF = CHIPS * BLOCK
STEPS_Z = (8, 4, 12)


def nt(left, right):
    return lax.dot_general(
        left, right, (((1,), (1,)), ((), ())), preferred_element_type=F32
    )


def tn(left, right):
    return lax.dot_general(
        left, right, (((0,), (0,)), ((), ())), preferred_element_type=F32
    )


def nn(left, right):
    return jnp.dot(left, right, preferred_element_type=F32)


def block_places():
    places = [(BLOCK * p, p, 0) for p in range(4)]
    for p in range(4):
        for j, step in enumerate(STEPS_Z):
            places.append((PLANE + ZROWS * p + BLOCK * j, p, step))
    return places


PLACES = block_places()
PIECES = [(0, PLANE)] + [(PLANE + ZROWS * p, ZROWS) for p in range(4)]


def shard_index(chip, core, plane, step, other):
    owner = 1 - core if other else core
    first = 1 + owner
    mask = (0, first, 3 - first, 3)[plane]
    return 2 * (chip ^ mask ^ step) + owner


def call(body, outs, args, scratch=(), smem=0, place=pltpu.VMEM, name=None):
    name = name or body.__name__
    held = [math.prod(s.shape) * 4 for s in scratch]
    limit = int(sum(held) + (MB << 20))
    in_specs = [
        pl.BlockSpec(memory_space=pltpu.SMEM if i < smem else place)
        for i in range(len(args))
    ]
    return pl.pallas_call(
        body,
        out_shape=[jax.ShapeDtypeStruct(s, t) for s, t in outs],
        in_specs=in_specs,
        out_specs=[pl.BlockSpec(memory_space=pltpu.VMEM) for _ in outs],
        scratch_shapes=list(scratch),
        compiler_params=pltpu.CompilerParams(vmem_limit_bytes=limit),
        cost_estimate=pl.CostEstimate(
            flops=int(MICROS[name] * COST), bytes_accessed=0, transcendentals=0
        ),
        name=name,
    )(*args)


def sort_near(s0, s1, s2, s3, *groups):
    for g, out in enumerate(groups):
        for p, (ref, base) in enumerate(((s0, 0), (s1, 0), (s2, 0), (s3, 0))):
            at = base + BLOCK * g
            out[BLOCK * p : BLOCK * p + BLOCK, :] = ref[at : at + BLOCK, :]


def segment_of(lengths, place):
    start = jnp.int32(0)
    seg = jnp.full(place.shape, -1, jnp.int32)
    offset = jnp.zeros(place.shape, F32)
    extent = jnp.ones(place.shape, F32)
    for s in range(5):
        size = lengths[0, s]
        inside = (place >= start) & (place < start + size)
        seg = jnp.where(inside, s, seg)
        offset = jnp.where(inside, (place - start).astype(F32), offset)
        extent = jnp.where(inside, size.astype(F32), extent)
        start = start + size
    angle = 0.5 * math.pi * offset / extent
    return seg, jnp.cos(angle), jnp.sin(angle)


def pair_mask(lengths, rows):
    seg_i, cos_i, sin_i = segment_of(lengths, lax.broadcasted_iota(jnp.int32, (1, rows), 1))
    seg_j, cos_j, sin_j = segment_of(lengths, lax.broadcasted_iota(jnp.int32, (rows, 1), 0))
    same = (seg_i == seg_j) & (seg_i >= 0)
    dead = jnp.where(seg_i >= 0, 0.0, 1.0)
    return jnp.where(same, cos_j * cos_i + sin_j * sin_i, 0.0), dead


def softplus(v):
    return jnp.maximum(v, 0.0) + jnp.log1p(jnp.exp(-jnp.abs(v)))


def attend_forward(
    lengths, me, x_ref, so, z0, z1, z2, z3, sp, y0, y1, y2, y3,
    mix, att, den, rel_own, rel_par,
):
    rows = x_ref.shape[0]
    width = x_ref.shape[1]
    chip, core = me[0], me[1]
    x = x_ref[...]
    sides = ((False, (so, z0, z1, z2, z3), rel_own), (True, (sp, y0, y1, y2, y3), rel_par))
    for other, refs, _ in sides:
        for (base, size), ref in zip(PIECES, refs):
            got = nt(ref[...], x)
            for at, plane, step in PLACES:
                if base <= at < base + size:
                    d = shard_index(chip, core, plane, step, other)
                    mix[pl.ds(pl.multiple_of(QKV * d, 8), QKV), :] = got[
                        at - base : at - base + QKV
                    ]
    mask, dead = pair_mask(lengths, rows)
    for h in range(width // DH):
        here = slice(DH * h, DH * h + DH)
        fq = softplus(mix[here, :]).astype(BF)
        fk = softplus(mix[width + DH * h : width + DH * h + DH, :]).astype(BF)
        v = mix[2 * width + DH * h : 2 * width + DH * h + DH, :].astype(BF)
        pairs = tn(fk, fq) * mask
        total = jnp.sum(pairs, axis=0, keepdims=True) + dead
        den[h : h + 1, :] = total
        att[here, :] = nn(v, pairs.astype(BF)) / total
    side = QKV // 3
    blank = jnp.zeros((QKV, rows), F32)
    for other, _, rel in sides:
        for at, plane, step in PLACES:
            d = shard_index(chip, core, plane, step, other)
            part = att[pl.ds(pl.multiple_of(side * d, 8), side), :]
            rel[at : at + BLOCK, :] = jnp.concatenate([blank, part], axis=0).astype(BF)


def attend_close(
    x_ref, rel_own, rel_par, so, z0, z1, z2, z3, sp, y0, y1, y2, y3, norms,
    first, first_low, xhat, rstd,
):
    branch = x_ref[...].astype(F32)
    for refs, rel in (((so, z0, z1, z2, z3), rel_own), ((sp, y0, y1, y2, y3), rel_par)):
        for (base, size), ref in zip(PIECES, refs):
            branch = branch + tn(rel[base : base + size, :], ref[...])
    centered = branch - jnp.mean(branch, axis=-1, keepdims=True)
    spread = jnp.mean(centered * centered, axis=-1, keepdims=True)
    scale = lax.rsqrt(spread + 1e-05)
    hat = centered * scale
    xhat[...] = hat
    rstd[...] = scale
    out = hat * norms[0:1, :] + norms[1:2, :]
    first[...] = out
    first_low[...] = out.astype(BF)


GELU_A = math.sqrt(2.0 / math.pi)
GELU_B = 0.044715


def feed_up(ya, yb, s, z0, z1, z2, z3, hid, slope):
    rows = ya.shape[0]
    for half, y in ((0, ya), (1, yb)):
        cols = slice(half * rows, half * rows + rows)
        for (base, size), ref in zip(PIECES, (s, z0, z1, z2, z3)):
            u = nt(ref[...], y[...])
            sq = u * u
            t = jnp.tanh(GELU_A * u * (1.0 + GELU_B * sq))
            half_up = 0.5 * (1.0 + t)
            hid[base : base + size, cols] = (u * half_up).astype(BF)
            slope[base : base + size, cols] = half_up + 0.5 * u * (1.0 - t * t) * (
                GELU_A * (1.0 + 3.0 * GELU_B * sq)
            )


def down_away(hid, s, z0, z1, z2, z3, other, whole):
    for (base, size), ref in zip(PIECES, (s, z0, z1, z2, z3)):
        whole[base : base + size, :] = ref[...]
    rows = other.shape[0]
    other[...] = tn(hid[:, rows : 2 * rows], whole[...]).astype(other.dtype)


def down_here(hid, whole, own):
    own[...] = tn(hid[:, 0 : own.shape[0]], whole[...])


def norm_back(dy, gain, hat, scale):
    dhat = dy * gain
    return scale * (
        dhat
        - jnp.mean(dhat, axis=-1, keepdims=True)
        - hat * jnp.mean(dhat * hat, axis=-1, keepdims=True)
    )


def live_rows(lengths, rows):
    used = jnp.int32(0)
    for s in range(5):
        used = used + lengths[0, s]
    return jnp.where(lax.broadcasted_iota(jnp.int32, (rows, 1), 0) < used, 1.0, 0.0)


def turn_round(lengths, first, own, got, cot, norms, ds2, dz, xhat):
    h = first[...] + (own[...] + got[...].astype(F32))
    centered = h - jnp.mean(h, axis=-1, keepdims=True)
    spread = jnp.mean(centered * centered, axis=-1, keepdims=True)
    scale = lax.rsqrt(spread + 1e-05)
    hat = centered * scale
    xhat[...] = hat
    dy = cot[...].astype(F32) * live_rows(lengths, first.shape[0])
    back = norm_back(dy, norms[2:3, :], hat, scale)
    ds2[...] = back
    dz[...] = back.astype(BF)


def finish_forward(lengths, xhat, cot, norms, out, terms):
    live = live_rows(lengths, xhat.shape[0])
    hat = xhat[...]
    out[...] = ((hat * norms[2:3, :] + norms[3:4, :]) * live).astype(BF)
    dy = cot[...].astype(F32) * live
    terms[0:1, :] = jnp.sum(dy * hat, axis=0, keepdims=True)
    terms[1:2, :] = jnp.sum(dy, axis=0, keepdims=True)


def rows_away(get, send):
    near = get(slice(2 * BLOCK, PLANE)).astype(BF)
    far = get(slice(PLANE + 2 * ZROWS, HALF)).astype(BF)
    for p in range(2):
        send[PLANE * p : PLANE * p + BLOCK, :] = near[BLOCK * p : BLOCK * p + BLOCK]
        send[PLANE * p + BLOCK : PLANE * p + PLANE, :] = far[ZROWS * p : ZROWS * p + ZROWS]


def rows_here(get, turn, own):
    near = get(slice(0, 2 * BLOCK))
    far = get(slice(PLANE, PLANE + 2 * ZROWS))
    for p, ref in enumerate((own, turn)):
        ref[0:BLOCK, :] = near[BLOCK * p : BLOCK * p + BLOCK]
        ref[BLOCK:PLANE, :] = far[ZROWS * p : ZROWS * p + ZROWS]


def two_cores(hid, za, zb):
    rows = za.shape[0]
    return lambda here: nn(hid[here, 0:rows], za[...]) + nn(
        hid[here, rows : 2 * rows], zb[...]
    )


def grad_away(hid, za, zb, send):
    rows_away(two_cores(hid, za, zb), send)


def grad_here(hid, za, zb, turn, own):
    rows_here(two_cores(hid, za, zb), turn, own)


def feed_back(
    slope, za, zb, d, s, z0, z1, z2, z3, dup, mine, other, whole,
):
    rows = za.shape[0]
    for base, size in PIECES:
        here = slice(base, base + size)
        w = d[here, :]
        dup[here, 0:rows] = (nt(w, za[...]) * slope[here, 0:rows]).astype(BF)
        dup[here, rows:] = (nt(w, zb[...]) * slope[here, rows:]).astype(BF)
    for (base, size), ref in zip(PIECES, (s, z0, z1, z2, z3)):
        whole[base : base + size, :] = ref[...]
    w = whole[...]
    other[...] = tn(dup[:, rows : 2 * rows], w)
    mine[...] = tn(dup[:, 0:rows], w)


def attend_backward(
    lengths, me, ds2, mine, got, xhat, rstd, norms, mix, att, den,
    so, z0, z1, z2, z3, sp, y0, y1, y2, y3,
    dh_ref, do_ref, terms, rel_own, rel_par, datt, dmix,
):
    rows, width = ds2.shape
    chip, core = me[0], me[1]
    dy1 = ds2[...] + (mine[...] + got[...])
    hat = xhat[...]
    terms[0:1, :] = jnp.sum(dy1 * hat, axis=0, keepdims=True)
    terms[1:2, :] = jnp.sum(dy1, axis=0, keepdims=True)
    dh = norm_back(dy1, norms[0:1, :], hat, rstd[...])
    dh_ref[...] = dh
    do = dh.astype(BF)
    do_ref[...] = do
    side = QKV // 3
    sides = ((False, (so, z0, z1, z2, z3), rel_own), (True, (sp, y0, y1, y2, y3), rel_par))
    for other, refs, _ in sides:
        for (base, size), ref in zip(PIECES, refs):
            got_t = nt(ref[...], do)
            for at, plane, step in PLACES:
                if base <= at < base + size:
                    d = shard_index(chip, core, plane, step, other)
                    datt[pl.ds(pl.multiple_of(side * d, 8), side), :] = got_t[
                        at - base + QKV : at - base + BLOCK
                    ]
    mask, _ = pair_mask(lengths, rows)
    for h in range(width // DH):
        here = slice(DH * h, DH * h + DH)
        q = mix[here, :]
        k = mix[width + DH * h : width + DH * h + DH, :]
        v = mix[2 * width + DH * h : 2 * width + DH * h + DH, :].astype(BF)
        fq = softplus(q).astype(BF)
        fk = softplus(k).astype(BF)
        pairs = (tn(fk, fq) * mask).astype(BF)
        da = datt[here, :]
        total = den[h : h + 1, :]
        dnum = da / total
        dden = -jnp.sum(dnum * att[here, :], axis=0, keepdims=True)
        dnum = dnum.astype(BF)
        dpairs = ((tn(v, dnum) + dden) * mask).astype(BF)
        dmix[2 * width + DH * h : 2 * width + DH * h + DH, :] = nt(dnum, pairs)
        dmix[width + DH * h : width + DH * h + DH, :] = nt(fq, dpairs) * jax.nn.sigmoid(k)
        dmix[here, :] = nn(fk, dpairs) * jax.nn.sigmoid(q)
    blank = jnp.zeros((BLOCK - QKV, rows), F32)
    for other, _, rel in sides:
        for at, plane, step in PLACES:
            d = shard_index(chip, core, plane, step, other)
            part = dmix[pl.ds(pl.multiple_of(QKV * d, 8), QKV), :]
            rel[at : at + BLOCK, :] = jnp.concatenate([part, blank], axis=0).astype(BF)


def four_terms(dma, dmb, xa, xb, ata, atb, doa, dob):
    return lambda here: (nn(dma[here, :], xa[...]) + nn(dmb[here, :], xb[...])) + (
        nn(ata[here, :], doa[...]) + nn(atb[here, :], dob[...])
    )


def mix_away(dma, dmb, xa, xb, ata, atb, doa, dob, send):
    rows_away(four_terms(dma, dmb, xa, xb, ata, atb, doa, dob), send)


def mix_here(dma, dmb, xa, xb, ata, atb, doa, dob, turn, own):
    rows_here(four_terms(dma, dmb, xa, xb, ata, atb, doa, dob), turn, own)


def grad_input(dh, rel_own, rel_par, so, z0, z1, z2, z3, sp, y0, y1, y2, y3, out):
    total = dh[...]
    for refs, rel in (((so, z0, z1, z2, z3), rel_own), ((sp, y0, y1, y2, y3), rel_par)):
        for (base, size), ref in zip(PIECES, refs):
            total = total + tn(rel[base : base + size, :], ref[...])
    out[...] = total


def close_sums(k1, a1, b1, c1, g2, g3, t1, t2, g1, note):
    s1 = (k1[...] + a1[...].astype(F32)) + (b1[...].astype(F32) + c1[...].astype(F32))
    g1[...] = s1
    sq = s1 * s1 + g2[...] * g2[...] + g3[...] * g3[...]
    note[0:2, :] = t1[...]
    note[2:4, :] = t2[...]
    note[4:5, :] = jnp.sum(sq, axis=0, keepdims=True)
    note[5:8, :] = jnp.zeros((3, note.shape[1]), F32)


def update(
    n0, n1, n2, n3, g1, g2, g3, mw, ow, uw, dw, nw, mm, om, um, dm, nm, mv, ov, uv, dv, nv,
    norm_out, mw2, ow2, uw2, dw2, nw2, mm2, om2, um2, dm2, nm2, mv2, ov2, uv2, dv2, nv2,
):
    note = (n0[...] + n1[...]) + (n2[...] + n3[...])
    terms = note[0:4, :]
    total = jnp.sum(note[4:5, :]) + jnp.sum(terms * terms)
    norm = jnp.sqrt(jnp.full((1, 1), total, F32))
    norm_out[...] = norm
    scale = 1.0 / jnp.maximum(norm, 1.0)

    one = g1[...]
    grads = (one[0:QKV], one[QKV:BLOCK], g2[...], g3[...], terms)
    groups = (
        (mw, mm, mv, mw2, mm2, mv2),
        (ow, om, ov, ow2, om2, ov2),
        (uw, um, uv, uw2, um2, uv2),
        (dw, dm, dv, dw2, dm2, dv2),
        (nw, nm, nv, nw2, nm2, nv2),
    )
    for g, (w, m, v, w2, m2, v2), rate, decay in zip(grads, groups, RATES, DECAYS):
        new_w, new_m, new_v = adamw(w[...], scale * g, m[...], v[...], rate, decay)
        w2[...] = new_w
        m2[...] = new_m
        v2[...] = new_v


def tie(value, *others):
    return lax.optimization_barrier((value,) + others)[0]


def swap(value):
    return lax.ppermute(value, "fsdp", [(0, 1), (1, 0)])


def hop_first(value):
    return lax.ppermute(value, AXES, [(i, i ^ (4 if i % 2 else 2)) for i in range(2 * CHIPS)])


def hop_second(value):
    return lax.ppermute(value, AXES, [(i, i ^ (2 if i % 2 else 4)) for i in range(2 * CHIPS)])


def hop_z(value, step):
    return lax.ppermute(value, "dp", [(i, i ^ step) for i in range(CHIPS)])


def add_first(turn, got):
    return (turn + got[PLANE:].astype(F32)).astype(BF)


def add_second(own, got, back):
    total = own + got[:PLANE].astype(F32) + back.astype(F32)
    return total[:BLOCK], total.astype(BF)


def send_z(low):
    return [
        hop_z(low[BLOCK * (j + 1) : BLOCK * (j + 2)], step) for j, step in enumerate(STEPS_Z)
    ]


def tuned_device(
    tokens, cotangent, lengths,
    mix_weight, out_weight, up_weight, down_weight, norm_params,
    mix_first, out_first, up_first, down_first, norm_first,
    mix_second, out_second, up_second, down_second, norm_second,
):
    rows, width = tokens.shape
    chip, core = lax.axis_index("dp"), lax.axis_index("fsdp")
    me = jnp.stack([chip, core]).astype(jnp.int32)
    wide = 3 * width

    blocks = [
        jnp.concatenate([mix_weight.T.astype(BF), out_weight.astype(BF)], axis=0),
        up_weight.T.astype(BF),
        down_weight.astype(BF),
    ]
    s_all = jnp.concatenate(blocks, axis=0)
    def wide_join(*parts):
        return jnp.concatenate(parts, axis=0)

    def z_round(block, direct, before):
        if direct:
            got = [hop_z(tie(block, *before), step) for step in STEPS_Z]
            return got, wide_join(*got)
        far = hop_z(tie(block, *before), 8)
        near = hop_z(wide_join(block, far), 4)
        return [far, near], wide_join(far, near)

    s_first = hop_first(s_all)
    s_second = hop_second(s_all)
    near1, joined1 = z_round(blocks[0], True, ())
    near2, joined2 = z_round(blocks[1], False, (near1[2],))
    near3, joined3 = z_round(blocks[2], False, (near2[0],))
    s_third = hop_second(s_first)
    s_parts = (s_all, s_first, s_second, s_third)
    turned1 = hop_first(tie(joined1, s_first, s_second))
    across1 = hop_second(tie(joined1, s_second))
    corner1 = hop_second(tie(turned1, s_third))
    turned2 = hop_first(tie(joined2, turned1, across1))
    across2 = hop_second(tie(joined2, across1))
    corner2 = hop_second(tie(turned2, corner1, across2))
    sorted1, sorted2, sorted3 = call(
        sort_near,
        [((PLANE, width), BF)] * 3,
        s_parts,
    )
    up_all = (sorted2, joined2, turned2, across2, corner2)
    attn_own = (sorted1, joined1, turned1, across1, corner1)
    attn_par = tuple(swap(p) for p in attn_own)
    x_par = swap(tokens)

    mix, att, den, at_own, at_par = call(
        attend_forward,
        [
            ((wide, rows), F32), ((width, rows), F32), ((16, rows), F32),
            ((HALF, rows), BF), ((HALF, rows), BF),
        ],
        (lengths, me, tie(tokens, x_par)) + attn_own + attn_par,
        smem=2,
    )
    turned3 = hop_first(tie(joined3, turned2))
    across3 = hop_second(tie(joined3, across2, den))
    first, first_low, xhat, rstd = call(
        attend_close,
        [((rows, width), F32), ((rows, width), BF), ((rows, width), F32), ((rows, 1), F32)],
        (tokens, at_own, at_par) + attn_own + attn_par + (norm_params,),
    )
    corner3 = hop_second(tie(turned3, corner2, first_low))
    down_all = (sorted3, joined3, turned3, across3, corner3)
    at_got = swap(at_par)
    first_par = swap(first_low)
    hid, slope = call(
        feed_up,
        [((HALF, 2 * rows), BF), ((HALF, 2 * rows), F32)],
        (first_low, tie(first_par, at_got)) + up_all,
    )
    down_par, down_full = call(
        down_away, [((rows, width), BF), ((HALF, width), BF)], (hid,) + down_all
    )
    down_got = swap(down_par)
    (down_own,) = call(down_here, [((rows, width), F32)], (tie(hid, down_par), down_full))
    ds2, dz, xhat_two = call(
        turn_round,
        [((rows, width), F32), ((rows, width), BF), ((rows, width), F32)],
        (lengths, first, down_own, down_got, cotangent, norm_params),
        smem=1,
    )
    dz_par = swap(dz)
    output, terms_two = call(
        finish_forward,
        [((rows, width), BF), ((2, width), F32)],
        (lengths, xhat_two, cotangent, norm_params),
        smem=1,
    )
    away = [((2 * PLANE, width), BF)]
    stay = [((PLANE, width), F32)] * 2
    (send3,) = call(grad_away, away, (hid, dz, dz_par), name="grad_down_away")
    got3 = hop_second(send3)
    dup, dy_own, dy_par = call(
        feed_back,
        [((HALF, 2 * rows), BF)] + [((rows, width), F32)] * 2,
        (slope, tie(dz, send3, terms_two), dz_par, down_full) + up_all,
        scratch=[pltpu.VMEM((HALF, width), BF)],
    )
    (send2,) = call(grad_away, away, (dup, first_low, first_par), name="grad_up_away")
    got2 = hop_second(send2)
    dh, do, terms_one, dm_own, dm_par = call(
        attend_backward,
        [
            ((rows, width), F32), ((rows, width), BF), ((2, width), F32),
            ((HALF, rows), BF), ((HALF, rows), BF),
        ],
        (
            lengths, me, ds2, dy_own, swap(dy_par), xhat, rstd,
            norm_params, mix, att, den,
        ) + attn_own + attn_par,
        scratch=[pltpu.VMEM((width, rows), F32), pltpu.VMEM((wide, rows), F32)],
        smem=2,
    )
    turn3, own3 = call(
        grad_here, stay, (hid, dz, dz_par), name="grad_down_here"
    )
    turn2, own2 = call(
        grad_here, stay, (dup, first_low, first_par),
        name="grad_up_here",
    )
    low_turn3 = add_first(turn3, got3)
    back3 = hop_first(low_turn3)
    low_turn2 = add_first(turn2, got2)
    back2 = hop_first(low_turn2)
    factors = (
        dm_own, swap(dm_par), tokens, x_par, at_own, at_got,
        do, swap(do),
    )
    (send1,) = call(mix_away, away, factors)
    keep3, low3 = add_second(own3, got3, back3)
    parts3 = send_z(low3)
    got1 = hop_second(tie(send1, back3))
    turn1, own1 = call(mix_here, stay, (tie(dm_own, send1),) + factors[1:])
    (grad_tokens,) = call(
        grad_input,
        [((rows, width), F32)],
        (tie(dh, send1), dm_own, dm_par) + attn_own + attn_par,
    )
    keep2, low2 = add_second(own2, got2, back2)
    parts2 = send_z(tie(low2, parts3[1]))
    back1 = hop_first(add_first(tie(turn1, grad_tokens), got1))
    keep1, low1 = add_second(own1, got1, back1)
    parts1 = send_z(tie(low1, parts2[1]))
    g3 = (keep3 + parts3[0]) + (parts3[1].astype(F32) + parts3[2].astype(F32))
    g2 = (keep2 + parts2[0]) + (parts2[1].astype(F32) + parts2[2].astype(F32))
    g1, note = call(
        close_sums,
        [((BLOCK, width), F32), ((8, width), F32)],
        (keep1,) + tuple(parts1) + (g2, g3, terms_one, terms_two),
    )
    note = note + swap(note)
    note = (note + hop_z(note, 1)) + (hop_z(note, 2) + hop_z(note, 3))
    notes = (note, hop_z(note, 4), hop_z(note, 8), hop_z(note, 12))
    shapes = [
        (mix_weight.shape[::-1], F32), (out_weight.shape, F32), (up_weight.shape[::-1], F32),
        (down_weight.shape, F32), (norm_params.shape, F32),
    ]
    norm, *news = call(
        update,
        [((1, 1), F32)] + shapes * 3,
        notes + (
            g1, g2, g3, mix_weight.T, out_weight, up_weight.T, down_weight, norm_params,
            mix_first.T, out_first, up_first.T, down_first, norm_first,
            mix_second.T, out_second, up_second.T, down_second, norm_second,
        ),
    )
    for at in (0, 2, 5, 7, 10, 12):
        news[at] = news[at].T
    return (output, grad_tokens, norm.reshape(())) + tuple(news)


def solution(mesh):
    in_specs = (
        P(("dp", "fsdp"), None),
        P(("dp", "fsdp"), None),
        P(("dp", "fsdp"), None),
        P(None, ("dp", "fsdp")),
        P(("dp", "fsdp"), None),
        P(None, ("dp", "fsdp")),
        P(("dp", "fsdp"), None),
        P(),
        P(None, ("dp", "fsdp")),
        P(("dp", "fsdp"), None),
        P(None, ("dp", "fsdp")),
        P(("dp", "fsdp"), None),
        P(),
        P(None, ("dp", "fsdp")),
        P(("dp", "fsdp"), None),
        P(None, ("dp", "fsdp")),
        P(("dp", "fsdp"), None),
        P(),
    )
    out_specs = (
        P(("dp", "fsdp"), None),
        P(("dp", "fsdp"), None),
        P(),
        P(None, ("dp", "fsdp")),
        P(("dp", "fsdp"), None),
        P(None, ("dp", "fsdp")),
        P(("dp", "fsdp"), None),
        P(),
        P(None, ("dp", "fsdp")),
        P(("dp", "fsdp"), None),
        P(None, ("dp", "fsdp")),
        P(("dp", "fsdp"), None),
        P(),
        P(None, ("dp", "fsdp")),
        P(("dp", "fsdp"), None),
        P(None, ("dp", "fsdp")),
        P(("dp", "fsdp"), None),
        P(),
    )
    sizes = dict(mesh.shape)
    tuned = sizes["dp"] == CHIPS and sizes["fsdp"] == 2
    return jax.shard_map(
        tuned_device if tuned else on_device, mesh=mesh, in_specs=in_specs, out_specs=out_specs, check_vma=False
    )
```
